256 devices in a mesh: pd: 2 (over core), dp: 4 (over x), ep: 32 (over z, y).
Axes of the slice: x: 4, y: 4, z: 8, core: 2. Of those that a mesh axis runs over, the one named last changes fastest.
Arguments:
- queries: bfloat16 [512, 64, 576], P(('pd', 'dp', 'ep')), may hold values from -270 to 270
- cache_vals: bfloat16 [256, 1024, 576], P(('pd', 'dp', 'ep')), may hold values from -6 to 6
- cache_scales: bfloat16 [256, 4, 1024], P(('pd', 'dp', 'ep')), may hold values from 0.25 to 2, as said below
- cache_len: int32 [256], P(('pd', 'dp', 'ep')), may hold values from 256 to 1024, as said below
- fresh_vals: bfloat16 [256, 1024, 576], P(('pd', 'dp', 'ep')), may hold values from -6 to 6
- fresh_scales: bfloat16 [256, 4, 1024], P(('pd', 'dp', 'ep')), may hold values from 0.25 to 2, as said below
- fresh_len: int32 [256], P(('pd', 'dp', 'ep')), may hold values from 512 to 1024, as said below
- fresh_owner: int32 [256], P(('pd', 'dp', 'ep')), may hold values from 0 to 3, as said below
- hidden: bfloat16 [512, 7168], P(('pd', 'dp', 'ep')), may hold values from -4 to 4
- w_uv: bfloat16 [64, 512, 128], P(('pd', 'ep')), may hold values from -1 to 1
- w_out: bfloat16 [8192, 7168], P(('pd', 'ep')), may hold values from -0.0625 to 0.0625
- norm_gain: bfloat16 [7168], replicated, may hold values from 0.5 to 1.5
- route_ids: int32 [512, 8], replicated, may hold values from 0 to 31, all different within a row; in each aligned block of 64 rows (0 to 63, 64 to 127, ...) at most 32 rows name the same one
- route_weights: float32 [512, 8], replicated, may hold values from 0.05 to 0.5
- w_gate: bfloat16 [32, 7168, 1024], P('ep', None, ('pd', 'dp')), may hold values from -0.0625 to 0.0625
- w_up: bfloat16 [32, 7168, 1024], P('ep', None, ('pd', 'dp')), may hold values from -0.0625 to 0.0625
- w_down: bfloat16 [32, 1024, 7168], P('ep', ('pd', 'dp')), may hold values from -0.1875 to 0.1875
Outputs:
- layer_out: bfloat16 [512, 7168], P(('pd', 'dp', 'ep'))
The draws below stay inside these ranges and needn't reach their ends.
Inputs may be any that keep to these rules, and one draw needn't show every extreme that they name: `cache_scales`: every entry is a power of two. `fresh_scales`: every entry is a power of two. `cache_len`: some old request has all 1024 tokens valid. `fresh_len`: some new request has all 1024 tokens valid. For each p < 2 and e < 32, the entries fresh_owner[(p * 4 + i) * 32 + e] over i < 4 take every index along dp exactly once. `route_ids`: each row names 8 different experts. In each aligned block of 64 rows no expert is named by more than 32 rows, a bound that some block reaches.
All inputs are finite; a program needn't handle non-finite values.
Results may differ from the reference program's by a relative error of at most 0.013.
Values may be sent and summed in bfloat16 or wider, within the bound.
No kernel may reach another device: no remote copies, remote signals or barrier semaphores. Data moves between devices by JAX's collectives and lax.ppermute only.
A program may use at most 64 MiB of HBM per device.

```python
import math
import jax
import jax.numpy as jnp
import numpy as np
from jax import lax

D = 7168
DLAT = 512
DV = 128
TOPK = 8
HEADS = 64
FF_E = 1024
EXPERTS = 32
QB = 128
ROWS_DEV = 2
CTX = 1024
PLEN = 1024
NBLK = 4
DKEY = 576
NOLD = 256
NEWREQ = 256
ROWS = 512
SLAB_CAP = 32
N_PD = 2
N_DP = 4
N_EP = 32


def power_scales(key, shape):
    exponents = jax.random.randint(key, shape, -2, 2)
    return jnp.exp2(exponents.astype(jnp.float32)).astype(jnp.bfloat16)


def draw_queries(key, part):
    key = jax.random.fold_in(key, 11)
    base = jnp.clip(jax.random.normal(key, (ROWS, HEADS, DKEY), jnp.float32), -6.0, 6.0)
    return base.astype(jnp.bfloat16)


def draw_cache_scales(key, part):
    key = jax.random.fold_in(key, 12)
    return power_scales(key, (NOLD, NBLK, CTX))


def draw_fresh_scales(key, part):
    key = jax.random.fold_in(key, 13)
    return power_scales(key, (NEWREQ, NBLK, PLEN))


def draw_cache_len(key, part):
    key = jax.random.fold_in(key, 14)
    lengths = jax.random.randint(key, (NOLD,), CTX // 4, CTX + 1)
    longest = jax.random.randint(jax.random.fold_in(key, 1), (), 0, NOLD)
    return lengths.at[longest].set(CTX).astype(jnp.int32)


def draw_fresh_len(key, part):
    key = jax.random.fold_in(key, 15)
    lengths = jax.random.randint(key, (NEWREQ,), PLEN // 2, PLEN + 1)
    longest = jax.random.randint(jax.random.fold_in(key, 1), (), 0, NEWREQ)
    return lengths.at[longest].set(PLEN).astype(jnp.int32)


def draw_fresh_owner(key, part):
    key = jax.random.fold_in(key, 16)
    ranks = jax.random.randint(key, (N_PD, N_EP, N_DP), 0, 1 << 20)
    ranks = ranks * N_DP + jnp.arange(N_DP, dtype=jnp.int32)[None, None, :]
    owners = jnp.argsort(ranks, axis=2).astype(jnp.int32)
    return jnp.transpose(owners, (0, 2, 1)).reshape(NEWREQ).astype(jnp.int32)


def draw_hidden(key, part):
    key = jax.random.fold_in(key, 17)
    first_key, second_key, third_key = jax.random.split(key, 3)
    row_scale = jnp.exp(jax.random.uniform(first_key, (ROWS, 1), jnp.float32, math.log(0.05), math.log(0.5)))
    column_scale = jnp.exp(jax.random.uniform(second_key, (1, D), jnp.float32, math.log(0.5), math.log(2.0)))
    base = jnp.clip(jax.random.normal(third_key, (ROWS, D), jnp.float32), -4.0, 4.0)
    return jnp.clip(base * row_scale * column_scale, -4.0, 4.0).astype(jnp.bfloat16)


def shard_levels(own_key, extent, shards, least, high):
    gain, own = 1.0, jax.random.fold_in(own_key, 6)
    for axis_at, parts in shards:
        heights = jnp.exp(jax.random.uniform(jax.random.fold_in(own, axis_at), (parts,), jnp.float32, least / len(shards), high / len(shards)))
        gain = gain * jnp.repeat(heights, extent[axis_at] // parts).reshape([-1 if axis == axis_at else 1 for axis in range(len(extent))])
    return gain


def assign_block(stream_key, own, number, rows, number_of, top, limit, slope):
    sequence = jax.random.permutation(stream_key, number_of)
    crowded, usual = portions_of(number_of, rows * top, limit, slope, True), portions_of(number_of, rows * top, limit, slope, False)
    places = jnp.arange(number_of)

    def named(sizes, turn):
        used = int((sizes > 0).sum())
        fixed = max(1, used // 4)
        passed = fixed + (places - fixed + turn * (used - fixed)) % max(1, number_of - fixed)
        return jnp.zeros((number_of,), jnp.int32).at[sequence[jnp.where(places < fixed, places, passed)]].set(jnp.asarray(sizes, jnp.int32))

    sizes = jnp.where(number % 4 == 0, named(crowded, number // 4), named(usual, number - number // 4 - 1))
    mixed = jax.random.permutation(jax.random.fold_in(own, 3), number_of)
    donor, sink = mixed[0:number_of // 2 * 2:2], mixed[1:number_of // 2 * 2:2]
    room = jnp.minimum(sizes[donor] - 1, limit - sizes[sink]) // 2
    room = jnp.where((donor == sequence[0]) | (sink == sequence[0]) | (sizes[sink] == 0), 0, jnp.maximum(room, 0))
    passed = jax.random.randint(jax.random.fold_in(own, 4), (number_of // 2,), 0, 1 << 20) % (room + 1)
    sizes = sizes.at[donor].add(-passed).at[sink].add(passed)
    labels = jnp.searchsorted(jnp.cumsum(sizes), jnp.arange(rows * top), side="right").astype(jnp.int32)
    grid = labels.reshape(top, rows).T
    grid = grid[jax.random.permutation(jax.random.fold_in(own, 1), rows)]
    turn = jax.random.randint(jax.random.fold_in(own, 2), (rows, 1), 0, top)
    return jnp.take_along_axis(grid, (jnp.arange(top)[None, :] + turn) % top, axis=1)


def portions_of(count, total, limit, lean, full):
    portions = [(1 << 20) // math.isqrt(rank ** lean) + 1 for rank in range(1, count + 1)]
    largest = limit if full else min(limit, max(-(-total // count), total * portions[0] // sum(portions)))
    least = 1 if total - largest >= count - 1 else 0
    given, rest = [largest] + [least] * (count - 1), total - largest - least * (count - 1)
    while rest > 0:
        candidates = [i for i in range(1, count) if given[i] < largest] or [i for i in range(1, count) if given[i] < limit]
        pool, remaining = sum([portions[i] for i in candidates]), rest
        for i in candidates:
            addition = min(limit - given[i], max(1, remaining * portions[i] // pool), rest)
            given[i] = given[i] + addition
            rest = rest - addition
    return np.array(given)


def scatter_about(own_key, shape, scale, most, cuts=(), held_as=jnp.bfloat16):
    factor_of = shard_levels(own_key, shape, cuts, -0.22, 0.18) if cuts else 1.0
    result = jax.random.normal(own_key, shape, jnp.float32) * scale * factor_of
    return jnp.minimum(jnp.maximum(result, -most), most).astype(held_as)


def setup_inputs(seed: int = 0) -> dict:
    seeds = jax.random.split(jax.random.key(seed), 18)
    queries = draw_queries(jax.random.fold_in(seeds[17], 71), 0)
    cache_vals = scatter_about(seeds[1], (NOLD, CTX, DKEY), 1.0, 6.0, ((0, 256),))
    cache_scales = draw_cache_scales(jax.random.fold_in(seeds[17], 71), 0)
    cache_len = draw_cache_len(jax.random.fold_in(seeds[17], 71), 0)
    fresh_vals = scatter_about(seeds[4], (NEWREQ, PLEN, DKEY), 1.0, 6.0, ((0, 256),))
    fresh_scales = draw_fresh_scales(jax.random.fold_in(seeds[17], 71), 0)
    fresh_len = draw_fresh_len(jax.random.fold_in(seeds[17], 71), 0)
    fresh_owner = draw_fresh_owner(jax.random.fold_in(seeds[17], 71), 0)
    hidden = draw_hidden(jax.random.fold_in(seeds[17], 71), 0)
    w_uv = scatter_about(seeds[9], (HEADS, DLAT, DV), 32 ** -0.5, 1.0, ((0, 64),))
    w_out = scatter_about(seeds[10], (HEADS * DV, D), (HEADS * DV) ** -0.5, 0.0625, ((0, 64),))
    norm_gain = jnp.clip(1.0 + 0.1 * jax.random.normal(seeds[11], (D,), jnp.float32), 0.5, 1.5).astype(jnp.bfloat16)
    route_ids_keys = jax.random.split(jax.random.fold_in(seeds[12], 1), ROWS // (N_EP * ROWS_DEV))
    route_ids_turns = jax.random.permutation(jax.random.fold_in(seeds[12], 3), ROWS // (N_EP * ROWS_DEV))
    route_ids = jax.vmap(lambda own, number: assign_block(jax.random.fold_in(seeds[12], 2), own, number, N_EP * ROWS_DEV, EXPERTS, TOPK, SLAB_CAP, 2))(route_ids_keys, route_ids_turns).reshape((ROWS, TOPK))
    route_weights = jnp.clip(jnp.exp(jax.random.uniform(seeds[13], (ROWS, TOPK), jnp.float32, math.log(0.05), math.log(0.5))), 0.05, 0.5)
    w_gate = scatter_about(seeds[14], (EXPERTS, D, FF_E), D ** -0.5, 0.0625, ((0, 32), (2, 8)))
    w_up = scatter_about(seeds[15], (EXPERTS, D, FF_E), D ** -0.5, 0.0625, ((0, 32), (2, 8)))
    w_down = scatter_about(seeds[16], (EXPERTS, FF_E, D), FF_E ** -0.5, 0.1875, ((0, 32), (1, 8)))
    return {"queries": queries, "cache_vals": cache_vals, "cache_scales": cache_scales, "cache_len": cache_len, "fresh_vals": fresh_vals, "fresh_scales": fresh_scales, "fresh_len": fresh_len, "fresh_owner": fresh_owner, "hidden": hidden, "w_uv": w_uv, "w_out": w_out, "norm_gain": norm_gain, "route_ids": route_ids, "route_weights": route_weights, "w_gate": w_gate, "w_up": w_up, "w_down": w_down}


SOFT_SCALE = 0.07216878364870323
EPSILON = 1e-06

def dequantize(values, scales):
    length = values.shape[0]
    latent = values[:, :DLAT].astype(jnp.float32).reshape(length, NBLK, QB)
    latent = latent * jnp.transpose(scales).astype(jnp.float32)[:, :, None]
    return jnp.concatenate([latent.reshape(length, DLAT).astype(jnp.bfloat16), values[:, DLAT:]], axis=1)

def attend(query_rows, key_rows, length):
    scores = jnp.dot(query_rows, jnp.transpose(key_rows), preferred_element_type=jnp.float32) * SOFT_SCALE
    key_valid = jnp.arange(key_rows.shape[0]) < length
    scores = jnp.where(key_valid[None, :], scores, -1e+30)
    row_top = lax.optimization_barrier(jnp.max(scores, axis=1, keepdims=True))
    weights = jnp.exp(scores - row_top)
    soft_probs = (weights / lax.optimization_barrier(jnp.sum(weights, axis=1, keepdims=True))).astype(jnp.bfloat16)
    return jnp.dot(soft_probs, key_rows[:, :DLAT], preferred_element_type=jnp.float32).astype(jnp.bfloat16)

def reference(queries, cache_vals, cache_scales, cache_len, fresh_vals, fresh_scales, fresh_len, fresh_owner, hidden, w_uv, w_out, norm_gain, route_ids, route_weights, w_gate, w_up, w_down):
    owner_table = fresh_owner.reshape(N_PD, N_DP, N_EP)
    dp_iota = jnp.arange(N_DP, dtype=jnp.int32)
    owner_match = owner_table[:, None, :, :] == dp_iota[None, :, None, None]
    inverse = lax.optimization_barrier(jnp.sum(jnp.where(owner_match, dp_iota[None, None, :, None], 0), axis=2)).astype(jnp.int32)
    device_iota = jnp.arange(NOLD, dtype=jnp.int32)
    pool_index = device_iota // (N_DP * N_EP)
    group_index = device_iota // N_EP % N_DP
    expert_index = device_iota % N_EP
    source = inverse[pool_index, group_index, expert_index]
    fresh_index = ((pool_index * N_DP + source) * N_EP + expert_index).astype(jnp.int32)
    query_pairs = queries.reshape(NOLD, ROWS_DEV, HEADS, DKEY)

    def one_device(per_item):
        query_pair, old_vals, old_scales, old_len, new_index = per_item
        old_out = attend(query_pair[0], dequantize(old_vals, old_scales), old_len)
        new_keys = dequantize(fresh_vals[new_index], fresh_scales[new_index])
        new_out = attend(query_pair[1], new_keys, fresh_len[new_index])
        return jnp.stack([old_out, new_out])
    attn_latent = lax.map(one_device, (query_pairs, cache_vals, cache_scales, cache_len, fresh_index))
    attn_latent = attn_latent.reshape(ROWS, HEADS, DLAT)
    head_values = jnp.einsum('rhl,hlv->rhv', attn_latent.astype(jnp.float32), w_uv.astype(jnp.float32)).astype(jnp.bfloat16)
    attn_out = jnp.dot(head_values.reshape(ROWS, HEADS * DV), w_out, preferred_element_type=jnp.float32)
    resid = hidden.astype(jnp.float32) + attn_out
    mean_square = lax.optimization_barrier(jnp.mean(resid * resid, axis=1, keepdims=True))
    normed = (resid * lax.rsqrt(mean_square + EPSILON) * norm_gain.astype(jnp.float32)[None, :]).astype(jnp.bfloat16)
    capacity = N_PD * N_DP * SLAB_CAP
    slot_iota = jnp.arange(capacity, dtype=jnp.int32)
    groups = N_PD * N_DP
    unit_count = FF_E // groups
    local_count = EXPERTS // N_EP

    def add_expert(total, per_item):
        expert, gate_w, up_w, down_w = per_item
        chosen = route_ids == expert
        weight = lax.optimization_barrier(jnp.sum(jnp.where(chosen, route_weights, 0.0), axis=1))
        routed = jnp.any(chosen, axis=1)
        slot_place = (jnp.cumsum(routed.astype(jnp.int32)) - 1).astype(jnp.int32)
        slot_select = ((slot_place[None, :] == slot_iota[:, None]) & routed[None, :]).astype(jnp.float32)
        slot_rows = jnp.dot(slot_select, normed.astype(jnp.float32), precision=lax.Precision.HIGHEST).astype(jnp.bfloat16)
        gate_proj = jnp.dot(slot_rows, gate_w, preferred_element_type=jnp.float32)
        up_proj = jnp.dot(slot_rows, up_w, preferred_element_type=jnp.float32)
        expert_hidden = (jax.nn.silu(gate_proj) * up_proj).astype(jnp.bfloat16)
        partial_value = jnp.einsum('cgf,gfd->cgd', expert_hidden.reshape(capacity, groups, unit_count).astype(jnp.float32), down_w.reshape(groups, unit_count, D).astype(jnp.float32)).astype(jnp.bfloat16)
        partial_value = lax.optimization_barrier(partial_value)
        expert_out = lax.optimization_barrier(jnp.sum(partial_value.astype(jnp.float32), axis=1))
        slot_weight = jnp.dot(slot_select, weight, precision=lax.Precision.HIGHEST)
        back = jnp.dot(jnp.transpose(slot_select), expert_out * slot_weight[:, None], precision=lax.Precision.HIGHEST)
        return (total + back, None)

    def add_device(mixture, per_device):
        device_experts, gate_set, up_set, down_set = per_device
        table, _ = lax.scan(add_expert, jnp.zeros((ROWS, D), jnp.float32), (device_experts, gate_set, up_set, down_set))
        rounded = lax.optimization_barrier(table.astype(jnp.bfloat16))
        return (mixture + rounded.astype(jnp.float32), None)
    experts_iota = jnp.arange(EXPERTS, dtype=jnp.int32).reshape(N_EP, local_count)
    mixture, _ = lax.scan(add_device, jnp.zeros((ROWS, D), jnp.float32), (experts_iota, w_gate.reshape(N_EP, local_count, D, FF_E), w_up.reshape(N_EP, local_count, D, FF_E), w_down.reshape(N_EP, local_count, FF_E, D)))
    return (resid + mixture).astype(jnp.bfloat16)
```

```python
import jax
import jax.numpy as jnp
from jax import lax
from jax.sharding import PartitionSpec as P

DLAT = 512
QB = 128


SOFT_SCALE = 0.07216878364870323
EPSILON = 1e-06
BF16 = jnp.bfloat16
F32 = jnp.float32


def dequantize(values, scales):
    length = values.shape[0]
    latent = values[:, :DLAT].astype(jnp.float32).reshape(length, DLAT // QB, QB)
    latent = latent * jnp.transpose(scales).astype(jnp.float32)[:, :, None]
    return jnp.concatenate(
        [latent.reshape(length, DLAT).astype(jnp.bfloat16), values[:, DLAT:]], axis=1
    )


def attend(query_rows, key_rows, length):
    scores = (
        jnp.einsum("hk,tk->ht", query_rows, key_rows, preferred_element_type=jnp.float32)
        * SOFT_SCALE
    )
    key_valid = jnp.arange(key_rows.shape[0], dtype=jnp.int32) < length
    scores = jnp.where(key_valid[None, :], scores, -1e30)
    row_top = jnp.max(scores, axis=1, keepdims=True)
    weights = jnp.exp(scores - row_top)
    soft_probs = (weights / jnp.sum(weights, axis=1, keepdims=True)).astype(jnp.bfloat16)
    return jnp.dot(soft_probs, key_rows[:, :DLAT], preferred_element_type=jnp.float32).astype(
        jnp.bfloat16
    )


def shift(value, axis, amount):
    size = lax.axis_size(axis)
    return lax.ppermute(value, axis, [(i, (i + amount) % size) for i in range(size)])


def exchange(value, axis):
    return lax.all_to_all(value, axis, 0, 0)


def dot(left, right):
    return jnp.dot(left, right, preferred_element_type=F32)


def shards(
    queries,
    cache_vals,
    cache_scales,
    cache_len,
    fresh_vals,
    fresh_scales,
    fresh_len,
    fresh_owner,
    hidden,
    w_uv,
    w_out,
    norm_gain,
    route_ids,
    route_weights,
    w_gate,
    w_up,
    w_down,
):
    pd, dp, ep = lax.axis_index("pd"), lax.axis_index("dp"), lax.axis_index("ep")
    n_pd, n_dp, n_ep = lax.axis_size("pd"), lax.axis_size("dp"), lax.axis_size("ep")
    heads, key_width = queries.shape[1:]
    width = hidden.shape[1]
    cols = width // n_dp
    units = w_gate.shape[2]
    tiles = cols // 128

    mark = jnp.broadcast_to(fresh_owner.astype(BF16)[:, None], (heads, 1))
    parcel = jnp.concatenate([queries[1], hidden[1].reshape(heads, width // heads), mark], axis=1)
    parcels = [parcel] + [shift(parcel, "dp", s) for s in range(1, n_dp)]
    step = (dp - fresh_owner[0]) % n_dp
    wanted = lax.dynamic_index_in_dim(jnp.stack(parcels), step, 0, keepdims=False)
    new_query = wanted[:, :key_width]
    new_hidden = wanted[:, key_width : key_width + width // heads].reshape(width)
    marks = jnp.stack([piece[0, -1] for piece in parcels]).astype(jnp.int32)
    owners = marks[(dp - jnp.arange(n_dp, dtype=jnp.int32)) % n_dp]

    uv_other = shift(w_uv[0], "pd", 1)
    out_other = shift(w_out, "pd", 1)
    gate_parts = w_gate[0].reshape(n_dp, cols, units)
    up_parts = w_up[0].reshape(n_dp, cols, units)
    down_parts = w_down[0].reshape(units, n_dp, tiles, 128).transpose(1, 2, 0, 3)
    down_parts = down_parts.reshape(n_dp, tiles * units, 128)
    expert_parts = jnp.concatenate([gate_parts, up_parts, down_parts], axis=1)
    pieces = [lax.dynamic_index_in_dim(expert_parts, dp, 0, keepdims=False)]
    for s in range(1, n_dp):
        part = lax.dynamic_index_in_dim(expert_parts, (dp + s) % n_dp, 0, keepdims=False)
        pieces.append(shift(part, "dp", s))

    old_out = attend(queries[0], dequantize(cache_vals[0], cache_scales[0]), cache_len[0])
    new_out = attend(new_query, dequantize(fresh_vals[0], fresh_scales[0]), fresh_len[0])
    latent = jnp.stack([old_out, new_out]).reshape(2, n_pd, n_ep, DLAT)
    latent = latent.transpose(2, 1, 0, 3).reshape(n_ep, n_pd * 2, DLAT)
    head_rows = exchange(latent, "ep").reshape(n_ep, n_pd, 2, DLAT)
    own_rows = lax.dynamic_index_in_dim(head_rows, pd, 1, keepdims=False).reshape(2 * n_ep, DLAT)
    other_rows = lax.dynamic_index_in_dim(head_rows, 1 - pd, 1, keepdims=False)
    other_rows = other_rows.reshape(2 * n_ep, DLAT)
    partial = dot(dot(own_rows, w_uv[0]).astype(BF16), w_out) + dot(
        dot(other_rows, uv_other).astype(BF16), out_other
    )
    summands = exchange(partial.astype(BF16).reshape(n_ep, 2, width), "ep")
    attn_out = jnp.sum(summands.astype(F32), axis=0)

    resid = jnp.stack([hidden[0], new_hidden]).astype(F32) + attn_out
    scale = lax.rsqrt(jnp.mean(resid * resid, axis=1, keepdims=True) + EPSILON)
    parcel = jnp.concatenate(
        [
            resid.reshape(2, n_dp, cols),
            jnp.broadcast_to(scale[:, :, None], (2, n_dp, 128)),
        ],
        axis=2,
    ).transpose(1, 0, 2)
    taken = exchange(parcel, "dp")
    owned = (owners[None, :] == jnp.arange(n_dp, dtype=jnp.int32)[:, None]).astype(F32)
    new_rows = jnp.sum(jnp.where(owned[:, :, None] > 0, taken[None, :, 1], 0.0), axis=1)
    rows = jnp.stack([taken[:, 0], new_rows], axis=1).reshape(2 * n_dp, cols + 128)
    resid_cols = rows[:, :cols]
    gain = lax.dynamic_slice_in_dim(norm_gain, dp * cols, cols, 0).astype(F32)
    normed = (resid_cols * rows[:, cols : cols + 1] * gain[None, :]).astype(BF16)
    gathered = exchange(jnp.broadcast_to(normed[None], (n_ep,) + normed.shape), "ep")
    gathered = gathered.reshape(n_ep * 2 * n_dp, cols)

    slab = 2 * n_ep
    topk = route_ids.shape[1]
    capacity = 2 * slab * topk // n_ep
    ids = lax.dynamic_slice_in_dim(route_ids, pd * n_dp * slab, n_dp * slab, 0)
    gates = lax.dynamic_slice_in_dim(route_weights, pd * n_dp * slab, n_dp * slab, 0)
    hits = ids == ep
    routed = jnp.any(hits, axis=1).reshape(n_dp, slab)
    gate_of_row = jnp.sum(jnp.where(hits, gates, 0.0), axis=1).reshape(n_dp, slab)
    place = jnp.cumsum(routed.astype(jnp.int32), axis=1) - 1
    slot_mask = (
        place[:, None, :] == jnp.arange(capacity, dtype=jnp.int32)[None, :, None]
    ) & routed[:, None, :]
    slot_gate = jnp.sum(jnp.where(slot_mask, gate_of_row[:, None, :], 0.0), axis=2)
    slots = n_dp * capacity
    select = slot_mask.reshape(n_dp, capacity, n_ep, 1, 2) & jnp.eye(n_dp, dtype=bool).reshape(
        n_dp, 1, 1, n_dp, 1
    )
    select = select.reshape(slots, n_ep * n_dp * 2).astype(BF16)
    slot_rows = dot(select, gathered).astype(BF16)
    all_rows = lax.all_gather(slot_rows, "pd").reshape(n_pd * slots, cols)

    halves = [
        jnp.concatenate([dot(all_rows, w[:cols]), dot(all_rows, w[cols : 2 * cols])], axis=1)
        for w in pieces
    ]
    halves = jnp.stack(halves).astype(BF16)
    order = (dp - jnp.arange(n_dp, dtype=jnp.int32)) % n_dp
    halves = halves[order].reshape(n_dp, n_pd, n_dp, capacity, 2 * units)
    halves = halves.transpose(2, 1, 3, 0, 4).reshape(n_dp, n_pd * capacity, n_dp * 2 * units)
    summed = jnp.sum(exchange(halves, "dp").astype(F32), axis=0)
    summed = summed.reshape(n_pd * capacity, n_dp, 2, units)
    acts = (jax.nn.silu(summed[:, :, 0]) * summed[:, :, 1]).astype(BF16)
    acts = acts.reshape(n_pd * capacity, n_dp * units)
    all_acts = exchange(jnp.broadcast_to(acts[None], (n_dp,) + acts.shape), "dp")
    all_acts = all_acts.reshape(n_dp, n_pd, capacity, n_dp, units).transpose(1, 0, 2, 3, 4)
    all_acts = all_acts.reshape(n_pd * slots, n_dp, units)[:, order]
    downs = jnp.stack([w[2 * cols :].reshape(tiles, units, 128) for w in pieces])
    outs = jnp.einsum("rsu,stuc->rtc", all_acts, downs, preferred_element_type=F32)
    outs = outs.astype(BF16).reshape(n_pd, slots, cols)
    mine = lax.dynamic_index_in_dim(outs, pd, 0, keepdims=False)
    theirs = shift(lax.dynamic_index_in_dim(outs, 1 - pd, 0, keepdims=False), "pd", 1)
    weighted = (mine.astype(F32) + theirs.astype(F32)) * slot_gate.reshape(slots, 1)
    table = dot(select.T, weighted.astype(BF16)).astype(BF16)
    mixture = exchange(table.reshape(n_ep, 2 * n_dp, cols), "ep")
    mixture = jnp.sum(mixture.astype(F32), axis=0)
    out_cols = (resid_cols + mixture).astype(BF16).reshape(n_dp, 2, cols)
    return exchange(out_cols, "dp").transpose(1, 0, 2).reshape(2, width)


def solution(mesh):
    in_specs = (
        P(("pd", "dp", "ep"), None, None),
        P(("pd", "dp", "ep"), None, None),
        P(("pd", "dp", "ep"), None, None),
        P(("pd", "dp", "ep")),
        P(("pd", "dp", "ep"), None, None),
        P(("pd", "dp", "ep"), None, None),
        P(("pd", "dp", "ep")),
        P(("pd", "dp", "ep")),
        P(("pd", "dp", "ep"), None),
        P(("pd", "ep"), None, None),
        P(("pd", "ep"), None),
        P(),
        P(),
        P(),
        P("ep", None, ("pd", "dp")),
        P("ep", None, ("pd", "dp")),
        P("ep", ("pd", "dp"), None),
    )
    out_specs = P(("pd", "dp", "ep"), None)
    return jax.shard_map(shards, mesh=mesh, in_specs=in_specs, out_specs=out_specs, check_vma=False)
```

```python
import jax
import jax.numpy as jnp
from jax import lax
from jax.sharding import PartitionSpec as P

DLAT = 512
QB = 128
CHIPS_Y = 4


SOFT_SCALE = 0.07216878364870323
EPSILON = 1e-06
BF16 = jnp.bfloat16
F32 = jnp.float32


def dequantize(values, scales):
    length = values.shape[0]
    latent = values[:, :DLAT].astype(jnp.float32).reshape(length, DLAT // QB, QB)
    latent = latent * jnp.transpose(scales).astype(jnp.float32)[:, :, None]
    return jnp.concatenate(
        [latent.reshape(length, DLAT).astype(jnp.bfloat16), values[:, DLAT:]], axis=1
    )


def attend(query_rows, key_rows, length):
    scores = (
        jnp.einsum("hk,tk->ht", query_rows, key_rows, preferred_element_type=jnp.float32)
        * SOFT_SCALE
    )
    key_valid = jnp.arange(key_rows.shape[0], dtype=jnp.int32) < length
    scores = jnp.where(key_valid[None, :], scores, -1e30)
    row_top = jnp.max(scores, axis=1, keepdims=True)
    weights = jnp.exp(scores - row_top)
    soft_probs = (weights / jnp.sum(weights, axis=1, keepdims=True)).astype(jnp.bfloat16)
    return jnp.dot(soft_probs, key_rows[:, :DLAT], preferred_element_type=jnp.float32).astype(
        jnp.bfloat16
    )


def shift(value, axis, amount):
    size = lax.axis_size(axis)
    return lax.ppermute(value, axis, [(i, (i + amount) % size) for i in range(size)])


def exchange(value, axis, groups=None):
    return lax.all_to_all(value, axis, 0, 0, axis_index_groups=groups)


def dot(left, right):
    return jnp.dot(left, right, preferred_element_type=F32)


def shards(
    queries,
    cache_vals,
    cache_scales,
    cache_len,
    fresh_vals,
    fresh_scales,
    fresh_len,
    fresh_owner,
    hidden,
    w_uv,
    w_out,
    norm_gain,
    route_ids,
    route_weights,
    w_gate,
    w_up,
    w_down,
):
    pd, dp, ep = lax.axis_index("pd"), lax.axis_index("dp"), lax.axis_index("ep")
    n_pd, n_dp, n_ep = lax.axis_size("pd"), lax.axis_size("dp"), lax.axis_size("ep")
    heads, key_width = queries.shape[1:]
    width = hidden.shape[1]
    cols = width // n_dp
    units = w_gate.shape[2]

    chips_y = CHIPS_Y
    chips_z = n_ep // chips_y
    z_groups = [[z * chips_y + y for z in range(chips_z)] for y in range(chips_y)]
    place_y = ep % chips_y

    def shift_y(value, amount):
        pairs = [
            (z * chips_y + y, z * chips_y + (y + amount) % chips_y)
            for z in range(chips_z)
            for y in range(chips_y)
        ]
        return lax.ppermute(value, "ep", pairs)

    mark = jnp.broadcast_to(fresh_owner.astype(BF16)[:, None], (heads, 1))
    hidden_parts = hidden.reshape(2, n_dp, cols).transpose(1, 0, 2)
    hidden_parts = hidden_parts.reshape(n_dp, heads, 2 * cols // heads)
    query_parts = jnp.broadcast_to(queries[1][None], (n_dp, heads, key_width))
    mark_parts = jnp.broadcast_to(mark[None], (n_dp, heads, 1))
    parcels = exchange(
        jnp.concatenate([query_parts, hidden_parts, mark_parts], axis=2), "dp"
    )
    new_query = lax.dynamic_index_in_dim(parcels, fresh_owner[0], 0, keepdims=False)
    new_query = new_query[:, :key_width]
    hidden_cols = parcels[:, :, key_width : key_width + 2 * cols // heads]
    hidden_cols = hidden_cols.reshape(n_dp, 2, cols).astype(F32)
    owners = parcels[:, 0, -1].astype(jnp.int32)

    uv_own = w_uv[0]
    out_own = lax.dynamic_slice_in_dim(w_out, dp * cols, cols, 1)
    uv_parts = [uv_own] + [shift_y(uv_own, s) for s in range(1, chips_y)]
    out_parts = [out_own] + [shift_y(out_own, s) for s in range(1, chips_y)]

    def sliced(weights, axis):
        return [
            lax.dynamic_slice_in_dim(weights, (dp + s) % n_dp * cols, cols, axis)
            for s in range(n_dp)
        ]

    def sent(parts):
        return parts[:1] + [shift(parts[s], "dp", s) for s in range(1, n_dp)]

    gate_parts = sent(sliced(w_gate[0], 0))

    old_out = attend(queries[0], dequantize(cache_vals[0], cache_scales[0]), cache_len[0])
    new_out = attend(new_query, dequantize(fresh_vals[0], fresh_scales[0]), fresh_len[0])
    latent = jnp.stack([old_out, new_out]).reshape(2, n_pd, chips_z, chips_y, DLAT)
    latent = latent.transpose(2, 1, 3, 0, 4).reshape(chips_z, n_pd * chips_y * 2, DLAT)
    up_parts = sent(sliced(w_up[0], 0))
    head_rows = exchange(latent, "ep", z_groups)
    head_rows, gate_parts, near = lax.optimization_barrier((head_rows, gate_parts, out_parts[1::2]))
    head_rows = head_rows.reshape(chips_z, n_pd, chips_y, 2, DLAT)
    head_rows = head_rows.transpose(1, 2, 0, 3, 4).reshape(n_pd, chips_y, chips_z * 2, DLAT)
    mine = lax.dynamic_index_in_dim(head_rows, pd, 0, keepdims=False)
    theirs = lax.dynamic_index_in_dim(head_rows, 1 - pd, 0, keepdims=False)
    head_rows = jnp.concatenate([mine, shift(theirs, "pd", 1)], axis=1)
    values = [
        dot(
            lax.dynamic_index_in_dim(head_rows, (place_y - s) % chips_y, 0, keepdims=False),
            uv_parts[s],
        ).astype(BF16)
        for s in range(chips_y)
    ]
    values = jnp.concatenate(values, axis=1)
    values, far = lax.optimization_barrier((values, out_parts[2]))
    out_parts = [out_own, near[0], far, near[1]]
    values = exchange(jnp.broadcast_to(values[None], (n_dp,) + values.shape), "dp")
    values = values.reshape(n_dp, 2, chips_z, 2, chips_y * 128).transpose(1, 2, 0, 3, 4)
    values = values.reshape(2 * chips_z * n_dp * 2, chips_y * 128)
    partial = sum(dot(values[:, s * 128 : s * 128 + 128], out_parts[s]) for s in range(chips_y))
    partial = partial.reshape(2, chips_z * n_dp * 2, cols)
    crossing = shift(partial[1].astype(BF16), "pd", 1)
    partial = (partial[0] + crossing.astype(F32)).astype(BF16)
    partial = partial.reshape(chips_z, n_dp * 2, cols)
    down_parts = sent(sliced(w_down[0], 1))
    summands = exchange(partial, "ep", z_groups)
    summands, near = lax.optimization_barrier((summands, up_parts[1::2]))
    up_parts = [up_parts[0], near[0], up_parts[2], near[1]]
    attn_out = jnp.sum(summands.astype(F32), axis=0).reshape(n_dp, 2, cols)
    owned = owners[None, :] == jnp.arange(n_dp, dtype=jnp.int32)[:, None]
    new_rows = jnp.sum(jnp.where(owned[:, :, None], attn_out[None, :, 1], 0.0), axis=1)
    resid_cols = hidden_cols + jnp.stack([attn_out[:, 0], new_rows], axis=1)
    resid_cols = resid_cols.reshape(n_dp * 2, cols)
    squares = jnp.sum(resid_cols * resid_cols, axis=1, keepdims=True)
    squares_high = squares.astype(BF16)
    squares_low = (squares - squares_high.astype(F32)).astype(BF16)
    gain = lax.dynamic_slice_in_dim(norm_gain, dp * cols, cols, 0).astype(F32)
    lanes = (n_dp * 2, 64)
    parcel = jnp.concatenate(
        [
            (resid_cols * gain[None, :]).astype(BF16),
            jnp.broadcast_to(squares_high, lanes),
            jnp.broadcast_to(squares_low, lanes),
        ],
        axis=1,
    )
    column = exchange(jnp.broadcast_to(parcel[None], (chips_z,) + parcel.shape), "ep", z_groups)
    column, near, far = lax.optimization_barrier((column, down_parts[1::2], up_parts[2]))
    up_parts = [up_parts[0], up_parts[1], far, up_parts[3]]
    down_parts = [down_parts[0], near[0], down_parts[2], near[1]]
    column = column.reshape(chips_z * n_dp * 2, cols + 128)
    columns = [column] + [shift_y(column, s) for s in range(1, chips_y)]

    slab = 2 * n_ep
    topk = route_ids.shape[1]
    capacity = 2 * slab * topk // n_ep
    ids = lax.dynamic_slice_in_dim(route_ids, pd * n_dp * slab, n_dp * slab, 0)
    gates = lax.dynamic_slice_in_dim(route_weights, pd * n_dp * slab, n_dp * slab, 0)
    hits = ids == ep
    routed = jnp.any(hits, axis=1).reshape(n_dp, slab)
    gate_of_row = jnp.sum(jnp.where(hits, gates, 0.0), axis=1).reshape(n_dp, slab)
    place = jnp.cumsum(routed.astype(jnp.int32), axis=1) - 1
    slot_mask = (
        place[:, None, :] == jnp.arange(capacity, dtype=jnp.int32)[None, :, None]
    ) & routed[:, None, :]
    slot_gate = jnp.sum(jnp.where(slot_mask, gate_of_row[:, None, :], 0.0), axis=2)
    slots = n_dp * capacity
    select = slot_mask.reshape(slots, chips_z, chips_y, 1, 2)
    same = jnp.arange(slots, dtype=jnp.int32)[:, None] // capacity == jnp.arange(n_dp)[None, :]
    select = select & same.reshape(slots, 1, 1, n_dp, 1)
    select = select.transpose(2, 0, 1, 3, 4).reshape(chips_y, slots, chips_z * n_dp * 2)
    turn = (place_y - jnp.arange(chips_y, dtype=jnp.int32)) % chips_y
    select = select.astype(BF16)[turn]
    slot_rows = sum(dot(select[s], columns[s]) for s in range(chips_y)).astype(BF16)
    other_rows = shift(slot_rows, "pd", 1)
    all_rows = jnp.concatenate([slot_rows, other_rows], axis=0)

    order = (dp - jnp.arange(n_dp, dtype=jnp.int32)) % n_dp
    halves = [
        jnp.concatenate([dot(all_rows[:, :cols], w) for w in pair], axis=1)
        for pair in zip(gate_parts, up_parts)
    ]
    halves = jnp.stack(halves).astype(BF16)[order]
    halves = halves.transpose(1, 0, 2).reshape(n_pd * slots, n_dp * 2 * units)
    halves = jnp.concatenate([halves, all_rows[:, cols:]], axis=1)
    halves = halves.reshape(n_pd, n_dp, capacity, -1).transpose(1, 0, 2, 3)
    halves = halves.reshape(n_dp, n_pd * capacity, n_dp * 2 * units + 128)
    summed = jnp.sum(exchange(halves, "dp").astype(F32), axis=0)
    squares = summed[:, n_dp * 2 * units] + summed[:, n_dp * 2 * units + 64]
    scale = lax.rsqrt(squares / width + EPSILON)[:, None, None, None]
    summed = summed[:, : n_dp * 2 * units].reshape(n_pd * capacity, n_dp, 2, units) * scale
    acts = (jax.nn.silu(summed[:, :, 0]) * summed[:, :, 1]).astype(BF16)
    acts = acts.reshape(n_pd * capacity, n_dp * units)
    all_acts = exchange(jnp.broadcast_to(acts[None], (n_dp,) + acts.shape), "dp")
    all_acts = all_acts.reshape(n_dp, n_pd, capacity, n_dp, units).transpose(1, 0, 2, 3, 4)
    all_acts = all_acts.reshape(n_pd * slots, n_dp, units)[:, order]
    outs = sum(dot(all_acts[:, s], down_parts[s]) for s in range(n_dp))
    outs = outs.reshape(n_pd, slots, cols)
    crossing = shift(outs[1].astype(BF16), "pd", 1)
    weighted = (outs[0] + crossing.astype(F32)) * slot_gate.reshape(slots, 1)
    weighted = weighted.astype(BF16).reshape(n_dp, capacity, cols)
    table = jnp.einsum(
        "dcr,dcx->drx", slot_mask.astype(BF16), weighted, preferred_element_type=F32
    ).reshape(n_dp, n_ep, 2, cols)
    own_line = (jnp.arange(n_ep, dtype=jnp.int32) == ep).reshape(1, n_ep, 1, 1)
    table = table + jnp.where(own_line, resid_cols.reshape(n_dp, 1, 2, cols), 0.0)
    table = table.astype(BF16).reshape(n_dp * n_ep, 2, cols)
    table = exchange(table, ("dp", "ep")).reshape(n_dp, n_ep, 2, cols)
    out = jnp.sum(table.astype(F32), axis=1).astype(BF16)
    return out.transpose(1, 0, 2).reshape(2, width)


def solution(mesh):
    in_specs = (
        P(("pd", "dp", "ep"), None, None),
        P(("pd", "dp", "ep"), None, None),
        P(("pd", "dp", "ep"), None, None),
        P(("pd", "dp", "ep")),
        P(("pd", "dp", "ep"), None, None),
        P(("pd", "dp", "ep"), None, None),
        P(("pd", "dp", "ep")),
        P(("pd", "dp", "ep")),
        P(("pd", "dp", "ep"), None),
        P(("pd", "ep"), None, None),
        P(("pd", "ep"), None),
        P(),
        P(),
        P(),
        P("ep", None, ("pd", "dp")),
        P("ep", None, ("pd", "dp")),
        P("ep", ("pd", "dp"), None),
    )
    out_specs = P(("pd", "dp", "ep"), None)
    return jax.shard_map(shards, mesh=mesh, in_specs=in_specs, out_specs=out_specs, check_vma=False)
```

```python
import functools

import jax
import jax.numpy as jnp
import numpy as np
from jax import lax
from jax.experimental import pallas as pl
from jax.experimental.pallas import tpu as pltpu
from jax.sharding import PartitionSpec as P

DLAT = 512
QB = 128
CHIPS_Y = 4


SOFT_SCALE = 0.07216878364870323
EPSILON = 1e-06
BF16 = jnp.bfloat16
F32 = jnp.float32


def dequantize(values, scales):
    length = values.shape[0]
    latent = values[:, :DLAT].astype(jnp.float32).reshape(length, DLAT // QB, QB)
    latent = latent * jnp.transpose(scales).astype(jnp.float32)[:, :, None]
    return jnp.concatenate(
        [latent.reshape(length, DLAT).astype(jnp.bfloat16), values[:, DLAT:]], axis=1
    )


def attend(query_rows, key_rows, length):
    scores = (
        jnp.einsum("hk,tk->ht", query_rows, key_rows, preferred_element_type=jnp.float32)
        * SOFT_SCALE
    )
    key_valid = jnp.arange(key_rows.shape[0], dtype=jnp.int32) < length
    scores = jnp.where(key_valid[None, :], scores, -1e30)
    row_top = jnp.max(scores, axis=1, keepdims=True)
    weights = jnp.exp(scores - row_top)
    soft_probs = (weights / jnp.sum(weights, axis=1, keepdims=True)).astype(jnp.bfloat16)
    return jnp.dot(soft_probs, key_rows[:, :DLAT], preferred_element_type=jnp.float32).astype(
        jnp.bfloat16
    )


def shift(value, axis, amount):
    size = lax.axis_size(axis)
    return lax.ppermute(value, axis, [(i, (i + amount) % size) for i in range(size)])


def exchange(value, axis, groups=None):
    return lax.all_to_all(value, axis, 0, 0, axis_index_groups=groups)


def dot(left, right):
    return jnp.dot(left, right, preferred_element_type=F32)


HIGHEST = lax.Precision.HIGHEST
VMEM = pl.BlockSpec(memory_space=pltpu.VMEM)
SMEM = pl.BlockSpec(memory_space=pltpu.SMEM)
HBM = pl.BlockSpec(memory_space=pltpu.HBM)
ANY = pl.BlockSpec(memory_space=pl.ANY)
PARAMS = pltpu.CompilerParams(vmem_limit_bytes=16 * 1024 * 1024)


def shape(dims, dtype):
    return jax.ShapeDtypeStruct(dims, dtype)


def pack_kernel(lines, at_ref, gate_ref, up_ref, down_ref, *rest):
    outs, sems = rest[:-1], rest[-1]
    cols, units = outs[1].shape[1], gate_ref.shape[1]
    copies = []
    for s in range(1, lines):
        start = pl.multiple_of(lax.rem(at_ref[0] + s, lines) * cols, 128)
        both, down = outs[2 * s - 2], outs[2 * s - 1]
        copies.append((gate_ref.at[pl.ds(start, cols)], both.at[:, pl.ds(0, units)]))
        copies.append((up_ref.at[pl.ds(start, cols)], both.at[:, pl.ds(units, units)]))
        copies.append((down_ref.at[:, pl.ds(start, cols)], down))
    copies = [pltpu.make_async_copy(a, b, sems.at[i]) for i, (a, b) in enumerate(copies)]
    for copy in copies:
        copy.start()
    for copy in copies:
        copy.wait()


def pack(dp, lines, gate, up, down):
    cols, units = gate.shape[0] // lines, gate.shape[1]
    return pl.pallas_call(
        functools.partial(pack_kernel, lines),
        out_shape=[shape((cols, 2 * units), BF16), shape((units, cols), BF16)] * (lines - 1),
        in_specs=[SMEM, HBM, HBM, HBM],
        out_specs=[HBM] * (2 * lines - 2),
        scratch_shapes=[pltpu.SemaphoreType.DMA((3 * lines - 3,))],
        compiler_params=PARAMS,
    )(dp, gate, up, down)


def values_kernel(turns, at_ref, own_ref, other_ref, *rest):
    uv_refs, out_ref = rest[:-1], rest[-1]
    rows, width = own_ref.shape[1], uv_refs[0].shape[1]
    for s, uv in enumerate(uv_refs):
        head = lax.rem(at_ref[0] - s + turns, turns)
        for q, ref in enumerate((own_ref, other_ref)):
            result = dot(ref[head], uv[...]).astype(BF16)
            for i in range(out_ref.shape[0]):
                out_ref[i, q * rows : (q + 1) * rows, s * width : (s + 1) * width] = result


def head_values(place_y, lines, own, other, uv_parts):
    rows, width = own.shape[1], uv_parts[0].shape[1]
    return pl.pallas_call(
        functools.partial(values_kernel, len(uv_parts)),
        out_shape=shape((lines, 2 * rows, len(uv_parts) * width), BF16),
        in_specs=[SMEM] + [VMEM] * (2 + len(uv_parts)),
        out_specs=VMEM,
        compiler_params=PARAMS,
    )(place_y, own, other, *uv_parts)


def project_kernel(values_ref, order_ref, *rest):
    out_refs, own_ref, other_ref = rest[:-2], rest[-2], rest[-1]
    rows = values_ref.shape[0] // 2
    values = dot(order_ref[...], values_ref[...]).astype(BF16)
    width = out_refs[0].shape[0]
    for start in range(0, own_ref.shape[1], 256):
        total = sum(
            dot(values[:, s * width : (s + 1) * width], ref[:, start : start + 256])
            for s, ref in enumerate(out_refs)
        )
        own_ref[:, start : start + 256] = total[:rows]
        other_ref[:, start : start + 256] = total[rows:].astype(BF16)


def project(values, order, out_parts):
    rows, cols = values.shape[0] // 2, out_parts[0].shape[1]
    return pl.pallas_call(
        project_kernel,
        out_shape=[shape((rows, cols), F32), shape((rows, cols), BF16)],
        in_specs=[VMEM] * (2 + len(out_parts)),
        out_specs=[VMEM, VMEM],
        compiler_params=PARAMS,
    )(values, order, *out_parts)


def residual_kernel(sums_ref, order_ref, hidden_ref, gain_ref, resid_ref, parcel_ref):
    cols = hidden_ref.shape[1]
    total = sums_ref[0].astype(F32)
    for i in range(1, sums_ref.shape[0]):
        total = total + sums_ref[i].astype(F32)
    attn_out = jnp.dot(order_ref[...], total, precision=HIGHEST, preferred_element_type=F32)
    resid = hidden_ref[...] + attn_out
    resid_ref[...] = resid
    squares = jnp.sum(resid * resid, axis=1, keepdims=True)
    high = squares.astype(BF16)
    low = (squares - high.astype(F32)).astype(BF16)
    lanes = lax.broadcasted_iota(jnp.int32, (resid.shape[0], 128), 1)
    beside = jnp.where(lanes < 64, high.astype(F32), low.astype(F32)).astype(BF16)
    rows = (resid * gain_ref[...]).astype(BF16)
    for i in range(parcel_ref.shape[0]):
        parcel_ref[i, :, :cols] = rows
        parcel_ref[i, :, cols:] = beside


def residual(sums, order, hidden_cols, gain):
    copies, rows, cols = sums.shape
    return pl.pallas_call(
        residual_kernel,
        out_shape=[shape((rows, cols), F32), shape((copies, rows, cols + 128), BF16)],
        in_specs=[VMEM] * 4,
        out_specs=[VMEM, VMEM],
        compiler_params=PARAMS,
    )(sums, order, hidden_cols, gain)


def gate_up_kernel(lines, at_ref, own_ref, other_ref, gate_ref, up_ref, *rest):
    parts, out_ref, held, sems = rest[:-3], rest[-3], rest[-2], rest[-1]
    cols, units = held.shape[1], gate_ref.shape[1]
    start = pl.multiple_of(at_ref[0] * cols, 128)
    copies = [
        pltpu.make_async_copy(
            gate_ref.at[pl.ds(start, cols)], held.at[0, :, pl.ds(0, units)], sems.at[0]
        ),
        pltpu.make_async_copy(
            up_ref.at[pl.ds(start, cols)], held.at[0, :, pl.ds(units, units)], sems.at[lines]
        ),
    ]
    for s in range(1, lines):
        copies.append(pltpu.make_async_copy(parts[s - 1], held.at[s], sems.at[s]))
    for copy in copies:
        copy.start()
    for s in range(lines):
        for copy in copies[:2] if s == 0 else copies[s + 1 : s + 2]:
            copy.wait()
        part = lax.rem(at_ref[0] - s + lines, lines)
        lane = pl.multiple_of(part * 2 * units, 128)
        for q, ref in enumerate((own_ref, other_ref)):
            capacity = ref.shape[0] // lines
            result = dot(ref[:, :cols], held[s]).astype(BF16)
            for d in range(lines):
                out_ref[d, q * capacity : (q + 1) * capacity, pl.ds(lane, 2 * units)] = result[
                    d * capacity : (d + 1) * capacity
                ]
    for q, ref in enumerate((own_ref, other_ref)):
        capacity = ref.shape[0] // lines
        for d in range(lines):
            out_ref[d, q * capacity : (q + 1) * capacity, lines * 2 * units :] = ref[
                d * capacity : (d + 1) * capacity, cols:
            ]


def gate_up(dp, lines, own, other, gate, up, parts):
    cols, units = gate.shape[0] // lines, gate.shape[1]
    return pl.pallas_call(
        functools.partial(gate_up_kernel, lines),
        out_shape=shape((lines, 2 * own.shape[0] // lines, lines * 2 * units + 128), BF16),
        in_specs=[SMEM, VMEM, VMEM, HBM, HBM] + [ANY] * (lines - 1),
        out_specs=VMEM,
        scratch_shapes=[
            pltpu.VMEM((lines, cols, 2 * units), BF16),
            pltpu.SemaphoreType.DMA((lines + 1,)),
        ],
        compiler_params=PARAMS,
    )(dp, own, other, gate, up, *parts)


def down_kernel(lines, at_ref, acts_ref, down_ref, *rest):
    parts, own_ref, other_ref, held, sems = rest[:-4], rest[-4], rest[-3], rest[-2], rest[-1]
    units, cols = down_ref.shape[0], held.shape[1]
    start = pl.multiple_of(at_ref[0] * cols, 128)
    sources = [down_ref.at[:, pl.ds(start, cols)]] + list(parts)
    copies = []
    for s in range(lines):
        row = pl.multiple_of(lax.rem(at_ref[0] - s + lines, lines) * units, 128)
        copies.append(pltpu.make_async_copy(sources[s], held.at[pl.ds(row, units)], sems.at[s]))
    for copy in copies:
        copy.start()
    for copy in copies:
        copy.wait()
    capacity = acts_ref.shape[1] // 2
    own = jnp.concatenate([acts_ref[d, :capacity] for d in range(lines)], axis=0)
    other = jnp.concatenate([acts_ref[d, capacity:] for d in range(lines)], axis=0)
    for at in range(0, cols, 256):
        own_ref[:, at : at + 256] = dot(own, held[:, at : at + 256])
        other_ref[:, at : at + 256] = dot(other, held[:, at : at + 256]).astype(BF16)


def down(dp, lines, acts, weights, parts):
    units, cols = weights.shape[0], weights.shape[1] // lines
    slots = acts.shape[0] * acts.shape[1] // 2
    return pl.pallas_call(
        functools.partial(down_kernel, lines),
        out_shape=[shape((slots, cols), F32), shape((slots, cols), BF16)],
        in_specs=[SMEM, VMEM, HBM] + [ANY] * (lines - 1),
        out_specs=[VMEM, VMEM],
        scratch_shapes=[
            pltpu.VMEM((lines * units, cols), BF16),
            pltpu.SemaphoreType.DMA((lines,)),
        ],
        compiler_params=PARAMS,
    )(dp, acts, weights, *parts)


def expand_kernel(own_ref, other_ref, gate_ref, select_ref, out_ref):
    for at in range(0, own_ref.shape[1], 256):
        total = own_ref[:, at : at + 256] + other_ref[:, at : at + 256].astype(F32)
        weighted = (total * gate_ref[...]).astype(BF16)
        out_ref[:, at : at + 256] = dot(select_ref[...], weighted).astype(BF16)


def expand(own, other, gates, select):
    return pl.pallas_call(
        expand_kernel,
        out_shape=shape((select.shape[0], own.shape[1]), BF16),
        in_specs=[VMEM] * 4,
        out_specs=VMEM,
        compiler_params=PARAMS,
    )(own, other, gates, select)


def join_kernel(line_ref, resid_ref, *rest):
    parts, out_ref = rest[:-1], rest[-1]
    total = jnp.dot(
        line_ref[...], resid_ref[...], precision=HIGHEST, preferred_element_type=F32
    )
    for part in parts:
        total = total + part[...].astype(F32)
    out_ref[...] = total.astype(BF16)


def join(line, resid, parts):
    return pl.pallas_call(
        join_kernel,
        out_shape=shape(parts[0].shape, BF16),
        in_specs=[VMEM] * (2 + len(parts)),
        out_specs=VMEM,
        compiler_params=PARAMS,
    )(line, resid, *parts)


def shards(
    queries,
    cache_vals,
    cache_scales,
    cache_len,
    fresh_vals,
    fresh_scales,
    fresh_len,
    fresh_owner,
    hidden,
    w_uv,
    w_out,
    norm_gain,
    route_ids,
    route_weights,
    w_gate,
    w_up,
    w_down,
):
    pd, dp, ep = lax.axis_index("pd"), lax.axis_index("dp"), lax.axis_index("ep")
    n_pd, n_dp, n_ep = lax.axis_size("pd"), lax.axis_size("dp"), lax.axis_size("ep")
    heads, key_width = queries.shape[1:]
    width = hidden.shape[1]
    cols = width // n_dp
    units = w_gate.shape[2]

    chips_y = CHIPS_Y
    chips_z = n_ep // chips_y
    z_groups = [[z * chips_y + y for z in range(chips_z)] for y in range(chips_y)]
    place_y = ep % chips_y

    def shift_y(value, amount):
        pairs = [
            (z * chips_y + y, z * chips_y + (y + amount) % chips_y)
            for z in range(chips_z)
            for y in range(chips_y)
        ]
        return lax.ppermute(value, "ep", pairs)

    mark = jnp.broadcast_to(fresh_owner.astype(BF16)[:, None], (heads, 1))
    hidden_parts = hidden.reshape(2, n_dp, cols).transpose(1, 0, 2)
    hidden_parts = hidden_parts.reshape(n_dp, heads, 2 * cols // heads)
    query_parts = jnp.broadcast_to(queries[1][None], (n_dp, heads, key_width))
    mark_parts = jnp.broadcast_to(mark[None], (n_dp, heads, 1))
    parcels = exchange(
        jnp.concatenate([query_parts, hidden_parts, mark_parts], axis=2), "dp"
    )
    owners = parcels[:, 0, -1].astype(jnp.int32)
    line_iota = jnp.arange(n_dp, dtype=jnp.int32)
    owned = (owners[None, :] == line_iota[:, None])[:, None, :, None]
    pair = jnp.arange(2, dtype=jnp.int32)
    owned = jnp.where(pair == 0, jnp.eye(n_dp, dtype=bool)[:, None, :, None], owned)
    owned = owned & (pair[:, None] == pair)[None, :, None, :]
    owned = owned.astype(F32).reshape(2 * n_dp, 2 * n_dp)
    gain = lax.dynamic_slice_in_dim(norm_gain, dp * cols, cols, 0).astype(F32)[None]

    slab = 2 * n_ep
    topk = route_ids.shape[1]
    capacity = 2 * slab * topk // n_ep
    slots = n_dp * capacity
    ids = lax.dynamic_slice_in_dim(route_ids, pd * n_dp * slab, n_dp * slab, 0)
    gates = lax.dynamic_slice_in_dim(route_weights, pd * n_dp * slab, n_dp * slab, 0)
    hits = ids == ep
    routed = jnp.any(hits, axis=1)
    row_gate = jnp.sum(jnp.where(hits, gates, 0.0), axis=1)
    before = np.kron(np.eye(n_dp), np.triu(np.ones((slab, slab)), 1))
    place = dot(routed.astype(BF16)[None], jnp.asarray(before, BF16))[0].astype(jnp.int32)
    slot = place + jnp.asarray(np.repeat(np.arange(n_dp) * capacity, slab), jnp.int32)
    slot = jnp.where(routed, slot, -1).reshape(n_dp, chips_z, chips_y, 2)
    slot_iota = jnp.arange(slots, dtype=jnp.int32)
    back = slot.transpose(2, 0, 1, 3).reshape(n_dp * slab)
    select_back = (back[:, None] == slot_iota[None, :]).astype(BF16)
    row_gate = row_gate.reshape(n_dp, chips_z, chips_y, 2).transpose(2, 0, 1, 3)
    row_gate = row_gate.reshape(n_dp * slab, 1)
    slot_gate = jnp.sum(jnp.where(back[:, None] == slot_iota[None, :], row_gate, 0.0), axis=0)
    slot_gate = slot_gate.reshape(slots, 1)
    there = slot.transpose(2, 1, 0, 3).reshape(chips_y, n_dp * slab // chips_y)
    there = jnp.flip(jnp.concatenate([there, there], axis=0), axis=0)
    there = lax.dynamic_slice_in_dim(there, chips_y - 1 - place_y, chips_y, 0)
    select = (there[:, None, :] == slot_iota[None, :, None]).astype(BF16)
    own_line = jnp.arange(chips_z, dtype=jnp.int32)[None, :, None] == ep // chips_y
    own_line = jnp.broadcast_to(own_line, (n_dp, chips_z, 2)).reshape(-1, 1)
    own_line = own_line & jnp.asarray(
        np.kron(np.eye(n_dp), np.tile(np.eye(2), (chips_z, 1))), bool
    )
    own_line = own_line.astype(F32)
    parcels, select, select_back, slot_gate, own_line, gain = lax.optimization_barrier(
        (parcels, select, select_back, slot_gate, own_line, gain)
    )

    uv_own = w_uv[0]
    out_own = lax.dynamic_slice_in_dim(w_out, dp * cols, cols, 1)
    uv_parts = [uv_own] + [shift_y(uv_own, s) for s in range(1, chips_y)]
    out_parts = [out_own] + [shift_y(out_own, s) for s in range(1, chips_y)]

    at_dp = dp.astype(jnp.int32).reshape(1)
    at_y = place_y.astype(jnp.int32).reshape(1)
    packed = pack(at_dp, n_dp, w_gate[0], w_up[0], w_down[0])
    parcels, packed = lax.optimization_barrier((parcels, packed))
    both_parts = [shift(packed[2 * s - 2], "dp", s) for s in range(1, n_dp)]
    down_parts = [shift(packed[2 * s - 1], "dp", s) for s in range(1, n_dp)]

    new_query = lax.dynamic_index_in_dim(parcels, fresh_owner[0], 0, keepdims=False)
    new_query = new_query[:, :key_width]
    hidden_cols = parcels[:, :, key_width : key_width + 2 * cols // heads]
    hidden_cols = hidden_cols.reshape(n_dp * 2, cols).astype(F32)

    old_out = attend(queries[0], dequantize(cache_vals[0], cache_scales[0]), cache_len[0])
    new_out = attend(new_query, dequantize(fresh_vals[0], fresh_scales[0]), fresh_len[0])
    latent = jnp.stack([old_out, new_out]).reshape(2, n_pd, chips_z, chips_y, DLAT)
    latent = latent.transpose(2, 1, 3, 0, 4).reshape(chips_z, n_pd * chips_y * 2, DLAT)
    latent, uv_parts = lax.optimization_barrier((latent, uv_parts))
    head_rows = exchange(latent, "ep", z_groups)
    head_rows, near = lax.optimization_barrier((head_rows, out_parts[1::2]))
    head_rows = head_rows.reshape(chips_z, n_pd, chips_y, 2, DLAT)
    head_rows = head_rows.transpose(1, 2, 0, 3, 4).reshape(n_pd, chips_y, chips_z * 2, DLAT)
    mine = lax.dynamic_index_in_dim(head_rows, pd, 0, keepdims=False)
    theirs = lax.dynamic_index_in_dim(head_rows, 1 - pd, 0, keepdims=False)
    values = head_values(at_y, n_dp, mine, shift(theirs, "pd", 1), uv_parts)
    values, far = lax.optimization_barrier((values, out_parts[2]))
    out_parts = [out_own, near[0], far, near[1]]
    values = exchange(values, "dp")
    values, both_far = lax.optimization_barrier((values, both_parts[1]))
    rows = n_dp * 2 * chips_z * 2
    order = np.arange(rows).reshape(n_dp, 2, chips_z, 2).transpose(1, 2, 0, 3).reshape(rows)
    order = jnp.asarray(np.eye(rows)[order], BF16)
    own, other = project(values.reshape(rows, chips_y * 128), order, out_parts)
    partial = (own + shift(other, "pd", 1).astype(F32)).astype(BF16)
    summands = exchange(partial.reshape(chips_z, n_dp * 2, cols), "ep", z_groups)
    resid_cols, parcel = residual(summands, owned, hidden_cols, gain)
    column = exchange(parcel, "ep", z_groups)
    column, near = lax.optimization_barrier((column, both_parts[::2]))
    both_parts = [near[0], both_far, near[1]]
    column = column.reshape(chips_z * n_dp * 2, cols + 128)
    columns = [column] + [shift_y(column, s) for s in range(1, chips_y)]
    columns, down_parts = lax.optimization_barrier((columns, down_parts))
    slot_rows = sum(dot(select[s], columns[s]) for s in range(chips_y)).astype(BF16)
    other_rows = shift(slot_rows, "pd", 1)

    halves = gate_up(at_dp, n_dp, slot_rows, other_rows, w_gate[0], w_up[0], both_parts)
    summed = jnp.sum(exchange(halves, "dp").astype(F32), axis=0)
    squares = summed[:, n_dp * 2 * units] + summed[:, n_dp * 2 * units + 64]
    scale = lax.rsqrt(squares / width + EPSILON)[:, None, None, None]
    summed = summed[:, : n_dp * 2 * units].reshape(n_pd * capacity, n_dp, 2, units) * scale
    acts = (jax.nn.silu(summed[:, :, 0]) * summed[:, :, 1]).astype(BF16)
    acts = acts.reshape(n_pd * capacity, n_dp * units)
    all_acts = exchange(jnp.broadcast_to(acts[None], (n_dp,) + acts.shape), "dp")
    own, other = down(at_dp, n_dp, all_acts, w_down[0], down_parts)
    table = expand(own, shift(other, "pd", 1), slot_gate, select_back)
    table = table.reshape(chips_y, n_dp * chips_z * 2, cols)
    parts = [lax.dynamic_index_in_dim(table, place_y, 0, keepdims=False)]
    for s in range(1, chips_y):
        part = lax.dynamic_index_in_dim(table, (place_y + s) % chips_y, 0, keepdims=False)
        parts.append(shift_y(part, s))
    table = join(own_line, resid_cols, parts).reshape(n_dp * chips_z, 2, cols)
    planes = [
        [d * n_ep + z * chips_y + y for d in range(n_dp) for z in range(chips_z)]
        for y in range(chips_y)
    ]
    table = exchange(table, ("dp", "ep"), planes).reshape(n_dp, chips_z, 2, cols)
    out = jnp.sum(table.astype(F32), axis=1).astype(BF16)
    return out.transpose(1, 0, 2).reshape(2, width)


def solution(mesh):
    in_specs = (
        P(("pd", "dp", "ep"), None, None),
        P(("pd", "dp", "ep"), None, None),
        P(("pd", "dp", "ep"), None, None),
        P(("pd", "dp", "ep")),
        P(("pd", "dp", "ep"), None, None),
        P(("pd", "dp", "ep"), None, None),
        P(("pd", "dp", "ep")),
        P(("pd", "dp", "ep")),
        P(("pd", "dp", "ep"), None),
        P(("pd", "ep"), None, None),
        P(("pd", "ep"), None),
        P(),
        P(),
        P(),
        P("ep", None, ("pd", "dp")),
        P("ep", None, ("pd", "dp")),
        P("ep", ("pd", "dp"), None),
    )
    out_specs = P(("pd", "dp", "ep"), None)
    return jax.shard_map(shards, mesh=mesh, in_specs=in_specs, out_specs=out_specs, check_vma=False)
```

```python
import functools

import jax
import jax.numpy as jnp
import numpy as np
from jax import lax
from jax.experimental import pallas as pl
from jax.experimental.pallas import tpu as pltpu
from jax.sharding import PartitionSpec as P

DLAT = 512
CHIPS_Y = 4


SOFT_SCALE = 0.07216878364870323
EPSILON = 1e-06
BF16 = jnp.bfloat16
F32 = jnp.float32


def shift(value, axis, amount):
    size = lax.axis_size(axis)
    return lax.ppermute(value, axis, [(i, (i + amount) % size) for i in range(size)])


def exchange(value, axis, groups=None):
    return lax.all_to_all(value, axis, 0, 0, axis_index_groups=groups)


def dot(left, right):
    return jnp.dot(left, right, preferred_element_type=F32)


HIGHEST = lax.Precision.HIGHEST
VMEM = pl.BlockSpec(memory_space=pltpu.VMEM)
SMEM = pl.BlockSpec(memory_space=pltpu.SMEM)
HBM = pl.BlockSpec(memory_space=pltpu.HBM)
ANY = pl.BlockSpec(memory_space=pl.ANY)
PARAMS = pltpu.CompilerParams(vmem_limit_bytes=16 * 1024 * 1024)
WIDE = pltpu.CompilerParams(vmem_limit_bytes=58 * 1024 * 1024)


def shape(dims, dtype):
    return jax.ShapeDtypeStruct(dims, dtype)


def attend(query, keys_ref, scales_ref, length, held_ref):
    for block in range(scales_ref.shape[0]):
        at = slice(block * 128, block * 128 + 128)
        scale = scales_ref[...].astype(F32)[block : block + 1]
        held_ref[at] = (keys_ref[at].astype(F32) * scale).astype(BF16)
    scores = dot(query[:, :DLAT], held_ref[...]) + dot(query[:, DLAT:], keys_ref[DLAT:])
    scores = scores * SOFT_SCALE
    token = lax.broadcasted_iota(jnp.int32, scores.shape, 1)
    scores = jnp.where(token < length, scores, -1e30)
    weights = jnp.exp(scores - jnp.max(scores, axis=1, keepdims=True))
    probs = (weights / jnp.sum(weights, axis=1, keepdims=True)).astype(BF16)
    return lax.dot_general(
        probs, held_ref[...], (((1,), (1,)), ((), ())), preferred_element_type=F32
    )


def old_kernel(lines, at_ref, len_ref, query_ref, order_ref, keys_ref, scales_ref, *rest):
    gate_ref, up_ref, down_ref, out_ref = rest[:4]
    outs, held_ref, sems = rest[4:-2], rest[-2], rest[-1]
    cols, units = outs[1].shape[1], gate_ref.shape[1]
    copies = []
    for s in range(1, lines):
        start = pl.multiple_of(lax.rem(at_ref[0] + s, lines) * cols, 128)
        both, down = outs[2 * s - 2], outs[2 * s - 1]
        copies.append((gate_ref.at[pl.ds(start, cols)], both.at[:, pl.ds(0, units)]))
        copies.append((up_ref.at[pl.ds(start, cols)], both.at[:, pl.ds(units, units)]))
        copies.append((down_ref.at[:, pl.ds(start, cols)], down))
    copies = [pltpu.make_async_copy(a, b, sems.at[i]) for i, (a, b) in enumerate(copies)]
    for copy in copies:
        copy.start()
    query = dot(order_ref[...], query_ref[...]).astype(BF16)
    result = attend(query, keys_ref, scales_ref, len_ref[0], held_ref)
    rows = out_ref.shape[1]
    for z in range(out_ref.shape[0]):
        out_ref[z] = result[z * rows : (z + 1) * rows].astype(BF16)
    for copy in copies:
        copy.wait()


def old_attention(dp, lines, length, query, order, keys, scales, gate, up, down, pieces):
    cols, units = gate.shape[0] // lines, gate.shape[1]
    rows = query.shape[0] // pieces
    return pl.pallas_call(
        functools.partial(old_kernel, lines),
        out_shape=[shape((pieces, rows, DLAT), BF16)]
        + [shape((cols, 2 * units), BF16), shape((units, cols), BF16)] * (lines - 1),
        in_specs=[SMEM, SMEM] + [VMEM] * 4 + [HBM] * 3,
        out_specs=[VMEM] + [HBM] * (2 * lines - 2),
        scratch_shapes=[
            pltpu.VMEM((DLAT, keys.shape[1]), BF16),
            pltpu.SemaphoreType.DMA((3 * lines - 3,)),
        ],
        compiler_params=WIDE,
        cost_estimate=pl.CostEstimate(
            flops=4 * query.size * keys.shape[1],
            bytes_accessed=2 * (keys.size + 2 * (gate.size + up.size + down.size)),
            transcendentals=query.shape[0] * keys.shape[1],
        ),
    )(dp, length, query, order, keys, scales, gate, up, down)


def new_kernel(lines, step_ref, len_ref, order_ref, keys_ref, scales_ref, old_ref, *rest):
    parcel_refs, out_ref, held_ref = rest[:lines], rest[lines], rest[lines + 1]
    query = parcel_refs[0][:, : keys_ref.shape[0]]
    for s in range(1, lines):
        query = jnp.where(step_ref[0] == s, parcel_refs[s][:, : keys_ref.shape[0]], query)
    query = dot(order_ref[...], query).astype(BF16)
    result = attend(query, keys_ref, scales_ref, len_ref[0], held_ref)
    rows = out_ref.shape[2]
    for z in range(out_ref.shape[0]):
        out_ref[z, 0] = old_ref[z]
        out_ref[z, 1] = result[z * rows : (z + 1) * rows].astype(BF16)


def new_attention(step, length, order, keys, scales, old, parcels):
    return pl.pallas_call(
        functools.partial(new_kernel, len(parcels)),
        out_shape=shape((old.shape[0], 2) + old.shape[1:], BF16),
        in_specs=[SMEM, SMEM] + [VMEM] * (4 + len(parcels)),
        out_specs=VMEM,
        scratch_shapes=[pltpu.VMEM((DLAT, keys.shape[1]), BF16)],
        compiler_params=PARAMS,
    )(step, length, order, keys, scales, old, *parcels)


def sort_kernel(order_ref, rows_ref, own_ref, other_ref):
    result = dot(order_ref[...], rows_ref[...]).astype(BF16)
    half = own_ref.shape[0]
    own_ref[...] = result[:half]
    other_ref[...] = result[half:]


def sort_rows(order, rows):
    half = shape((rows.shape[0] // 2, rows.shape[1]), BF16)
    return pl.pallas_call(
        sort_kernel,
        out_shape=[half, half],
        in_specs=[VMEM, VMEM],
        out_specs=[VMEM, VMEM],
        compiler_params=PARAMS,
    )(order, rows)


def values_kernel(own_ref, other_ref, *rest):
    uv_refs, out_ref, held_ref, sems = rest[:-3], rest[-3], rest[-2], rest[-1]
    rows, width = own_ref.shape[0] // len(uv_refs), held_ref.shape[2]
    copies = [
        pltpu.make_async_copy(uv, held_ref.at[s], sems.at[s]) for s, uv in enumerate(uv_refs)
    ]
    for copy in copies:
        copy.start()
    for s, copy in enumerate(copies):
        copy.wait()
        for q, ref in enumerate((own_ref, other_ref)):
            result = dot(ref[s * rows : (s + 1) * rows], held_ref[s]).astype(BF16)
            for i in range(out_ref.shape[0]):
                out_ref[i, q * rows : (q + 1) * rows, s * width : (s + 1) * width] = result


def head_values(lines, own, other, uv_parts):
    count = len(uv_parts)
    rows, width = own.shape[0] // count, uv_parts[0].shape[1]
    return pl.pallas_call(
        values_kernel,
        out_shape=shape((lines, 2 * rows, count * width), BF16),
        in_specs=[VMEM] * 2 + [ANY] * count,
        out_specs=VMEM,
        scratch_shapes=[
            pltpu.VMEM((count,) + uv_parts[0].shape, BF16),
            pltpu.SemaphoreType.DMA((count,)),
        ],
        compiler_params=PARAMS,
    )(own, other, *uv_parts)


def project_kernel(values_ref, order_ref, *rest):
    out_refs, own_ref, other_ref = rest[:-2], rest[-2], rest[-1]
    rows = values_ref.shape[0] // 2
    values = dot(order_ref[...], values_ref[...]).astype(BF16)
    width = out_refs[0].shape[0]
    for start in range(0, own_ref.shape[1], 256):
        total = sum(
            dot(values[:, s * width : (s + 1) * width], ref[:, start : start + 256])
            for s, ref in enumerate(out_refs)
        )
        own_ref[:, start : start + 256] = total[:rows]
        other_ref[:, start : start + 256] = total[rows:].astype(BF16)


def project(values, order, out_parts):
    rows, cols = values.shape[0] // 2, out_parts[0].shape[1]
    return pl.pallas_call(
        project_kernel,
        out_shape=[shape((rows, cols), F32), shape((rows, cols), BF16)],
        in_specs=[VMEM] * (2 + len(out_parts)),
        out_specs=[VMEM, VMEM],
        compiler_params=PARAMS,
    )(values, order, *out_parts)


def residual_kernel(
    sums_ref, order_ref, hidden_ref, turned_ref, gain_ref, resid_ref, parcel_ref
):
    cols = hidden_ref.shape[1]
    total = sums_ref[0].astype(F32)
    for i in range(1, sums_ref.shape[0]):
        total = total + sums_ref[i].astype(F32)
    attn_out = jnp.dot(order_ref[...], total, precision=HIGHEST, preferred_element_type=F32)
    hidden = hidden_ref[...].astype(F32)
    resid = attn_out + jnp.dot(
        turned_ref[...], hidden, precision=HIGHEST, preferred_element_type=F32
    )
    resid_ref[...] = resid
    squares = jnp.sum(resid * resid, axis=1, keepdims=True)
    high = squares.astype(BF16)
    low = (squares - high.astype(F32)).astype(BF16)
    lanes = lax.broadcasted_iota(jnp.int32, (resid.shape[0], 128), 1)
    beside = jnp.where(lanes < 64, high.astype(F32), low.astype(F32)).astype(BF16)
    rows = (resid * gain_ref[...]).astype(BF16)
    for i in range(parcel_ref.shape[0]):
        parcel_ref[i, :, :cols] = rows
        parcel_ref[i, :, cols:] = beside


def residual(sums, order, hidden_cols, turned, gain):
    copies, rows, cols = sums.shape
    return pl.pallas_call(
        residual_kernel,
        out_shape=[shape((rows, cols), F32), shape((copies, rows, cols + 128), BF16)],
        in_specs=[VMEM] * 5,
        out_specs=[VMEM, VMEM],
        compiler_params=PARAMS,
    )(sums, order, hidden_cols, turned, gain)


def select_kernel(select_ref, *rest):
    columns, out_ref = rest[:-1], rest[-1]
    for at in range(0, out_ref.shape[1], 384):
        lanes = slice(at, min(at + 384, out_ref.shape[1]))
        out_ref[:, lanes] = sum(
            dot(select_ref[s], ref[:, lanes]) for s, ref in enumerate(columns)
        ).astype(BF16)


def select_rows(select, columns):
    return pl.pallas_call(
        select_kernel,
        out_shape=shape((select.shape[1], columns[0].shape[1]), BF16),
        in_specs=[VMEM] * (1 + len(columns)),
        out_specs=VMEM,
        compiler_params=PARAMS,
    )(select, *columns)


def acts_kernel(width, units, sums_ref, out_ref):
    total = sums_ref[0].astype(F32)
    for i in range(1, sums_ref.shape[0]):
        total = total + sums_ref[i].astype(F32)
    end = sums_ref.shape[2] - 128
    squares = total[:, end : end + 1] + total[:, end + 64 : end + 65]
    scale = lax.rsqrt(squares / width + EPSILON)
    for j in range(end // (2 * units)):
        at = 2 * units * j
        gate = total[:, at : at + units] * scale
        up = total[:, at + units : at + 2 * units] * scale
        acts = (gate / (1.0 + jnp.exp(-gate)) * up).astype(BF16)
        for i in range(out_ref.shape[0]):
            out_ref[i, :, j * units : (j + 1) * units] = acts


def activations(width, units, sums):
    lines, rows, lanes = sums.shape
    return pl.pallas_call(
        functools.partial(acts_kernel, width, units),
        out_shape=shape((lines, rows, (lanes - 128) // 2), BF16),
        in_specs=[VMEM],
        out_specs=VMEM,
        compiler_params=PARAMS,
    )(sums)


def gate_up_kernel(lines, at_ref, own_ref, other_ref, gate_ref, up_ref, *rest):
    parts, out_ref, held, sems = rest[:-3], rest[-3], rest[-2], rest[-1]
    cols, units = held.shape[1], gate_ref.shape[1]
    start = pl.multiple_of(at_ref[0] * cols, 128)
    copies = [
        pltpu.make_async_copy(
            gate_ref.at[pl.ds(start, cols)], held.at[0, :, pl.ds(0, units)], sems.at[0]
        ),
        pltpu.make_async_copy(
            up_ref.at[pl.ds(start, cols)], held.at[0, :, pl.ds(units, units)], sems.at[lines]
        ),
    ]
    for s in range(1, lines):
        copies.append(pltpu.make_async_copy(parts[s - 1], held.at[s], sems.at[s]))
    for copy in copies:
        copy.start()
    for s in range(lines):
        for copy in copies[:2] if s == 0 else copies[s + 1 : s + 2]:
            copy.wait()
        part = lax.rem(at_ref[0] - s + lines, lines)
        lane = pl.multiple_of(part * 2 * units, 128)
        for q, ref in enumerate((own_ref, other_ref)):
            capacity = ref.shape[0] // lines
            result = dot(ref[:, :cols], held[s]).astype(BF16)
            for d in range(lines):
                out_ref[d, q * capacity : (q + 1) * capacity, pl.ds(lane, 2 * units)] = result[
                    d * capacity : (d + 1) * capacity
                ]
    for q, ref in enumerate((own_ref, other_ref)):
        capacity = ref.shape[0] // lines
        for d in range(lines):
            out_ref[d, q * capacity : (q + 1) * capacity, lines * 2 * units :] = ref[
                d * capacity : (d + 1) * capacity, cols:
            ]


def gate_up(dp, lines, own, other, gate, up, parts):
    cols, units = gate.shape[0] // lines, gate.shape[1]
    return pl.pallas_call(
        functools.partial(gate_up_kernel, lines),
        out_shape=shape((lines, 2 * own.shape[0] // lines, lines * 2 * units + 128), BF16),
        in_specs=[SMEM, VMEM, VMEM, HBM, HBM] + [ANY] * (lines - 1),
        out_specs=VMEM,
        scratch_shapes=[
            pltpu.VMEM((lines, cols, 2 * units), BF16),
            pltpu.SemaphoreType.DMA((lines + 1,)),
        ],
        compiler_params=PARAMS,
    )(dp, own, other, gate, up, *parts)


def down_kernel(lines, at_ref, acts_ref, down_ref, *rest):
    parts, own_ref, other_ref, held, sems = rest[:-4], rest[-4], rest[-3], rest[-2], rest[-1]
    units, cols = down_ref.shape[0], held.shape[1]
    start = pl.multiple_of(at_ref[0] * cols, 128)
    sources = [down_ref.at[:, pl.ds(start, cols)]] + list(parts)
    copies = []
    for s in range(lines):
        row = pl.multiple_of(lax.rem(at_ref[0] - s + lines, lines) * units, 128)
        copies.append(pltpu.make_async_copy(sources[s], held.at[pl.ds(row, units)], sems.at[s]))
    for copy in copies:
        copy.start()
    for copy in copies:
        copy.wait()
    capacity = acts_ref.shape[1] // 2
    own = jnp.concatenate([acts_ref[d, :capacity] for d in range(lines)], axis=0)
    other = jnp.concatenate([acts_ref[d, capacity:] for d in range(lines)], axis=0)
    for at in range(0, cols, 256):
        own_ref[:, at : at + 256] = dot(own, held[:, at : at + 256])
        other_ref[:, at : at + 256] = dot(other, held[:, at : at + 256]).astype(BF16)


def down(dp, lines, acts, weights, parts):
    units, cols = weights.shape[0], weights.shape[1] // lines
    slots = acts.shape[0] * acts.shape[1] // 2
    return pl.pallas_call(
        functools.partial(down_kernel, lines),
        out_shape=[shape((slots, cols), F32), shape((slots, cols), BF16)],
        in_specs=[SMEM, VMEM, HBM] + [ANY] * (lines - 1),
        out_specs=[VMEM, VMEM],
        scratch_shapes=[
            pltpu.VMEM((lines * units, cols), BF16),
            pltpu.SemaphoreType.DMA((lines,)),
        ],
        compiler_params=PARAMS,
    )(dp, acts, weights, *parts)


def expand_kernel(own_ref, other_ref, gate_ref, select_ref, out_ref):
    for at in range(0, own_ref.shape[1], 256):
        total = own_ref[:, at : at + 256] + other_ref[:, at : at + 256].astype(F32)
        weighted = (total * gate_ref[...]).astype(BF16)
        out_ref[:, at : at + 256] = dot(select_ref[...], weighted).astype(BF16)


def expand(own, other, gates, select):
    return pl.pallas_call(
        expand_kernel,
        out_shape=shape((select.shape[0], own.shape[1]), BF16),
        in_specs=[VMEM] * 4,
        out_specs=VMEM,
        compiler_params=PARAMS,
    )(own, other, gates, select)


def join_kernel(line_ref, resid_ref, *rest):
    parts, out_ref = rest[:-1], rest[-1]
    total = jnp.dot(
        line_ref[...], resid_ref[...], precision=HIGHEST, preferred_element_type=F32
    )
    for part in parts:
        total = total + part[...].astype(F32)
    out_ref[...] = total.astype(BF16)


def join(line, resid, parts):
    return pl.pallas_call(
        join_kernel,
        out_shape=shape(parts[0].shape, BF16),
        in_specs=[VMEM] * (2 + len(parts)),
        out_specs=VMEM,
        compiler_params=PARAMS,
    )(line, resid, *parts)


def shards(
    queries,
    cache_vals,
    cache_scales,
    cache_len,
    fresh_vals,
    fresh_scales,
    fresh_len,
    fresh_owner,
    hidden,
    w_uv,
    w_out,
    norm_gain,
    route_ids,
    route_weights,
    w_gate,
    w_up,
    w_down,
):
    pd, dp, ep = lax.axis_index("pd"), lax.axis_index("dp"), lax.axis_index("ep")
    n_pd, n_dp, n_ep = lax.axis_size("pd"), lax.axis_size("dp"), lax.axis_size("ep")
    heads, key_width = queries.shape[1:]
    width = hidden.shape[1]
    cols = width // n_dp
    units = w_gate.shape[2]

    chips_y = CHIPS_Y
    chips_z = n_ep // chips_y
    z_groups = [[z * chips_y + y for z in range(chips_z)] for y in range(chips_y)]
    place_y = ep % chips_y

    def shift_y(value, amount):
        pairs = [
            (z * chips_y + y, z * chips_y + (y + amount) % chips_y)
            for z in range(chips_z)
            for y in range(chips_y)
        ]
        return lax.ppermute(value, "ep", pairs)

    mark = jnp.broadcast_to(fresh_owner.astype(BF16)[:, None], (heads, 1))
    hidden_parts = hidden.reshape(2, n_dp, cols).transpose(1, 0, 2)
    hidden_parts = hidden_parts.reshape(n_dp, heads, 2 * cols // heads)
    parcels = []
    for s in range(n_dp):
        part = lax.dynamic_index_in_dim(hidden_parts, (dp + s) % n_dp, 0, keepdims=False)
        parcels.append(jnp.concatenate([queries[1], part, mark], axis=1))
    parcels = parcels[:1] + [shift(parcels[s], "dp", s) for s in range(1, n_dp)]
    line_iota = jnp.arange(n_dp, dtype=jnp.int32)
    sources = (dp - line_iota) % n_dp
    owners = jnp.stack([parcel[0, -1] for parcel in parcels]).astype(jnp.int32)
    owners = jnp.sum(
        jnp.where(sources[None, :] == line_iota[:, None], owners[None, :], 0), axis=1
    )
    turned = jnp.repeat(sources[None, :] == line_iota[:, None], 2, axis=0)
    turned = jnp.repeat(turned, 2, axis=1) & jnp.asarray(
        np.tile(np.eye(2), (n_dp, n_dp)), bool
    )
    turned = turned.astype(F32)
    owned = (owners[None, :] == line_iota[:, None])[:, None, :, None]
    pair = jnp.arange(2, dtype=jnp.int32)
    owned = jnp.where(pair == 0, jnp.eye(n_dp, dtype=bool)[:, None, :, None], owned)
    owned = owned & (pair[:, None] == pair)[None, :, None, :]
    owned = owned.astype(F32).reshape(2 * n_dp, 2 * n_dp)
    gain = lax.dynamic_slice_in_dim(norm_gain, dp * cols, cols, 0).astype(F32)[None]

    slab = 2 * n_ep
    topk = route_ids.shape[1]
    capacity = 2 * slab * topk // n_ep
    slots = n_dp * capacity
    ids = lax.dynamic_slice_in_dim(route_ids, pd * n_dp * slab, n_dp * slab, 0)
    gates = lax.dynamic_slice_in_dim(route_weights, pd * n_dp * slab, n_dp * slab, 0)
    hits = ids == ep
    routed = jnp.any(hits, axis=1)
    row_gate = jnp.sum(jnp.where(hits, gates, 0.0), axis=1)
    before = np.kron(np.eye(n_dp), np.triu(np.ones((slab, slab)), 1))
    place = dot(routed.astype(BF16)[None], jnp.asarray(before, BF16))[0].astype(jnp.int32)
    slot = place + jnp.asarray(np.repeat(np.arange(n_dp) * capacity, slab), jnp.int32)
    slot = jnp.where(routed, slot, -1).reshape(n_dp, chips_z, chips_y, 2)
    slot_iota = jnp.arange(slots, dtype=jnp.int32)
    back = slot.transpose(2, 0, 1, 3).reshape(n_dp * slab)
    select_back = (back[:, None] == slot_iota[None, :]).astype(BF16)
    row_gate = row_gate.reshape(n_dp, chips_z, chips_y, 2).transpose(2, 0, 1, 3)
    row_gate = row_gate.reshape(n_dp * slab, 1)
    slot_gate = jnp.sum(jnp.where(back[:, None] == slot_iota[None, :], row_gate, 0.0), axis=0)
    slot_gate = slot_gate.reshape(slots, 1)
    there = slot.transpose(2, 1, 0, 3).reshape(chips_y, n_dp * slab // chips_y)
    there = jnp.flip(jnp.concatenate([there, there], axis=0), axis=0)
    there = lax.dynamic_slice_in_dim(there, chips_y - 1 - place_y, chips_y, 0)
    select = (there[:, None, :] == slot_iota[None, :, None]).astype(BF16)
    own_line = jnp.arange(chips_z, dtype=jnp.int32)[None, :, None] == ep // chips_y
    own_line = jnp.broadcast_to(own_line, (n_dp, chips_z, 2)).reshape(-1, 1)
    own_line = own_line & jnp.asarray(
        np.kron(np.eye(n_dp), np.tile(np.eye(2), (chips_z, 1))), bool
    )
    own_line = own_line.astype(F32)
    turns = (place_y - jnp.arange(chips_y, dtype=jnp.int32)) % chips_y
    cores = jnp.stack([pd, 1 - pd]).astype(jnp.int32)
    head_order = cores[:, None] * chips_y + turns[None, :]
    head_order = head_order[:, :, None] + jnp.arange(2 * chips_z, dtype=jnp.int32) * (2 * chips_y)
    head_order = head_order.reshape(-1, 1)
    head_order = head_order == jnp.arange(head_order.shape[0], dtype=jnp.int32)[None, :]
    head_order = head_order.astype(BF16)
    masks = (select, select_back, slot_gate, own_line, gain, head_order)
    masks, old_query, first = lax.optimization_barrier((masks, queries[0], parcels[1]))
    select, select_back, slot_gate, own_line, gain, head_order = masks

    at_dp = dp.astype(jnp.int32).reshape(1)
    order = np.arange(heads).reshape(n_pd, chips_z, chips_y).transpose(1, 0, 2).reshape(heads)
    order = jnp.asarray(np.eye(heads)[order], BF16)
    packed = old_attention(
        at_dp,
        n_dp,
        cache_len,
        old_query,
        order,
        cache_vals[0].T,
        cache_scales[0],
        w_gate[0],
        w_up[0],
        w_down[0],
        chips_z,
    )
    old_out, packed = packed[0], packed[1:]
    uv_own = w_uv[0]
    out_own = lax.dynamic_slice_in_dim(w_out, dp * cols, cols, 1)
    old_out, uv_own, out_own, rest = lax.optimization_barrier(
        (old_out, uv_own, out_own, parcels[2:])
    )
    parcels = [parcels[0], first] + list(rest)
    uv_parts = [uv_own] + [shift_y(uv_own, s) for s in range(1, chips_y)]
    out_parts = [out_own] + [shift_y(out_own, s) for s in range(1, chips_y)]
    parcels, packed = lax.optimization_barrier((parcels, packed))
    both_parts = [shift(packed[2 * s - 2], "dp", s) for s in range(1, n_dp)]
    down_parts = [shift(packed[2 * s - 1], "dp", s) for s in range(1, n_dp)]
    hidden_cols = jnp.stack(
        [parcel[:, key_width : key_width + 2 * cols // heads] for parcel in parcels]
    )
    hidden_cols = hidden_cols.reshape(n_dp * 2, cols)

    step = (dp - fresh_owner) % n_dp
    latent = new_attention(
        step, fresh_len, order, fresh_vals[0].T, fresh_scales[0], old_out, parcels
    )
    latent, uv_parts = lax.optimization_barrier((latent, uv_parts))
    head_rows = exchange(latent, "ep", z_groups)
    head_rows, near, hidden_cols, owned, turned = lax.optimization_barrier(
        (head_rows, out_parts[1::2], hidden_cols, owned, turned)
    )
    own, other = sort_rows(head_order, head_rows.reshape(2 * chips_z * heads // chips_z, DLAT))
    values = head_values(n_dp, own, shift(other, "pd", 1), uv_parts)
    values, far = lax.optimization_barrier((values, out_parts[2]))
    out_parts = [out_own, near[0], far, near[1]]
    values = exchange(values, "dp")
    values, both_far = lax.optimization_barrier((values, both_parts[1]))
    rows = n_dp * 2 * chips_z * 2
    order = np.arange(rows).reshape(n_dp, 2, chips_z, 2).transpose(1, 2, 0, 3).reshape(rows)
    order = jnp.asarray(np.eye(rows)[order], BF16)
    own, other = project(values.reshape(rows, chips_y * 128), order, out_parts)
    partial = (own + shift(other, "pd", 1).astype(F32)).astype(BF16)
    summands = exchange(partial.reshape(chips_z, n_dp * 2, cols), "ep", z_groups)
    summands, near = lax.optimization_barrier((summands, both_parts[::2]))
    both_parts = [near[0], both_far, near[1]]
    resid_cols, parcel = residual(summands, owned, hidden_cols, turned, gain)
    column = exchange(parcel, "ep", z_groups)
    column, down_parts = lax.optimization_barrier((column, down_parts))
    column = column.reshape(chips_z * n_dp * 2, cols + 128)
    columns = [column] + [shift_y(column, s) for s in range(1, chips_y)]
    slot_rows = select_rows(select, columns)
    other_rows = shift(slot_rows, "pd", 1)

    halves = gate_up(at_dp, n_dp, slot_rows, other_rows, w_gate[0], w_up[0], both_parts)
    all_acts = exchange(activations(width, units, exchange(halves, "dp")), "dp")
    own, other = down(at_dp, n_dp, all_acts, w_down[0], down_parts)
    table = expand(own, shift(other, "pd", 1), slot_gate, select_back)
    table = table.reshape(chips_y, n_dp * chips_z * 2, cols)
    parts = [lax.dynamic_index_in_dim(table, place_y, 0, keepdims=False)]
    for s in range(1, chips_y):
        part = lax.dynamic_index_in_dim(table, (place_y + s) % chips_y, 0, keepdims=False)
        parts.append(shift_y(part, s))
    table = join(own_line, resid_cols, parts).reshape(n_dp * chips_z, 2, cols)
    planes = [
        [d * n_ep + z * chips_y + y for d in range(n_dp) for z in range(chips_z)]
        for y in range(chips_y)
    ]
    table = exchange(table, ("dp", "ep"), planes).reshape(n_dp, chips_z, 2, cols)
    out = jnp.sum(table.astype(F32), axis=1).astype(BF16)
    return out.transpose(1, 0, 2).reshape(2, width)


def solution(mesh):
    in_specs = (
        P(("pd", "dp", "ep"), None, None),
        P(("pd", "dp", "ep"), None, None),
        P(("pd", "dp", "ep"), None, None),
        P(("pd", "dp", "ep")),
        P(("pd", "dp", "ep"), None, None),
        P(("pd", "dp", "ep"), None, None),
        P(("pd", "dp", "ep")),
        P(("pd", "dp", "ep")),
        P(("pd", "dp", "ep"), None),
        P(("pd", "ep"), None, None),
        P(("pd", "ep"), None),
        P(),
        P(),
        P(),
        P("ep", None, ("pd", "dp")),
        P("ep", None, ("pd", "dp")),
        P("ep", ("pd", "dp"), None),
    )
    out_specs = P(("pd", "dp", "ep"), None)
    return jax.shard_map(shards, mesh=mesh, in_specs=in_specs, out_specs=out_specs, check_vma=False)
```

```python
import functools

import jax
import jax.numpy as jnp
import numpy as np
from jax import lax
from jax.experimental import pallas as pl
from jax.experimental.pallas import tpu as pltpu
from jax.sharding import PartitionSpec as P

DLAT = 512
CHIPS_Y = 4


SOFT_SCALE = 0.07216878364870323
EPSILON = 1e-06
BF16 = jnp.bfloat16
F32 = jnp.float32


def shift(value, axis, amount):
    size = lax.axis_size(axis)
    return lax.ppermute(value, axis, [(i, (i + amount) % size) for i in range(size)])


def exchange(value, axis, groups=None):
    return lax.all_to_all(value, axis, 0, 0, axis_index_groups=groups)


def dot(left, right):
    return jnp.dot(left, right, preferred_element_type=F32)


HIGHEST = lax.Precision.HIGHEST
VMEM = pl.BlockSpec(memory_space=pltpu.VMEM)
SMEM = pl.BlockSpec(memory_space=pltpu.SMEM)
HBM = pl.BlockSpec(memory_space=pltpu.HBM)
ANY = pl.BlockSpec(memory_space=pl.ANY)
PARAMS = pltpu.CompilerParams(vmem_limit_bytes=16 * 1024 * 1024)
WIDE = pltpu.CompilerParams(vmem_limit_bytes=58 * 1024 * 1024)


def shape(dims, dtype):
    return jax.ShapeDtypeStruct(dims, dtype)


def attend(query, keys_ref, scales_ref, length, held_ref):
    for block in range(scales_ref.shape[0]):
        at = slice(block * 128, block * 128 + 128)
        scale = scales_ref[...].astype(F32)[block : block + 1]
        held_ref[at] = (keys_ref[at].astype(F32) * scale).astype(BF16)
    scores = dot(query[:, :DLAT], held_ref[...]) + dot(query[:, DLAT:], keys_ref[DLAT:])
    scores = scores * SOFT_SCALE
    token = lax.broadcasted_iota(jnp.int32, scores.shape, 1)
    scores = jnp.where(token < length, scores, -1e30)
    weights = jnp.exp(scores - jnp.max(scores, axis=1, keepdims=True))
    probs = (weights / jnp.sum(weights, axis=1, keepdims=True)).astype(BF16)
    return lax.dot_general(
        probs, held_ref[...], (((1,), (1,)), ((), ())), preferred_element_type=F32
    )


def parcel_kernel(lines, at_ref, owner_ref, query_ref, hidden_ref, *outs):
    heads, wide = query_ref.shape[1:]
    cols = hidden_ref.shape[1] // lines
    lanes = outs[0].shape[1]
    for s in range(lines):
        start = pl.multiple_of(lax.rem(at_ref[0] + s, lines) * cols, 128)
        hidden = hidden_ref[:, pl.ds(start, cols)].astype(F32)
        parts = [hidden[:, at : at + lanes] for at in range(0, cols, lanes)]
        parts = [jnp.pad(part, ((0, 0), (0, lanes - part.shape[1]))) for part in parts]
        used = 2 * len(parts)
        parts.append(jnp.full((16 - used, lanes), owner_ref[0].astype(F32)))
        outs[s][:heads, :wide] = query_ref[1]
        outs[s][:heads, wide:] = jnp.zeros((heads, lanes - wide), BF16)
        outs[s][heads:] = jnp.concatenate(parts, axis=0).astype(BF16)


def make_parcels(dp, lines, owner, query, hidden):
    out = shape((query.shape[1] + 16, -(-query.shape[2] // 128) * 128), BF16)
    return pl.pallas_call(
        functools.partial(parcel_kernel, lines),
        out_shape=[out] * lines,
        in_specs=[SMEM, SMEM, VMEM, VMEM],
        out_specs=[VMEM] * lines,
        compiler_params=PARAMS,
    )(dp, owner, query, hidden)


def mask_kernel(sizes, at_ref, ids_ref, gates_ref, before_ref, there_ref, back_ref, *outs):
    chips_y, chips_z, lines, capacity = sizes
    select_ref, table_ref, gate_ref, order_ref, line_ref = outs
    core, expert, place_y, place_z = (at_ref[i] for i in range(4))
    rows, slots = ids_ref.shape[1], lines * capacity
    hits = ids_ref[...] == expert
    routed = jnp.sum(jnp.where(hits, 1.0, 0.0), axis=0, keepdims=True)
    gates = jnp.sum(jnp.where(hits, gates_ref[...], 0.0), axis=0, keepdims=True)
    place = dot(jnp.broadcast_to(routed, (8, rows)).astype(BF16), before_ref[...])[:1]
    lane = lax.broadcasted_iota(jnp.int32, (1, rows), 1)
    first = lax.div(lane, rows // lines) * capacity
    slot = jnp.where(routed > 0.0, place + first.astype(F32), -1.0)
    wide = jnp.broadcast_to(slot, (8, rows)).astype(BF16)
    slot_iota = lax.broadcasted_iota(jnp.int32, (slots, rows), 0).astype(F32)
    select_ref[...] = jnp.where(dot(wide, there_ref[...])[:1] == slot_iota, 1.0, 0.0).astype(BF16)
    back = jnp.where(dot(wide, back_ref[...])[:1] == slot_iota, 1.0, 0.0)
    table_ref[...] = back.T.astype(BF16)
    gate_ref[...] = jnp.sum(jnp.where(slot == slot_iota, gates, 0.0), axis=1, keepdims=True)
    pairs = 2 * chips_z
    out = lax.broadcasted_iota(jnp.int32, order_ref.shape, 0)
    want = lax.div(out, chips_y * pairs)
    want = jnp.where(want == 0, core, 1 - core)
    turn = lax.rem(place_y - lax.rem(lax.div(out, pairs), chips_y) + chips_y, chips_y)
    want = lax.rem(out, pairs) * (2 * chips_y) + want * chips_y + turn
    come = lax.broadcasted_iota(jnp.int32, order_ref.shape, 1)
    order_ref[...] = jnp.where(want == come, 1.0, 0.0).astype(BF16)
    out = lax.broadcasted_iota(jnp.int32, line_ref.shape, 0)
    come = lax.broadcasted_iota(jnp.int32, line_ref.shape, 1)
    own = lax.rem(lax.div(out, 2), chips_z) == place_z
    own = own & (lax.div(out, pairs) * 2 + lax.rem(out, 2) == come)
    line_ref[...] = jnp.where(own, 1.0, 0.0)


def make_masks(at, sizes, ids, gates):
    chips_y, chips_z, lines, capacity = sizes
    rows, slots, pairs = ids.shape[1], lines * capacity, 2 * chips_z
    canon = np.arange(rows).reshape(lines, chips_z, chips_y, 2)
    eye = np.eye(rows)
    before = np.kron(np.eye(lines), np.triu(np.ones((rows // lines, rows // lines)), 1))
    there = eye[canon.transpose(2, 1, 0, 3).reshape(rows)].T
    back = eye[canon.transpose(2, 0, 1, 3).reshape(rows)].T
    heads = 2 * chips_y * pairs
    return pl.pallas_call(
        functools.partial(mask_kernel, sizes),
        out_shape=[
            shape((slots, rows), BF16),
            shape((rows, slots), BF16),
            shape((slots, 1), F32),
            shape((heads, heads), BF16),
            shape((lines * pairs, 2 * lines), F32),
        ],
        in_specs=[SMEM] + [VMEM] * 5,
        out_specs=[VMEM] * 5,
        compiler_params=PARAMS,
    )(at, ids, gates, *(jnp.asarray(m, BF16) for m in (before, there, back)))


def old_kernel(lines, at_ref, len_ref, query_ref, order_ref, keys_ref, scales_ref, *rest):
    gate_ref, up_ref, down_ref, out_ref = rest[:4]
    outs, held_ref, sems = rest[4:-2], rest[-2], rest[-1]
    cols, units = outs[1].shape[1], gate_ref.shape[1]
    copies = []
    for s in range(lines):
        start = pl.multiple_of(lax.rem(at_ref[0] + s, lines) * cols, 128)
        both, down = outs[2 * s], outs[2 * s + 1]
        copies.append((gate_ref.at[pl.ds(start, cols)], both.at[:, pl.ds(0, units)]))
        copies.append((up_ref.at[pl.ds(start, cols)], both.at[:, pl.ds(units, units)]))
        copies.append((down_ref.at[:, pl.ds(start, cols)], down))
    copies = [pltpu.make_async_copy(a, b, sems.at[i]) for i, (a, b) in enumerate(copies)]
    for copy in copies:
        copy.start()
    query = dot(order_ref[...], query_ref[0]).astype(BF16)
    result = attend(query, keys_ref, scales_ref, len_ref[0], held_ref)
    rows = out_ref.shape[1]
    for z in range(out_ref.shape[0]):
        out_ref[z] = result[z * rows : (z + 1) * rows].astype(BF16)
    for copy in copies:
        copy.wait()


def old_attention(dp, lines, length, query, order, keys, scales, gate, up, down, pieces):
    cols, units = gate.shape[0] // lines, gate.shape[1]
    rows = query.shape[1] // pieces
    return pl.pallas_call(
        functools.partial(old_kernel, lines),
        out_shape=[shape((pieces, rows, DLAT), BF16)]
        + [shape((cols, 2 * units), BF16), shape((units, cols), BF16)] * lines,
        in_specs=[SMEM, SMEM] + [VMEM] * 4 + [HBM] * 3,
        out_specs=[VMEM] * (2 * lines + 1),
        scratch_shapes=[
            pltpu.VMEM((DLAT, keys.shape[1]), BF16),
            pltpu.SemaphoreType.DMA((3 * lines,)),
        ],
        compiler_params=WIDE,
        cost_estimate=pl.CostEstimate(
            flops=2 * query.size * keys.shape[1],
            bytes_accessed=2 * (keys.size + 2 * (gate.size + up.size + down.size)),
            transcendentals=query.shape[1] * keys.shape[1],
        ),
    )(dp, length, query, order, keys, scales, gate, up, down)


def new_kernel(lines, step_ref, len_ref, order_ref, keys_ref, scales_ref, old_ref, *rest):
    parcel_refs, out_ref, held_ref = rest[:lines], rest[lines], rest[lines + 1]
    heads, width = order_ref.shape[0], keys_ref.shape[0]
    query = parcel_refs[0][:heads, :width]
    for s in range(1, lines):
        query = jnp.where(step_ref[0] == s, parcel_refs[s][:heads, :width], query)
    query = dot(order_ref[...], query).astype(BF16)
    result = attend(query, keys_ref, scales_ref, len_ref[0], held_ref)
    rows = out_ref.shape[2]
    for z in range(out_ref.shape[0]):
        out_ref[z, 0] = old_ref[z]
        out_ref[z, 1] = result[z * rows : (z + 1) * rows].astype(BF16)


def new_attention(step, length, order, keys, scales, old, parcels):
    return pl.pallas_call(
        functools.partial(new_kernel, len(parcels)),
        out_shape=shape((old.shape[0], 2) + old.shape[1:], BF16),
        in_specs=[SMEM, SMEM] + [VMEM] * (4 + len(parcels)),
        out_specs=VMEM,
        scratch_shapes=[pltpu.VMEM((DLAT, keys.shape[1]), BF16)],
        compiler_params=PARAMS,
    )(step, length, order, keys, scales, old, *parcels)


def sort_kernel(order_ref, rows_ref, own_ref, other_ref):
    result = dot(order_ref[...], rows_ref[...]).astype(BF16)
    half = own_ref.shape[0]
    own_ref[...] = result[:half]
    other_ref[...] = result[half:]


def sort_rows(order, rows):
    half = shape((rows.shape[0] // 2, rows.shape[1]), BF16)
    return pl.pallas_call(
        sort_kernel,
        out_shape=[half, half],
        in_specs=[VMEM, VMEM],
        out_specs=[VMEM, VMEM],
        compiler_params=PARAMS,
    )(order, rows)


def values_kernel(own_ref, other_ref, uv_ref, out_ref):
    count, _, width = uv_ref.shape
    rows = own_ref.shape[0] // count
    for s in range(count):
        for q, ref in enumerate((own_ref, other_ref)):
            result = dot(ref[s * rows : (s + 1) * rows], uv_ref[s]).astype(BF16)
            for i in range(out_ref.shape[0]):
                out_ref[i, q * rows : (q + 1) * rows, s * width : (s + 1) * width] = result


def head_values(lines, own, other, uv_all):
    count, _, width = uv_all.shape
    return pl.pallas_call(
        values_kernel,
        out_shape=shape((lines, 2 * own.shape[0] // count, count * width), BF16),
        in_specs=[VMEM] * 3,
        out_specs=VMEM,
        compiler_params=PARAMS,
    )(own, other, uv_all)


def project_kernel(values_ref, order_ref, *rest):
    out_refs, own_ref, other_ref = rest[:-2], rest[-2], rest[-1]
    rows = values_ref.shape[0] // 2
    values = dot(order_ref[...], values_ref[...]).astype(BF16)
    width = out_refs[0].shape[0]
    for start in range(0, own_ref.shape[1], 256):
        total = sum(
            dot(values[:, s * width : (s + 1) * width], ref[:, start : start + 256])
            for s, ref in enumerate(out_refs)
        )
        own_ref[:, start : start + 256] = total[:rows]
        other_ref[:, start : start + 256] = total[rows:].astype(BF16)


def project(values, order, out_parts):
    rows, cols = values.shape[0] // 2, out_parts[0].shape[1]
    return pl.pallas_call(
        project_kernel,
        out_shape=[shape((rows, cols), F32), shape((rows, cols), BF16)],
        in_specs=[VMEM] * (2 + len(out_parts)),
        out_specs=[VMEM, VMEM],
        compiler_params=PARAMS,
    )(values, order, *out_parts)


def line_kernel(heads, at_ref, gain_ref, *rest):
    parcel_refs, out_ref = rest[:-1], rest[-1]
    lines, cols = len(parcel_refs), gain_ref.shape[1]
    row = lax.broadcasted_iota(jnp.int32, (2 * lines, 128), 0)
    come = lax.broadcasted_iota(jnp.int32, (2 * lines, 128), 1)
    same = lax.rem(row, 2) == lax.rem(come, 2)
    old = lax.rem(row, 2) == 0
    row, come = lax.div(row, 2), lax.div(come, 2)
    order = jnp.where(same & old & (row == come), 1.0, 0.0)
    turned = jnp.zeros_like(order)
    hidden = []
    for s, ref in enumerate(parcel_refs):
        source = lax.rem(at_ref[0] - s + lines, lines)
        lower = ref[heads:].astype(F32)
        lanes = lower.shape[1]
        count = -(-cols // lanes)
        owner = lower[2 * count : 2 * count + 1, :1]
        moved = same & ~old & (come == source) & (row.astype(F32) == owner)
        order = order + jnp.where(moved, 1.0, 0.0)
        turned = turned + jnp.where(same & (come == s) & (row == source), 1.0, 0.0)
        pieces = [
            lower[2 * j : 2 * j + 2, : min(lanes, cols - j * lanes)] for j in range(count)
        ]
        hidden.append(jnp.concatenate(pieces, axis=1))
    hidden = jnp.concatenate(hidden, axis=0)
    rows = 2 * lines
    out_ref[:rows] = jnp.dot(
        turned[:, :rows], hidden, precision=HIGHEST, preferred_element_type=F32
    )
    out_ref[rows : 2 * rows] = jnp.broadcast_to(gain_ref[...].astype(F32), (rows, cols))
    out_ref[2 * rows :, :128] = order
    out_ref[2 * rows :, 128:] = jnp.zeros((rows, cols - 128), F32)


def line_rows(dp, heads, gain, parcels):
    return pl.pallas_call(
        functools.partial(line_kernel, heads),
        out_shape=shape((6 * len(parcels), gain.shape[1]), F32),
        in_specs=[SMEM] + [VMEM] * (1 + len(parcels)),
        out_specs=VMEM,
        compiler_params=PARAMS,
    )(dp, gain, *parcels)


def residual_kernel(sums_ref, line_ref, resid_ref, parcel_ref):
    rows, cols = resid_ref.shape
    total = sums_ref[0].astype(F32)
    for i in range(1, sums_ref.shape[0]):
        total = total + sums_ref[i].astype(F32)
    order = line_ref[2 * rows :, :128][:, :rows]
    resid = jnp.dot(order, total, precision=HIGHEST, preferred_element_type=F32)
    resid = resid + line_ref[:rows]
    resid_ref[...] = resid
    squares = jnp.sum(resid * resid, axis=1, keepdims=True)
    high = squares.astype(BF16)
    low = (squares - high.astype(F32)).astype(BF16)
    lanes = lax.broadcasted_iota(jnp.int32, (rows, 128), 1)
    beside = jnp.where(lanes < 64, high.astype(F32), low.astype(F32)).astype(BF16)
    parcel = (resid * line_ref[rows : 2 * rows]).astype(BF16)
    for i in range(parcel_ref.shape[0]):
        parcel_ref[i, :, :cols] = parcel
        parcel_ref[i, :, cols:] = beside


def residual(sums, line):
    copies, rows, cols = sums.shape
    return pl.pallas_call(
        residual_kernel,
        out_shape=[shape((rows, cols), F32), shape((copies, rows, cols + 128), BF16)],
        in_specs=[VMEM, VMEM],
        out_specs=[VMEM, VMEM],
        compiler_params=PARAMS,
    )(sums, line)


def select_kernel(at_ref, select_ref, *rest):
    columns, out_ref, held_ref = rest[:-2], rest[-2], rest[-1]
    count, rows = len(columns), columns[0].shape[0]
    for s, ref in enumerate(columns):
        held_ref[lax.rem(at_ref[2] - s + count, count)] = ref[...]
    for at in range(0, out_ref.shape[1], 384):
        lanes = slice(at, min(at + 384, out_ref.shape[1]))
        gathered = held_ref[:, :, lanes].reshape(count * rows, lanes.stop - at)
        out_ref[:, lanes] = dot(select_ref[...], gathered).astype(BF16)


def select_rows(at, select, columns):
    return pl.pallas_call(
        select_kernel,
        out_shape=shape((select.shape[0], columns[0].shape[1]), BF16),
        in_specs=[SMEM] + [VMEM] * (1 + len(columns)),
        out_specs=VMEM,
        scratch_shapes=[pltpu.VMEM((len(columns),) + columns[0].shape, BF16)],
        compiler_params=PARAMS,
    )(at, select, *columns)


def acts_kernel(width, units, sums_ref, out_ref):
    total = sums_ref[0].astype(F32)
    for i in range(1, sums_ref.shape[0]):
        total = total + sums_ref[i].astype(F32)
    end = sums_ref.shape[2] - 128
    squares = total[:, end : end + 1] + total[:, end + 64 : end + 65]
    scale = lax.rsqrt(squares / width + EPSILON)
    for j in range(end // (2 * units)):
        at = 2 * units * j
        gate = total[:, at : at + units] * scale
        up = total[:, at + units : at + 2 * units] * scale
        acts = (gate / (1.0 + jnp.exp(-gate)) * up).astype(BF16)
        for i in range(out_ref.shape[0]):
            out_ref[i, :, j * units : (j + 1) * units] = acts


def activations(width, units, sums):
    lines, rows, lanes = sums.shape
    return pl.pallas_call(
        functools.partial(acts_kernel, width, units),
        out_shape=shape((lines, rows, (lanes - 128) // 2), BF16),
        in_specs=[VMEM],
        out_specs=VMEM,
        compiler_params=PARAMS,
    )(sums)


def gate_up_kernel(lines, at_ref, own_ref, other_ref, *rest):
    parts, out_ref, held, sems = rest[:-3], rest[-3], rest[-2], rest[-1]
    cols, lanes = held.shape[1:]
    copies = [pltpu.make_async_copy(parts[s], held.at[s], sems.at[s]) for s in range(lines)]
    for copy in copies:
        copy.start()
    for s in range(lines):
        copies[s].wait()
        lane = pl.multiple_of(lax.rem(at_ref[0] - s + lines, lines) * lanes, 128)
        for q, ref in enumerate((own_ref, other_ref)):
            capacity = ref.shape[0] // lines
            result = dot(ref[:, :cols], held[s]).astype(BF16)
            for d in range(lines):
                out_ref[d, q * capacity : (q + 1) * capacity, pl.ds(lane, lanes)] = result[
                    d * capacity : (d + 1) * capacity
                ]
    for q, ref in enumerate((own_ref, other_ref)):
        capacity = ref.shape[0] // lines
        for d in range(lines):
            out_ref[d, q * capacity : (q + 1) * capacity, lines * lanes :] = ref[
                d * capacity : (d + 1) * capacity, cols:
            ]


def gate_up(dp, own, other, parts):
    lines, (cols, lanes) = len(parts), parts[0].shape
    return pl.pallas_call(
        functools.partial(gate_up_kernel, lines),
        out_shape=shape((lines, 2 * own.shape[0] // lines, lines * lanes + 128), BF16),
        in_specs=[SMEM, VMEM, VMEM] + [ANY] * lines,
        out_specs=VMEM,
        scratch_shapes=[
            pltpu.VMEM((lines, cols, lanes), BF16),
            pltpu.SemaphoreType.DMA((lines,)),
        ],
        compiler_params=PARAMS,
    )(dp, own, other, *parts)


def down_kernel(lines, at_ref, acts_ref, *rest):
    parts, own_ref, other_ref, held, sems = rest[:-4], rest[-4], rest[-3], rest[-2], rest[-1]
    units, cols = parts[0].shape
    copies = []
    for s in range(lines):
        row = pl.multiple_of(lax.rem(at_ref[0] - s + lines, lines) * units, 128)
        copies.append(pltpu.make_async_copy(parts[s], held.at[pl.ds(row, units)], sems.at[s]))
    for copy in copies:
        copy.start()
    for copy in copies:
        copy.wait()
    capacity = acts_ref.shape[1] // 2
    own = jnp.concatenate([acts_ref[d, :capacity] for d in range(lines)], axis=0)
    other = jnp.concatenate([acts_ref[d, capacity:] for d in range(lines)], axis=0)
    for at in range(0, cols, 256):
        own_ref[:, at : at + 256] = dot(own, held[:, at : at + 256])
        other_ref[:, at : at + 256] = dot(other, held[:, at : at + 256]).astype(BF16)


def down(dp, acts, parts):
    lines, (units, cols) = len(parts), parts[0].shape
    slots = acts.shape[0] * acts.shape[1] // 2
    return pl.pallas_call(
        functools.partial(down_kernel, lines),
        out_shape=[shape((slots, cols), F32), shape((slots, cols), BF16)],
        in_specs=[SMEM, VMEM] + [ANY] * lines,
        out_specs=[VMEM, VMEM],
        scratch_shapes=[
            pltpu.VMEM((lines * units, cols), BF16),
            pltpu.SemaphoreType.DMA((lines,)),
        ],
        compiler_params=PARAMS,
    )(dp, acts, *parts)


def expand_kernel(own_ref, other_ref, gate_ref, select_ref, out_ref):
    for at in range(0, own_ref.shape[1], 256):
        total = own_ref[:, at : at + 256] + other_ref[:, at : at + 256].astype(F32)
        weighted = (total * gate_ref[...]).astype(BF16)
        out_ref[:, at : at + 256] = dot(select_ref[...], weighted).astype(BF16)


def expand(own, other, gates, select):
    return pl.pallas_call(
        expand_kernel,
        out_shape=shape((select.shape[0], own.shape[1]), BF16),
        in_specs=[VMEM] * 4,
        out_specs=VMEM,
        compiler_params=PARAMS,
    )(own, other, gates, select)


def join_kernel(line_ref, resid_ref, *rest):
    parts, out_ref = rest[:-1], rest[-1]
    total = jnp.dot(
        line_ref[...], resid_ref[...], precision=HIGHEST, preferred_element_type=F32
    )
    for part in parts:
        total = total + part[...].astype(F32)
    out_ref[...] = total.astype(BF16)


def join(line, resid, parts):
    return pl.pallas_call(
        join_kernel,
        out_shape=shape(parts[0].shape, BF16),
        in_specs=[VMEM] * (2 + len(parts)),
        out_specs=VMEM,
        compiler_params=PARAMS,
    )(line, resid, *parts)


def shards(
    queries,
    cache_vals,
    cache_scales,
    cache_len,
    fresh_vals,
    fresh_scales,
    fresh_len,
    fresh_owner,
    hidden,
    w_uv,
    w_out,
    norm_gain,
    route_ids,
    route_weights,
    w_gate,
    w_up,
    w_down,
):
    pd, dp, ep = lax.axis_index("pd"), lax.axis_index("dp"), lax.axis_index("ep")
    n_pd, n_dp, n_ep = lax.axis_size("pd"), lax.axis_size("dp"), lax.axis_size("ep")
    heads, key_width = queries.shape[1:]
    width = hidden.shape[1]
    cols = width // n_dp
    units = w_gate.shape[2]

    chips_y = CHIPS_Y
    chips_z = n_ep // chips_y
    z_groups = [[z * chips_y + y for z in range(chips_z)] for y in range(chips_y)]
    place_y = ep % chips_y

    def shift_y(value, amount):
        pairs = [
            (z * chips_y + y, z * chips_y + (y + amount) % chips_y)
            for z in range(chips_z)
            for y in range(chips_y)
        ]
        return lax.ppermute(value, "ep", pairs)

    at_dp = dp.astype(jnp.int32).reshape(1)
    parcels = make_parcels(at_dp, n_dp, fresh_owner, queries, hidden)
    parcels = list(parcels[:1]) + [shift(parcels[s], "dp", s) for s in range(1, n_dp)]
    gain = lax.dynamic_slice_in_dim(norm_gain, dp * cols, cols, 0)[None]

    whole, first = lax.optimization_barrier((queries, parcels[1]))

    order = np.arange(heads).reshape(n_pd, chips_z, chips_y).transpose(1, 0, 2).reshape(heads)
    order = jnp.asarray(np.eye(heads)[order], BF16)
    packed = old_attention(
        at_dp,
        n_dp,
        cache_len,
        whole,
        order,
        cache_vals[0].T,
        cache_scales[0],
        w_gate[0],
        w_up[0],
        w_down[0],
        chips_z,
    )
    old_out, packed = packed[0], packed[1:]
    uv_own = w_uv[0]
    out_own = lax.dynamic_slice_in_dim(w_out, dp * cols, cols, 1)
    old_out, uv_own, out_own, rest = lax.optimization_barrier(
        (old_out, uv_own, out_own, parcels[2:])
    )
    parcels = [parcels[0], first] + list(rest)
    uv_parts = [uv_own] + [shift_y(uv_own, s) for s in range(1, chips_y)]
    out_parts = [out_own] + [shift_y(out_own, s) for s in range(1, chips_y)]
    parcels, packed = lax.optimization_barrier((parcels, packed))
    both_parts = [packed[0]] + [shift(packed[2 * s], "dp", s) for s in range(1, n_dp)]
    down_parts = [packed[1]] + [shift(packed[2 * s + 1], "dp", s) for s in range(1, n_dp)]
    step = (dp - fresh_owner) % n_dp
    latent = new_attention(
        step, fresh_len, order, fresh_vals[0].T, fresh_scales[0], old_out, parcels
    )
    latent, uv_parts = lax.optimization_barrier((latent, uv_parts))
    slab = 2 * n_ep
    capacity = 2 * slab * route_ids.shape[1] // n_ep
    latent, ids, gates, parcels = lax.optimization_barrier(
        (latent, route_ids.T, route_weights.T, parcels)
    )
    at = jnp.stack([pd, ep, place_y, ep // chips_y]).astype(jnp.int32)
    masks = make_masks(
        at,
        (chips_y, chips_z, n_dp, capacity),
        lax.dynamic_slice_in_dim(ids, pd * n_dp * slab, n_dp * slab, 1),
        lax.dynamic_slice_in_dim(gates, pd * n_dp * slab, n_dp * slab, 1),
    )
    head_rows = exchange(latent, "ep", z_groups)
    line = line_rows(at_dp, heads, gain, parcels)
    head_rows, near, uv_all, masks, line = lax.optimization_barrier(
        (head_rows, out_parts[1::2], jnp.stack(uv_parts), masks, line)
    )
    select, select_back, slot_gate, head_order, own_line = masks
    own, other = sort_rows(head_order, head_rows.reshape(2 * chips_z * heads // chips_z, DLAT))
    values = head_values(n_dp, own, shift(other, "pd", 1), uv_all)
    values, far = lax.optimization_barrier((values, out_parts[2]))
    out_parts = [out_own, near[0], far, near[1]]
    values = exchange(values, "dp")
    values, both_far = lax.optimization_barrier((values, both_parts[2]))
    rows = n_dp * 2 * chips_z * 2
    order = np.arange(rows).reshape(n_dp, 2, chips_z, 2).transpose(1, 2, 0, 3).reshape(rows)
    order = jnp.asarray(np.eye(rows)[order], BF16)
    own, other = project(values.reshape(rows, chips_y * 128), order, out_parts)
    partial = (own + shift(other, "pd", 1).astype(F32)).astype(BF16)
    summands = exchange(partial.reshape(chips_z, n_dp * 2, cols), "ep", z_groups)
    resid_cols, parcel = residual(summands, line)
    column = exchange(parcel, "ep", z_groups)
    column, near = lax.optimization_barrier((column, both_parts[1::2]))
    both_parts = [both_parts[0], near[0], both_far, near[1]]
    column = column.reshape(chips_z * n_dp * 2, cols + 128)
    columns = [column] + [shift_y(column, s) for s in range(1, chips_y)]
    columns, down_parts = lax.optimization_barrier((columns, down_parts))
    slot_rows = select_rows(at, select, columns)
    other_rows = shift(slot_rows, "pd", 1)

    halves = gate_up(at_dp, slot_rows, other_rows, both_parts)
    all_acts = exchange(activations(width, units, exchange(halves, "dp")), "dp")
    own, other = down(at_dp, all_acts, down_parts)
    table = expand(own, shift(other, "pd", 1), slot_gate, select_back)
    table = table.reshape(chips_y, n_dp * chips_z * 2, cols)
    parts = [lax.dynamic_index_in_dim(table, place_y, 0, keepdims=False)]
    for s in range(1, chips_y):
        part = lax.dynamic_index_in_dim(table, (place_y + s) % chips_y, 0, keepdims=False)
        parts.append(shift_y(part, s))
    table = join(own_line, resid_cols, parts).reshape(n_dp * chips_z, 2, cols)
    planes = [
        [d * n_ep + z * chips_y + y for d in range(n_dp) for z in range(chips_z)]
        for y in range(chips_y)
    ]
    table = exchange(table, ("dp", "ep"), planes).reshape(n_dp, chips_z, 2, cols)
    out = jnp.sum(table.astype(F32), axis=1).astype(BF16)
    return out.transpose(1, 0, 2).reshape(2, width)


def solution(mesh):
    in_specs = (
        P(("pd", "dp", "ep"), None, None),
        P(("pd", "dp", "ep"), None, None),
        P(("pd", "dp", "ep"), None, None),
        P(("pd", "dp", "ep")),
        P(("pd", "dp", "ep"), None, None),
        P(("pd", "dp", "ep"), None, None),
        P(("pd", "dp", "ep")),
        P(("pd", "dp", "ep")),
        P(("pd", "dp", "ep"), None),
        P(("pd", "ep"), None, None),
        P(("pd", "ep"), None),
        P(),
        P(),
        P(),
        P("ep", None, ("pd", "dp")),
        P("ep", None, ("pd", "dp")),
        P("ep", ("pd", "dp"), None),
    )
    out_specs = P(("pd", "dp", "ep"), None)
    return jax.shard_map(shards, mesh=mesh, in_specs=in_specs, out_specs=out_specs, check_vma=False)
```

```python
import functools

import jax
import jax.numpy as jnp
import numpy as np
from jax import lax
from jax.experimental import pallas as pl
from jax.experimental.pallas import tpu as pltpu
from jax.sharding import PartitionSpec as P

DLAT = 512
CHIPS_Y = 4


SOFT_SCALE = 0.07216878364870323
EPSILON = 1e-06
BF16 = jnp.bfloat16
F32 = jnp.float32


def shift(value, axis, amount):
    size = lax.axis_size(axis)
    return lax.ppermute(value, axis, [(i, (i + amount) % size) for i in range(size)])


def exchange(value, axis, groups=None):
    return lax.all_to_all(value, axis, 0, 0, axis_index_groups=groups)


def dot(left, right):
    return jnp.dot(left, right, preferred_element_type=F32)


HIGHEST = lax.Precision.HIGHEST
VMEM = pl.BlockSpec(memory_space=pltpu.VMEM)
SMEM = pl.BlockSpec(memory_space=pltpu.SMEM)
HBM = pl.BlockSpec(memory_space=pltpu.HBM)
ANY = pl.BlockSpec(memory_space=pl.ANY)
PARAMS = pltpu.CompilerParams(vmem_limit_bytes=16 * 1024 * 1024)
WIDE = pltpu.CompilerParams(vmem_limit_bytes=58 * 1024 * 1024)


def shape(dims, dtype):
    return jax.ShapeDtypeStruct(dims, dtype)


def attend(query, keys_ref, scales_ref, length, held_ref):
    for block in range(scales_ref.shape[0]):
        at = slice(block * 128, block * 128 + 128)
        scale = scales_ref[...].astype(F32)[block : block + 1]
        held_ref[at] = (keys_ref[at].astype(F32) * scale).astype(BF16)
    scores = dot(query[:, :DLAT], held_ref[...]) + dot(query[:, DLAT:], keys_ref[DLAT:])
    scores = scores * SOFT_SCALE
    token = lax.broadcasted_iota(jnp.int32, scores.shape, 1)
    scores = jnp.where(token < length, scores, -1e30)
    weights = jnp.exp(scores - jnp.max(scores, axis=1, keepdims=True))
    probs = (weights / jnp.sum(weights, axis=1, keepdims=True)).astype(BF16)
    return lax.dot_general(
        probs, held_ref[...], (((1,), (1,)), ((), ())), preferred_element_type=F32
    )


def parcel_kernel(lines, at_ref, owner_ref, query_ref, hidden_ref, *outs):
    heads, wide = query_ref.shape[1:]
    cols = hidden_ref.shape[1] // lines
    lanes = outs[0].shape[1]
    for s in range(lines):
        start = pl.multiple_of(lax.rem(at_ref[0] + s, lines) * cols, 128)
        hidden = hidden_ref[:, pl.ds(start, cols)].astype(F32)
        parts = [hidden[:, at : at + lanes] for at in range(0, cols, lanes)]
        parts = [jnp.pad(part, ((0, 0), (0, lanes - part.shape[1]))) for part in parts]
        used = 2 * len(parts)
        parts.append(jnp.full((16 - used, lanes), owner_ref[0].astype(F32)))
        outs[s][:heads, :wide] = query_ref[1]
        outs[s][:heads, wide:] = jnp.zeros((heads, lanes - wide), BF16)
        outs[s][heads:] = jnp.concatenate(parts, axis=0).astype(BF16)


def make_parcels(dp, lines, owner, query, hidden):
    out = shape((query.shape[1] + 16, -(-query.shape[2] // 128) * 128), BF16)
    return pl.pallas_call(
        functools.partial(parcel_kernel, lines),
        out_shape=[out] * lines,
        in_specs=[SMEM, SMEM, VMEM, VMEM],
        out_specs=[VMEM] * lines,
        compiler_params=PARAMS,
    )(dp, owner, query, hidden)


def mask_kernel(sizes, at_ref, ids_ref, gates_ref, before_ref, there_ref, back_ref, *outs):
    chips_y, chips_z, lines, capacity = sizes
    select_ref, table_ref, gate_ref, line_ref = outs
    expert, place_z = at_ref[1], at_ref[3]
    rows, slots = ids_ref.shape[1], lines * capacity
    hits = ids_ref[...] == expert
    routed = jnp.sum(jnp.where(hits, 1.0, 0.0), axis=0, keepdims=True)
    gates = jnp.sum(jnp.where(hits, gates_ref[...], 0.0), axis=0, keepdims=True)
    place = dot(jnp.broadcast_to(routed, (8, rows)).astype(BF16), before_ref[...])[:1]
    lane = lax.broadcasted_iota(jnp.int32, (1, rows), 1)
    first = lax.div(lane, rows // lines) * capacity
    slot = jnp.where(routed > 0.0, place + first.astype(F32), -1.0)
    wide = jnp.broadcast_to(slot, (8, rows)).astype(BF16)
    slot_iota = lax.broadcasted_iota(jnp.int32, (slots, rows), 0).astype(F32)
    select_ref[...] = jnp.where(dot(wide, there_ref[...])[:1] == slot_iota, 1.0, 0.0).astype(BF16)
    back = jnp.where(dot(wide, back_ref[...])[:1] == slot_iota, 1.0, 0.0)
    table_ref[...] = back.T.astype(BF16)
    gate_ref[...] = jnp.sum(jnp.where(slot == slot_iota, gates, 0.0), axis=1, keepdims=True)
    pairs = 2 * chips_z
    out = lax.broadcasted_iota(jnp.int32, line_ref.shape, 0)
    come = lax.broadcasted_iota(jnp.int32, line_ref.shape, 1)
    own = lax.rem(lax.div(out, 2), chips_z) == place_z
    own = own & (lax.div(out, pairs) * 2 + lax.rem(out, 2) == come)
    line_ref[...] = jnp.where(own, 1.0, 0.0)


def make_masks(at, sizes, ids, gates):
    chips_y, chips_z, lines, capacity = sizes
    rows, slots, pairs = ids.shape[1], lines * capacity, 2 * chips_z
    canon = np.arange(rows).reshape(lines, chips_z, chips_y, 2)
    eye = np.eye(rows)
    before = np.kron(np.eye(lines), np.triu(np.ones((rows // lines, rows // lines)), 1))
    there = eye[canon.transpose(2, 1, 0, 3).reshape(rows)].T
    back = eye[canon.transpose(2, 0, 1, 3).reshape(rows)].T
    return pl.pallas_call(
        functools.partial(mask_kernel, sizes),
        out_shape=[
            shape((slots, rows), BF16),
            shape((rows, slots), BF16),
            shape((slots, 1), F32),
            shape((lines * pairs, 2 * lines), F32),
        ],
        in_specs=[SMEM] + [VMEM] * 5,
        out_specs=[VMEM] * 4,
        compiler_params=PARAMS,
    )(at, ids, gates, *(jnp.asarray(m, BF16) for m in (before, there, back)))


def old_kernel(lines, at_ref, len_ref, query_ref, order_ref, keys_ref, scales_ref, *rest):
    gate_ref, up_ref, down_ref, out_ref = rest[:4]
    outs, held_ref, sems = rest[4:-2], rest[-2], rest[-1]
    cols, units = outs[1].shape[1], gate_ref.shape[1]
    copies = []
    for s in range(lines):
        start = pl.multiple_of(lax.rem(at_ref[0] + s, lines) * cols, 128)
        both, down = outs[2 * s], outs[2 * s + 1]
        copies.append((gate_ref.at[pl.ds(start, cols)], both.at[:, pl.ds(0, units)]))
        copies.append((up_ref.at[pl.ds(start, cols)], both.at[:, pl.ds(units, units)]))
        copies.append((down_ref.at[:, pl.ds(start, cols)], down))
    copies = [pltpu.make_async_copy(a, b, sems.at[i]) for i, (a, b) in enumerate(copies)]
    for copy in copies:
        copy.start()
    query = dot(order_ref[...], query_ref[0]).astype(BF16)
    result = attend(query, keys_ref, scales_ref, len_ref[0], held_ref)
    rows = out_ref.shape[1]
    for z in range(out_ref.shape[0]):
        out_ref[z] = result[z * rows : (z + 1) * rows].astype(BF16)
    for copy in copies:
        copy.wait()


def old_attention(dp, lines, length, query, order, keys, scales, gate, up, down, pieces):
    cols, units = gate.shape[0] // lines, gate.shape[1]
    rows = query.shape[1] // pieces
    return pl.pallas_call(
        functools.partial(old_kernel, lines),
        out_shape=[shape((pieces, rows, DLAT), BF16)]
        + [shape((cols, 2 * units), BF16), shape((units, cols), BF16)] * lines,
        in_specs=[SMEM, SMEM] + [VMEM] * 4 + [HBM] * 3,
        out_specs=[VMEM] * (2 * lines + 1),
        scratch_shapes=[
            pltpu.VMEM((DLAT, keys.shape[1]), BF16),
            pltpu.SemaphoreType.DMA((3 * lines,)),
        ],
        compiler_params=WIDE,
        cost_estimate=pl.CostEstimate(
            flops=2 * query.size * keys.shape[1],
            bytes_accessed=2 * (keys.size + 2 * (gate.size + up.size + down.size)),
            transcendentals=query.shape[1] * keys.shape[1],
        ),
    )(dp, length, query, order, keys, scales, gate, up, down)


def new_kernel(lines, step_ref, len_ref, order_ref, keys_ref, scales_ref, old_ref, *rest):
    parcel_refs, out_ref, held_ref = rest[:lines], rest[lines], rest[lines + 1]
    heads, width = order_ref.shape[0], keys_ref.shape[0]
    query = parcel_refs[0][:heads, :width]
    for s in range(1, lines):
        query = jnp.where(step_ref[0] == s, parcel_refs[s][:heads, :width], query)
    query = dot(order_ref[...], query).astype(BF16)
    result = attend(query, keys_ref, scales_ref, len_ref[0], held_ref)
    rows = out_ref.shape[2]
    for z in range(out_ref.shape[0]):
        out_ref[z, 0] = old_ref[z]
        out_ref[z, 1] = result[z * rows : (z + 1) * rows].astype(BF16)


def new_attention(step, length, order, keys, scales, old, parcels):
    return pl.pallas_call(
        functools.partial(new_kernel, len(parcels)),
        out_shape=shape((old.shape[0], 2) + old.shape[1:], BF16),
        in_specs=[SMEM, SMEM] + [VMEM] * (4 + len(parcels)),
        out_specs=VMEM,
        scratch_shapes=[pltpu.VMEM((DLAT, keys.shape[1]), BF16)],
        compiler_params=PARAMS,
    )(step, length, order, keys, scales, old, *parcels)


def sort_kernel(chips_y, at_ref, rows_ref, own_ref, other_ref):
    half = own_ref.shape[0]
    pairs = half // chips_y
    core, place_y = at_ref[0], at_ref[2]
    out = lax.broadcasted_iota(jnp.int32, (2 * half, 2 * half), 0)
    want = lax.div(out, half)
    want = jnp.where(want == 0, core, 1 - core)
    turn = lax.rem(place_y - lax.rem(lax.div(out, pairs), chips_y) + chips_y, chips_y)
    want = lax.rem(out, pairs) * (2 * chips_y) + want * chips_y + turn
    come = lax.broadcasted_iota(jnp.int32, (2 * half, 2 * half), 1)
    order = jnp.where(want == come, 1.0, 0.0).astype(BF16)
    result = dot(order, rows_ref[...]).astype(BF16)
    own_ref[...] = result[:half]
    other_ref[...] = result[half:]


def sort_rows(at, chips_y, rows):
    half = shape((rows.shape[0] // 2, rows.shape[1]), BF16)
    return pl.pallas_call(
        functools.partial(sort_kernel, chips_y),
        out_shape=[half, half],
        in_specs=[SMEM, VMEM],
        out_specs=[VMEM, VMEM],
        compiler_params=PARAMS,
    )(at, rows)


def values_kernel(own_ref, other_ref, uv_ref, out_ref):
    count, _, width = uv_ref.shape
    rows = own_ref.shape[0] // count
    for s in range(count):
        for q, ref in enumerate((own_ref, other_ref)):
            result = dot(ref[s * rows : (s + 1) * rows], uv_ref[s]).astype(BF16)
            for i in range(out_ref.shape[0]):
                out_ref[i, q * rows : (q + 1) * rows, s * width : (s + 1) * width] = result


def head_values(lines, own, other, uv_all):
    count, _, width = uv_all.shape
    return pl.pallas_call(
        values_kernel,
        out_shape=shape((lines, 2 * own.shape[0] // count, count * width), BF16),
        in_specs=[VMEM] * 3,
        out_specs=VMEM,
        compiler_params=PARAMS,
    )(own, other, uv_all)


def project_kernel(values_ref, order_ref, *rest):
    out_refs, own_ref, other_ref = rest[:-2], rest[-2], rest[-1]
    rows = values_ref.shape[0] // 2
    values = dot(order_ref[...], values_ref[...]).astype(BF16)
    width = out_refs[0].shape[0]
    for start in range(0, own_ref.shape[1], 256):
        total = sum(
            dot(values[:, s * width : (s + 1) * width], ref[:, start : start + 256])
            for s, ref in enumerate(out_refs)
        )
        own_ref[:, start : start + 256] = total[:rows]
        other_ref[:, start : start + 256] = total[rows:].astype(BF16)


def project(values, order, out_parts):
    rows, cols = values.shape[0] // 2, out_parts[0].shape[1]
    return pl.pallas_call(
        project_kernel,
        out_shape=[shape((rows, cols), F32), shape((rows, cols), BF16)],
        in_specs=[VMEM] * (2 + len(out_parts)),
        out_specs=[VMEM, VMEM],
        compiler_params=PARAMS,
    )(values, order, *out_parts)


def line_kernel(heads, at_ref, gain_ref, *rest):
    parcel_refs, out_ref = rest[:-1], rest[-1]
    lines, cols = len(parcel_refs), gain_ref.shape[1]
    row = lax.broadcasted_iota(jnp.int32, (2 * lines, 128), 0)
    come = lax.broadcasted_iota(jnp.int32, (2 * lines, 128), 1)
    same = lax.rem(row, 2) == lax.rem(come, 2)
    old = lax.rem(row, 2) == 0
    row, come = lax.div(row, 2), lax.div(come, 2)
    order = jnp.where(same & old & (row == come), 1.0, 0.0)
    turned = jnp.zeros_like(order)
    hidden = []
    for s, ref in enumerate(parcel_refs):
        source = lax.rem(at_ref[0] - s + lines, lines)
        lower = ref[heads:].astype(F32)
        lanes = lower.shape[1]
        count = -(-cols // lanes)
        owner = lower[2 * count : 2 * count + 1, :1]
        moved = same & ~old & (come == source) & (row.astype(F32) == owner)
        order = order + jnp.where(moved, 1.0, 0.0)
        turned = turned + jnp.where(same & (come == s) & (row == source), 1.0, 0.0)
        pieces = [
            lower[2 * j : 2 * j + 2, : min(lanes, cols - j * lanes)] for j in range(count)
        ]
        hidden.append(jnp.concatenate(pieces, axis=1))
    hidden = jnp.concatenate(hidden, axis=0)
    rows = 2 * lines
    out_ref[:rows] = jnp.dot(
        turned[:, :rows], hidden, precision=HIGHEST, preferred_element_type=F32
    )
    out_ref[rows : 2 * rows] = jnp.broadcast_to(gain_ref[...].astype(F32), (rows, cols))
    out_ref[2 * rows :, :128] = order
    out_ref[2 * rows :, 128:] = jnp.zeros((rows, cols - 128), F32)


def line_rows(dp, heads, gain, parcels):
    return pl.pallas_call(
        functools.partial(line_kernel, heads),
        out_shape=shape((6 * len(parcels), gain.shape[1]), F32),
        in_specs=[SMEM] + [VMEM] * (1 + len(parcels)),
        out_specs=VMEM,
        compiler_params=PARAMS,
    )(dp, gain, *parcels)


def residual_kernel(sums_ref, line_ref, resid_ref, parcel_ref):
    rows, cols = resid_ref.shape
    total = sums_ref[0].astype(F32)
    for i in range(1, sums_ref.shape[0]):
        total = total + sums_ref[i].astype(F32)
    order = line_ref[2 * rows :, :128][:, :rows]
    resid = jnp.dot(order, total, precision=HIGHEST, preferred_element_type=F32)
    resid = resid + line_ref[:rows]
    resid_ref[...] = resid
    squares = jnp.sum(resid * resid, axis=1, keepdims=True)
    high = squares.astype(BF16)
    low = (squares - high.astype(F32)).astype(BF16)
    lanes = lax.broadcasted_iota(jnp.int32, (rows, 128), 1)
    beside = jnp.where(lanes < 64, high.astype(F32), low.astype(F32)).astype(BF16)
    parcel = (resid * line_ref[rows : 2 * rows]).astype(BF16)
    for i in range(parcel_ref.shape[0]):
        parcel_ref[i, :, :cols] = parcel
        parcel_ref[i, :, cols:] = beside


def residual(sums, line):
    copies, rows, cols = sums.shape
    return pl.pallas_call(
        residual_kernel,
        out_shape=[shape((rows, cols), F32), shape((copies, rows, cols + 128), BF16)],
        in_specs=[VMEM, VMEM],
        out_specs=[VMEM, VMEM],
        compiler_params=PARAMS,
    )(sums, line)


def select_kernel(at_ref, select_ref, *rest):
    columns, out_ref, held_ref = rest[:-2], rest[-2], rest[-1]
    count, rows = len(columns), columns[0].shape[0]
    for s, ref in enumerate(columns):
        held_ref[lax.rem(at_ref[2] - s + count, count)] = ref[...]
    for at in range(0, out_ref.shape[1], 384):
        lanes = slice(at, min(at + 384, out_ref.shape[1]))
        gathered = held_ref[:, :, lanes].reshape(count * rows, lanes.stop - at)
        out_ref[:, lanes] = dot(select_ref[...], gathered).astype(BF16)


def select_rows(at, select, columns):
    return pl.pallas_call(
        select_kernel,
        out_shape=shape((select.shape[0], columns[0].shape[1]), BF16),
        in_specs=[SMEM] + [VMEM] * (1 + len(columns)),
        out_specs=VMEM,
        scratch_shapes=[pltpu.VMEM((len(columns),) + columns[0].shape, BF16)],
        compiler_params=PARAMS,
    )(at, select, *columns)


def acts_kernel(width, units, sums_ref, out_ref):
    total = sums_ref[0].astype(F32)
    for i in range(1, sums_ref.shape[0]):
        total = total + sums_ref[i].astype(F32)
    end = sums_ref.shape[2] - 128
    squares = total[:, end : end + 1] + total[:, end + 64 : end + 65]
    scale = lax.rsqrt(squares / width + EPSILON)
    for j in range(end // (2 * units)):
        at = 2 * units * j
        gate = total[:, at : at + units] * scale
        up = total[:, at + units : at + 2 * units] * scale
        acts = (gate / (1.0 + jnp.exp(-gate)) * up).astype(BF16)
        for i in range(out_ref.shape[0]):
            out_ref[i, :, j * units : (j + 1) * units] = acts


def activations(width, units, sums):
    lines, rows, lanes = sums.shape
    return pl.pallas_call(
        functools.partial(acts_kernel, width, units),
        out_shape=shape((lines, rows, (lanes - 128) // 2), BF16),
        in_specs=[VMEM],
        out_specs=VMEM,
        compiler_params=PARAMS,
    )(sums)


def gate_up_kernel(lines, at_ref, own_ref, other_ref, *rest):
    parts, out_ref, held, sems = rest[:-3], rest[-3], rest[-2], rest[-1]
    cols, lanes = held.shape[1:]
    copies = [pltpu.make_async_copy(parts[s], held.at[s], sems.at[s]) for s in range(lines)]
    for copy in copies:
        copy.start()
    for s in range(lines):
        copies[s].wait()
        lane = pl.multiple_of(lax.rem(at_ref[0] - s + lines, lines) * lanes, 128)
        for q, ref in enumerate((own_ref, other_ref)):
            capacity = ref.shape[0] // lines
            result = dot(ref[:, :cols], held[s]).astype(BF16)
            for d in range(lines):
                out_ref[d, q * capacity : (q + 1) * capacity, pl.ds(lane, lanes)] = result[
                    d * capacity : (d + 1) * capacity
                ]
    for q, ref in enumerate((own_ref, other_ref)):
        capacity = ref.shape[0] // lines
        for d in range(lines):
            out_ref[d, q * capacity : (q + 1) * capacity, lines * lanes :] = ref[
                d * capacity : (d + 1) * capacity, cols:
            ]


def gate_up(dp, own, other, parts):
    lines, (cols, lanes) = len(parts), parts[0].shape
    return pl.pallas_call(
        functools.partial(gate_up_kernel, lines),
        out_shape=shape((lines, 2 * own.shape[0] // lines, lines * lanes + 128), BF16),
        in_specs=[SMEM, VMEM, VMEM] + [ANY] * lines,
        out_specs=VMEM,
        scratch_shapes=[
            pltpu.VMEM((lines, cols, lanes), BF16),
            pltpu.SemaphoreType.DMA((lines,)),
        ],
        compiler_params=PARAMS,
    )(dp, own, other, *parts)


def down_kernel(lines, at_ref, acts_ref, *rest):
    parts, own_ref, other_ref, held, sems = rest[:-4], rest[-4], rest[-3], rest[-2], rest[-1]
    units, cols = parts[0].shape
    copies = []
    for s in range(lines):
        row = pl.multiple_of(lax.rem(at_ref[0] - s + lines, lines) * units, 128)
        copies.append(pltpu.make_async_copy(parts[s], held.at[pl.ds(row, units)], sems.at[s]))
    for copy in copies:
        copy.start()
    for copy in copies:
        copy.wait()
    capacity = acts_ref.shape[1] // 2
    own = jnp.concatenate([acts_ref[d, :capacity] for d in range(lines)], axis=0)
    other = jnp.concatenate([acts_ref[d, capacity:] for d in range(lines)], axis=0)
    for at in range(0, cols, 256):
        own_ref[:, at : at + 256] = dot(own, held[:, at : at + 256])
        other_ref[:, at : at + 256] = dot(other, held[:, at : at + 256]).astype(BF16)


def down(dp, acts, parts):
    lines, (units, cols) = len(parts), parts[0].shape
    slots = acts.shape[0] * acts.shape[1] // 2
    return pl.pallas_call(
        functools.partial(down_kernel, lines),
        out_shape=[shape((slots, cols), F32), shape((slots, cols), BF16)],
        in_specs=[SMEM, VMEM] + [ANY] * lines,
        out_specs=[VMEM, VMEM],
        scratch_shapes=[
            pltpu.VMEM((lines * units, cols), BF16),
            pltpu.SemaphoreType.DMA((lines,)),
        ],
        compiler_params=PARAMS,
    )(dp, acts, *parts)


def expand_kernel(own_ref, other_ref, gate_ref, select_ref, out_ref):
    for at in range(0, own_ref.shape[1], 256):
        total = own_ref[:, at : at + 256] + other_ref[:, at : at + 256].astype(F32)
        weighted = (total * gate_ref[...]).astype(BF16)
        out_ref[:, at : at + 256] = dot(select_ref[...], weighted).astype(BF16)


def expand(own, other, gates, select):
    return pl.pallas_call(
        expand_kernel,
        out_shape=shape((select.shape[0], own.shape[1]), BF16),
        in_specs=[VMEM] * 4,
        out_specs=VMEM,
        compiler_params=PARAMS,
    )(own, other, gates, select)


def join_kernel(line_ref, resid_ref, *rest):
    parts, out_ref = rest[:-1], rest[-1]
    total = jnp.dot(
        line_ref[...], resid_ref[...], precision=HIGHEST, preferred_element_type=F32
    )
    for part in parts:
        total = total + part[...].astype(F32)
    out_ref[...] = total.astype(BF16)


def join(line, resid, parts):
    return pl.pallas_call(
        join_kernel,
        out_shape=shape(parts[0].shape, BF16),
        in_specs=[VMEM] * (2 + len(parts)),
        out_specs=VMEM,
        compiler_params=PARAMS,
    )(line, resid, *parts)


def shards(
    queries,
    cache_vals,
    cache_scales,
    cache_len,
    fresh_vals,
    fresh_scales,
    fresh_len,
    fresh_owner,
    hidden,
    w_uv,
    w_out,
    norm_gain,
    route_ids,
    route_weights,
    w_gate,
    w_up,
    w_down,
):
    pd, dp, ep = lax.axis_index("pd"), lax.axis_index("dp"), lax.axis_index("ep")
    n_pd, n_dp, n_ep = lax.axis_size("pd"), lax.axis_size("dp"), lax.axis_size("ep")
    heads, key_width = queries.shape[1:]
    width = hidden.shape[1]
    cols = width // n_dp
    units = w_gate.shape[2]

    chips_y = CHIPS_Y
    chips_z = n_ep // chips_y
    z_groups = [[z * chips_y + y for z in range(chips_z)] for y in range(chips_y)]
    place_y = ep % chips_y

    def shift_y(value, amount):
        pairs = [
            (z * chips_y + y, z * chips_y + (y + amount) % chips_y)
            for z in range(chips_z)
            for y in range(chips_y)
        ]
        return lax.ppermute(value, "ep", pairs)

    at_dp = dp.astype(jnp.int32).reshape(1)
    parcels = make_parcels(at_dp, n_dp, fresh_owner, queries, hidden)
    parcels = list(parcels[:1]) + [shift(parcels[s], "dp", s) for s in range(1, n_dp)]
    gain = lax.dynamic_slice_in_dim(norm_gain, dp * cols, cols, 0)[None]

    whole, first = lax.optimization_barrier((queries, parcels[1]))

    order = np.arange(heads).reshape(n_pd, chips_z, chips_y).transpose(1, 0, 2).reshape(heads)
    order = jnp.asarray(np.eye(heads)[order], BF16)
    packed = old_attention(
        at_dp,
        n_dp,
        cache_len,
        whole,
        order,
        cache_vals[0].T,
        cache_scales[0],
        w_gate[0],
        w_up[0],
        w_down[0],
        chips_z,
    )
    old_out, packed = packed[0], packed[1:]
    uv_own = w_uv[0]
    out_own = lax.dynamic_slice_in_dim(w_out, dp * cols, cols, 1)
    uv_parts = [uv_own] + [shift_y(uv_own, s) for s in range(1, chips_y)]
    out_parts = [out_own] + [shift_y(out_own, s) for s in range(1, chips_y)]
    old_out, rest, uv_parts = lax.optimization_barrier((old_out, parcels[2:], uv_parts))
    parcels = [parcels[0], first] + list(rest)
    parcels, packed = lax.optimization_barrier((parcels, packed))
    both_parts = [packed[0]] + [shift(packed[2 * s], "dp", s) for s in range(1, n_dp)]
    down_parts = [packed[1]] + [shift(packed[2 * s + 1], "dp", s) for s in range(1, n_dp)]
    step = (dp - fresh_owner) % n_dp
    latent = new_attention(
        step, fresh_len, order, fresh_vals[0].T, fresh_scales[0], old_out, parcels
    )
    slab = 2 * n_ep
    capacity = 2 * slab * route_ids.shape[1] // n_ep
    latent, ids, gates, parcels = lax.optimization_barrier(
        (latent, route_ids.T, route_weights.T, parcels)
    )
    at = jnp.stack([pd, ep, place_y, ep // chips_y]).astype(jnp.int32)
    masks = make_masks(
        at,
        (chips_y, chips_z, n_dp, capacity),
        lax.dynamic_slice_in_dim(ids, pd * n_dp * slab, n_dp * slab, 1),
        lax.dynamic_slice_in_dim(gates, pd * n_dp * slab, n_dp * slab, 1),
    )
    head_rows = exchange(latent, "ep", z_groups)
    line = line_rows(at_dp, heads, gain, parcels)
    head_rows, near, uv_all, masks, line = lax.optimization_barrier(
        (head_rows, out_parts[1::2], jnp.stack(uv_parts), masks, line)
    )
    select, select_back, slot_gate, own_line = masks
    own, other = sort_rows(at, chips_y, head_rows.reshape(2 * chips_z * heads // chips_z, DLAT))
    values = head_values(n_dp, own, shift(other, "pd", 1), uv_all)
    values, far = lax.optimization_barrier((values, out_parts[2]))
    out_parts = [out_own, near[0], far, near[1]]
    values = exchange(values, "dp")
    values, near = lax.optimization_barrier((values, both_parts[1::2]))
    rows = n_dp * 2 * chips_z * 2
    order = np.arange(rows).reshape(n_dp, 2, chips_z, 2).transpose(1, 2, 0, 3).reshape(rows)
    order = jnp.asarray(np.eye(rows)[order], BF16)
    own, other = project(values.reshape(rows, chips_y * 128), order, out_parts)
    partial = (own + shift(other, "pd", 1).astype(F32)).astype(BF16)
    summands = exchange(partial.reshape(chips_z, n_dp * 2, cols), "ep", z_groups)
    resid_cols, parcel = residual(summands, line)
    column = exchange(parcel, "ep", z_groups)
    column, far = lax.optimization_barrier((column, both_parts[2]))
    both_parts = [both_parts[0], near[0], far, near[1]]
    column = column.reshape(chips_z * n_dp * 2, cols + 128)
    columns = [column] + [shift_y(column, s) for s in range(1, chips_y)]
    columns, down_parts = lax.optimization_barrier((columns, down_parts))
    slot_rows = select_rows(at, select, columns)
    other_rows = shift(slot_rows, "pd", 1)

    halves = gate_up(at_dp, slot_rows, other_rows, both_parts)
    all_acts = exchange(activations(width, units, exchange(halves, "dp")), "dp")
    own, other = down(at_dp, all_acts, down_parts)
    table = expand(own, shift(other, "pd", 1), slot_gate, select_back)
    table = table.reshape(chips_y, n_dp * chips_z * 2, cols)
    parts = [lax.dynamic_index_in_dim(table, place_y, 0, keepdims=False)]
    for s in range(1, chips_y):
        part = lax.dynamic_index_in_dim(table, (place_y + s) % chips_y, 0, keepdims=False)
        parts.append(shift_y(part, s))
    table = join(own_line, resid_cols, parts).reshape(n_dp * chips_z, 2, cols)
    planes = [
        [d * n_ep + z * chips_y + y for d in range(n_dp) for z in range(chips_z)]
        for y in range(chips_y)
    ]
    table = exchange(table, ("dp", "ep"), planes).reshape(n_dp, chips_z, 2, cols)
    out = jnp.sum(table.astype(F32), axis=1).astype(BF16)
    return out.transpose(1, 0, 2).reshape(2, width)


def solution(mesh):
    in_specs = (
        P(("pd", "dp", "ep"), None, None),
        P(("pd", "dp", "ep"), None, None),
        P(("pd", "dp", "ep"), None, None),
        P(("pd", "dp", "ep")),
        P(("pd", "dp", "ep"), None, None),
        P(("pd", "dp", "ep"), None, None),
        P(("pd", "dp", "ep")),
        P(("pd", "dp", "ep")),
        P(("pd", "dp", "ep"), None),
        P(("pd", "ep"), None, None),
        P(("pd", "ep"), None),
        P(),
        P(),
        P(),
        P("ep", None, ("pd", "dp")),
        P("ep", None, ("pd", "dp")),
        P("ep", ("pd", "dp"), None),
    )
    out_specs = P(("pd", "dp", "ep"), None)
    return jax.shard_map(shards, mesh=mesh, in_specs=in_specs, out_specs=out_specs, check_vma=False)
```

```python
import functools

import jax
import jax.numpy as jnp
import numpy as np
from jax import lax
from jax.experimental import pallas as pl
from jax.experimental.pallas import tpu as pltpu
from jax.sharding import PartitionSpec as P

DLAT = 512
CHIPS_Y = 4


SOFT_SCALE = 0.07216878364870323
EPSILON = 1e-06
BF16 = jnp.bfloat16
F32 = jnp.float32


def shift(value, axis, amount):
    size = lax.axis_size(axis)
    return lax.ppermute(value, axis, [(i, (i + amount) % size) for i in range(size)])


def exchange(value, axis, groups=None):
    return lax.all_to_all(value, axis, 0, 0, axis_index_groups=groups)


def dot(left, right):
    return jnp.dot(left, right, preferred_element_type=F32)


HIGHEST = lax.Precision.HIGHEST
VMEM = pl.BlockSpec(memory_space=pltpu.VMEM)
SMEM = pl.BlockSpec(memory_space=pltpu.SMEM)
HBM = pl.BlockSpec(memory_space=pltpu.HBM)
ANY = pl.BlockSpec(memory_space=pl.ANY)
PARAMS = pltpu.CompilerParams(vmem_limit_bytes=16 * 1024 * 1024)
WIDE = pltpu.CompilerParams(vmem_limit_bytes=58 * 1024 * 1024)


def shape(dims, dtype):
    return jax.ShapeDtypeStruct(dims, dtype)


def attend(query, keys_ref, scales_ref, length, held_ref):
    for block in range(scales_ref.shape[0]):
        at = slice(block * 128, block * 128 + 128)
        scale = scales_ref[...].astype(F32)[block : block + 1]
        held_ref[at] = (keys_ref[at].astype(F32) * scale).astype(BF16)
    scores = dot(query[:, :DLAT], held_ref[...]) + dot(query[:, DLAT:], keys_ref[DLAT:])
    scores = scores * SOFT_SCALE
    token = lax.broadcasted_iota(jnp.int32, scores.shape, 1)
    scores = jnp.where(token < length, scores, -1e30)
    weights = jnp.exp(scores - jnp.max(scores, axis=1, keepdims=True))
    probs = (weights / jnp.sum(weights, axis=1, keepdims=True)).astype(BF16)
    return lax.dot_general(
        probs, held_ref[...], (((1,), (1,)), ((), ())), preferred_element_type=F32
    )


def parcel_kernel(lines, at_ref, owner_ref, query_ref, hidden_ref, *outs):
    heads, wide = query_ref.shape[1:]
    cols = hidden_ref.shape[1] // lines
    lanes = outs[0].shape[1]
    for s in range(lines):
        start = pl.multiple_of(lax.rem(at_ref[0] + s, lines) * cols, 128)
        hidden = hidden_ref[:, pl.ds(start, cols)].astype(F32)
        parts = [hidden[:, at : at + lanes] for at in range(0, cols, lanes)]
        parts = [jnp.pad(part, ((0, 0), (0, lanes - part.shape[1]))) for part in parts]
        used = 2 * len(parts)
        parts.append(jnp.full((16 - used, lanes), owner_ref[0].astype(F32)))
        outs[s][:heads, :wide] = query_ref[1]
        outs[s][:heads, wide:] = jnp.zeros((heads, lanes - wide), BF16)
        outs[s][heads:] = jnp.concatenate(parts, axis=0).astype(BF16)


def make_parcels(dp, lines, owner, query, hidden):
    out = shape((query.shape[1] + 16, -(-query.shape[2] // 128) * 128), BF16)
    return pl.pallas_call(
        functools.partial(parcel_kernel, lines),
        out_shape=[out] * lines,
        in_specs=[SMEM, SMEM, VMEM, VMEM],
        out_specs=[VMEM] * lines,
        compiler_params=PARAMS,
    )(dp, owner, query, hidden)


def mask_kernel(sizes, at_ref, ids_ref, gates_ref, before_ref, there_ref, back_ref, *outs):
    chips_y, chips_z, lines, capacity = sizes
    select_ref, table_ref, gate_ref, line_ref = outs
    expert, place_z = at_ref[1], at_ref[3]
    rows, slots = ids_ref.shape[1], lines * capacity
    hits = ids_ref[...] == expert
    routed = jnp.sum(jnp.where(hits, 1.0, 0.0), axis=0, keepdims=True)
    gates = jnp.sum(jnp.where(hits, gates_ref[...], 0.0), axis=0, keepdims=True)
    place = dot(jnp.broadcast_to(routed, (8, rows)).astype(BF16), before_ref[...])[:1]
    lane = lax.broadcasted_iota(jnp.int32, (1, rows), 1)
    first = lax.div(lane, rows // lines) * capacity
    slot = jnp.where(routed > 0.0, place + first.astype(F32), -1.0)
    wide = jnp.broadcast_to(slot, (8, rows)).astype(BF16)
    slot_iota = lax.broadcasted_iota(jnp.int32, (slots, rows), 0).astype(F32)
    select_ref[...] = jnp.where(dot(wide, there_ref[...])[:1] == slot_iota, 1.0, 0.0).astype(BF16)
    back = jnp.where(dot(wide, back_ref[...])[:1] == slot_iota, 1.0, 0.0)
    table_ref[...] = back.T.astype(BF16)
    gate_ref[...] = jnp.sum(jnp.where(slot == slot_iota, gates, 0.0), axis=1, keepdims=True)
    pairs = 2 * chips_z
    out = lax.broadcasted_iota(jnp.int32, line_ref.shape, 0)
    come = lax.broadcasted_iota(jnp.int32, line_ref.shape, 1)
    own = lax.rem(lax.div(out, 2), chips_z) == place_z
    own = own & (lax.div(out, pairs) * 2 + lax.rem(out, 2) == come)
    line_ref[...] = jnp.where(own, 1.0, 0.0)


def make_masks(at, sizes, ids, gates):
    chips_y, chips_z, lines, capacity = sizes
    rows, slots, pairs = ids.shape[1], lines * capacity, 2 * chips_z
    canon = np.arange(rows).reshape(lines, chips_z, chips_y, 2)
    eye = np.eye(rows)
    before = np.kron(np.eye(lines), np.triu(np.ones((rows // lines, rows // lines)), 1))
    there = eye[canon.transpose(2, 1, 0, 3).reshape(rows)].T
    back = eye[canon.transpose(2, 0, 1, 3).reshape(rows)].T
    return pl.pallas_call(
        functools.partial(mask_kernel, sizes),
        out_shape=[
            shape((slots, rows), BF16),
            shape((rows, slots), BF16),
            shape((slots, 1), F32),
            shape((lines * pairs, 2 * lines), F32),
        ],
        in_specs=[SMEM] + [VMEM] * 5,
        out_specs=[VMEM] * 4,
        compiler_params=PARAMS,
    )(at, ids, gates, *(jnp.asarray(m, BF16) for m in (before, there, back)))


def old_kernel(lines, at_ref, len_ref, query_ref, order_ref, keys_ref, scales_ref, *rest):
    gate_ref, up_ref, down_ref, out_ref = rest[:4]
    outs, held_ref, sems = rest[4:-2], rest[-2], rest[-1]
    cols, units = gate_ref.shape[0] // lines, gate_ref.shape[1]
    copies = []
    for s, out in enumerate(outs):
        start = pl.multiple_of(lax.rem(at_ref[0] + s, lines) * cols, 128)
        copies.append((gate_ref.at[pl.ds(start, cols)], out.at[pl.ds(0, cols), pl.ds(0, units)]))
        copies.append((up_ref.at[pl.ds(start, cols)], out.at[pl.ds(0, cols), pl.ds(units, units)]))
        for block in range(cols // 256):
            at = pl.multiple_of(start + block * 256, 128)
            to = out.at[pl.ds(cols + block * units, units)]
            copies.append((down_ref.at[:, pl.ds(at, 256)], to))
    copies = [pltpu.make_async_copy(a, b, sems.at[i]) for i, (a, b) in enumerate(copies)]
    for copy in copies:
        copy.start()
    query = dot(order_ref[...], query_ref[0]).astype(BF16)
    result = attend(query, keys_ref, scales_ref, len_ref[0], held_ref)
    rows = out_ref.shape[1]
    for z in range(out_ref.shape[0]):
        out_ref[z] = result[z * rows : (z + 1) * rows].astype(BF16)
    for copy in copies:
        copy.wait()


def old_attention(dp, lines, length, query, order, keys, scales, gate, up, down, pieces):
    cols, units = gate.shape[0] // lines, gate.shape[1]
    rows = query.shape[1] // pieces
    return pl.pallas_call(
        functools.partial(old_kernel, lines),
        out_shape=[shape((pieces, rows, DLAT), BF16)]
        + [shape((cols + cols // 256 * units, 256), BF16)] * lines,
        in_specs=[SMEM, SMEM] + [VMEM] * 4 + [HBM] * 3,
        out_specs=[VMEM] * (lines + 1),
        scratch_shapes=[
            pltpu.VMEM((DLAT, keys.shape[1]), BF16),
            pltpu.SemaphoreType.DMA(((2 + cols // 256) * lines,)),
        ],
        compiler_params=WIDE,
        cost_estimate=pl.CostEstimate(
            flops=2 * query.size * keys.shape[1],
            bytes_accessed=2 * (keys.size + 2 * (gate.size + up.size + down.size)),
            transcendentals=query.shape[1] * keys.shape[1],
        ),
    )(dp, length, query, order, keys, scales, gate, up, down)


def new_kernel(lines, step_ref, len_ref, order_ref, keys_ref, scales_ref, old_ref, *rest):
    parcel_refs, out_ref, held_ref = rest[:lines], rest[lines], rest[lines + 1]
    heads, width = order_ref.shape[0], keys_ref.shape[0]
    query = parcel_refs[0][:heads, :width]
    for s in range(1, lines):
        query = jnp.where(step_ref[0] == s, parcel_refs[s][:heads, :width], query)
    query = dot(order_ref[...], query).astype(BF16)
    result = attend(query, keys_ref, scales_ref, len_ref[0], held_ref)
    rows = out_ref.shape[2]
    for z in range(out_ref.shape[0]):
        out_ref[z, 0] = old_ref[z]
        out_ref[z, 1] = result[z * rows : (z + 1) * rows].astype(BF16)


def new_attention(step, length, order, keys, scales, old, parcels):
    return pl.pallas_call(
        functools.partial(new_kernel, len(parcels)),
        out_shape=shape((old.shape[0], 2) + old.shape[1:], BF16),
        in_specs=[SMEM, SMEM] + [VMEM] * (4 + len(parcels)),
        out_specs=VMEM,
        scratch_shapes=[pltpu.VMEM((DLAT, keys.shape[1]), BF16)],
        compiler_params=WIDE,
    )(step, length, order, keys, scales, old, *parcels)


def sort_kernel(chips_y, at_ref, rows_ref, own_ref, other_ref):
    half = own_ref.shape[0]
    pairs = half // chips_y
    core, place_y = at_ref[0], at_ref[2]
    out = lax.broadcasted_iota(jnp.int32, (2 * half, 2 * half), 0)
    want = lax.div(out, half)
    want = jnp.where(want == 0, core, 1 - core)
    turn = lax.rem(place_y - lax.rem(lax.div(out, pairs), chips_y) + chips_y, chips_y)
    want = lax.rem(out, pairs) * (2 * chips_y) + want * chips_y + turn
    come = lax.broadcasted_iota(jnp.int32, (2 * half, 2 * half), 1)
    order = jnp.where(want == come, 1.0, 0.0).astype(BF16)
    result = dot(order, rows_ref[...]).astype(BF16)
    own_ref[...] = result[:half]
    other_ref[...] = result[half:]


def sort_rows(at, chips_y, rows):
    half = shape((rows.shape[0] // 2, rows.shape[1]), BF16)
    return pl.pallas_call(
        functools.partial(sort_kernel, chips_y),
        out_shape=[half, half],
        in_specs=[SMEM, VMEM],
        out_specs=[VMEM, VMEM],
        compiler_params=PARAMS,
    )(at, rows)


def values_kernel(own_ref, other_ref, uv_ref, out_ref):
    count, _, width = uv_ref.shape
    rows = own_ref.shape[0] // count
    for s in range(count):
        for q, ref in enumerate((own_ref, other_ref)):
            result = dot(ref[s * rows : (s + 1) * rows], uv_ref[s]).astype(BF16)
            for i in range(out_ref.shape[0]):
                out_ref[i, q * rows : (q + 1) * rows, s * width : (s + 1) * width] = result


def head_values(lines, own, other, uv_all):
    count, _, width = uv_all.shape
    return pl.pallas_call(
        values_kernel,
        out_shape=shape((lines, 2 * own.shape[0] // count, count * width), BF16),
        in_specs=[VMEM] * 3,
        out_specs=VMEM,
        compiler_params=PARAMS,
    )(own, other, uv_all)


def project_kernel(values_ref, order_ref, *rest):
    out_refs, own_ref, other_ref = rest[:-2], rest[-2], rest[-1]
    rows = values_ref.shape[0] // 2
    values = dot(order_ref[...], values_ref[...]).astype(BF16)
    width = out_refs[0].shape[0]
    for start in range(0, own_ref.shape[1], 256):
        total = sum(
            dot(values[:, s * width : (s + 1) * width], ref[:, start : start + 256])
            for s, ref in enumerate(out_refs)
        )
        own_ref[:, start : start + 256] = total[:rows]
        other_ref[:, start : start + 256] = total[rows:].astype(BF16)


def project(values, order, out_parts):
    rows, cols = values.shape[0] // 2, out_parts[0].shape[1]
    return pl.pallas_call(
        project_kernel,
        out_shape=[shape((rows, cols), F32), shape((rows, cols), BF16)],
        in_specs=[VMEM] * (2 + len(out_parts)),
        out_specs=[VMEM, VMEM],
        compiler_params=PARAMS,
    )(values, order, *out_parts)


def line_kernel(heads, at_ref, gain_ref, *rest):
    parcel_refs, out_ref = rest[:-1], rest[-1]
    lines, cols = len(parcel_refs), gain_ref.shape[1]
    row = lax.broadcasted_iota(jnp.int32, (2 * lines, 128), 0)
    come = lax.broadcasted_iota(jnp.int32, (2 * lines, 128), 1)
    same = lax.rem(row, 2) == lax.rem(come, 2)
    old = lax.rem(row, 2) == 0
    row, come = lax.div(row, 2), lax.div(come, 2)
    order = jnp.where(same & old & (row == come), 1.0, 0.0)
    turned = jnp.zeros_like(order)
    hidden = []
    for s, ref in enumerate(parcel_refs):
        source = lax.rem(at_ref[0] - s + lines, lines)
        lower = ref[heads:].astype(F32)
        lanes = lower.shape[1]
        count = -(-cols // lanes)
        owner = lower[2 * count : 2 * count + 1, :1]
        moved = same & ~old & (come == source) & (row.astype(F32) == owner)
        order = order + jnp.where(moved, 1.0, 0.0)
        turned = turned + jnp.where(same & (come == s) & (row == source), 1.0, 0.0)
        pieces = [
            lower[2 * j : 2 * j + 2, : min(lanes, cols - j * lanes)] for j in range(count)
        ]
        hidden.append(jnp.concatenate(pieces, axis=1))
    hidden = jnp.concatenate(hidden, axis=0)
    rows = 2 * lines
    out_ref[:rows] = jnp.dot(
        turned[:, :rows], hidden, precision=HIGHEST, preferred_element_type=F32
    )
    out_ref[rows : 2 * rows] = jnp.broadcast_to(gain_ref[...].astype(F32), (rows, cols))
    out_ref[2 * rows :, :128] = order
    out_ref[2 * rows :, 128:] = jnp.zeros((rows, cols - 128), F32)


def line_rows(dp, heads, gain, parcels):
    return pl.pallas_call(
        functools.partial(line_kernel, heads),
        out_shape=shape((6 * len(parcels), gain.shape[1]), F32),
        in_specs=[SMEM] + [VMEM] * (1 + len(parcels)),
        out_specs=VMEM,
        compiler_params=PARAMS,
    )(dp, gain, *parcels)


def residual_kernel(sums_ref, line_ref, resid_ref, parcel_ref):
    rows, cols = resid_ref.shape
    total = sums_ref[0].astype(F32)
    for i in range(1, sums_ref.shape[0]):
        total = total + sums_ref[i].astype(F32)
    order = line_ref[2 * rows :, :128][:, :rows]
    resid = jnp.dot(order, total, precision=HIGHEST, preferred_element_type=F32)
    resid = resid + line_ref[:rows]
    resid_ref[...] = resid
    squares = jnp.sum(resid * resid, axis=1, keepdims=True)
    high = squares.astype(BF16)
    low = (squares - high.astype(F32)).astype(BF16)
    lanes = lax.broadcasted_iota(jnp.int32, (rows, 128), 1)
    beside = jnp.where(lanes < 64, high.astype(F32), low.astype(F32)).astype(BF16)
    parcel = (resid * line_ref[rows : 2 * rows]).astype(BF16)
    for i in range(parcel_ref.shape[0]):
        parcel_ref[i, :, :cols] = parcel
        parcel_ref[i, :, cols:] = beside


def residual(sums, line):
    copies, rows, cols = sums.shape
    return pl.pallas_call(
        residual_kernel,
        out_shape=[shape((rows, cols), F32), shape((copies, rows, cols + 128), BF16)],
        in_specs=[VMEM, VMEM],
        out_specs=[VMEM, VMEM],
        compiler_params=PARAMS,
    )(sums, line)


def select_kernel(at_ref, select_ref, *rest):
    columns, out_ref, held_ref = rest[:-2], rest[-2], rest[-1]
    count, rows = len(columns), columns[0].shape[0]
    for s, ref in enumerate(columns):
        held_ref[lax.rem(at_ref[2] - s + count, count)] = ref[...]
    for at in range(0, out_ref.shape[1], 384):
        lanes = slice(at, min(at + 384, out_ref.shape[1]))
        gathered = held_ref[:, :, lanes].reshape(count * rows, lanes.stop - at)
        out_ref[:, lanes] = dot(select_ref[...], gathered).astype(BF16)


def select_rows(at, select, columns):
    return pl.pallas_call(
        select_kernel,
        out_shape=shape((select.shape[0], columns[0].shape[1]), BF16),
        in_specs=[SMEM] + [VMEM] * (1 + len(columns)),
        out_specs=VMEM,
        scratch_shapes=[pltpu.VMEM((len(columns),) + columns[0].shape, BF16)],
        compiler_params=PARAMS,
    )(at, select, *columns)


def acts_kernel(width, units, sums_ref, out_ref):
    total = sums_ref[0].astype(F32)
    for i in range(1, sums_ref.shape[0]):
        total = total + sums_ref[i].astype(F32)
    end = sums_ref.shape[2] - 128
    squares = total[:, end : end + 1] + total[:, end + 64 : end + 65]
    scale = lax.rsqrt(squares / width + EPSILON)
    for j in range(end // (2 * units)):
        at = 2 * units * j
        gate = total[:, at : at + units] * scale
        up = total[:, at + units : at + 2 * units] * scale
        acts = (gate / (1.0 + jnp.exp(-gate)) * up).astype(BF16)
        for i in range(out_ref.shape[0]):
            out_ref[i, :, j * units : (j + 1) * units] = acts


def activations(width, units, sums):
    lines, rows, lanes = sums.shape
    return pl.pallas_call(
        functools.partial(acts_kernel, width, units),
        out_shape=shape((lines, rows, (lanes - 128) // 2), BF16),
        in_specs=[VMEM],
        out_specs=VMEM,
        compiler_params=PARAMS,
    )(sums)


def gate_up_kernel(lines, at_ref, own_ref, other_ref, *rest):
    parts, out_ref, held, sems = rest[:-3], rest[-3], rest[-2], rest[-1]
    cols, lanes = held.shape[1:]
    copies = [
        pltpu.make_async_copy(parts[s].at[pl.ds(0, cols)], held.at[s], sems.at[s])
        for s in range(lines)
    ]
    for copy in copies:
        copy.start()
    for s in range(lines):
        copies[s].wait()
        lane = pl.multiple_of(lax.rem(at_ref[0] - s + lines, lines) * lanes, 128)
        for q, ref in enumerate((own_ref, other_ref)):
            capacity = ref.shape[0] // lines
            result = dot(ref[:, :cols], held[s]).astype(BF16)
            for d in range(lines):
                out_ref[d, q * capacity : (q + 1) * capacity, pl.ds(lane, lanes)] = result[
                    d * capacity : (d + 1) * capacity
                ]
    for q, ref in enumerate((own_ref, other_ref)):
        capacity = ref.shape[0] // lines
        for d in range(lines):
            out_ref[d, q * capacity : (q + 1) * capacity, lines * lanes :] = ref[
                d * capacity : (d + 1) * capacity, cols:
            ]


def gate_up(dp, own, other, parts):
    lines, cols, lanes = len(parts), own.shape[1] - 128, parts[0].shape[1]
    return pl.pallas_call(
        functools.partial(gate_up_kernel, lines),
        out_shape=shape((lines, 2 * own.shape[0] // lines, lines * lanes + 128), BF16),
        in_specs=[SMEM, VMEM, VMEM] + [ANY] * lines,
        out_specs=VMEM,
        scratch_shapes=[
            pltpu.VMEM((lines, cols, lanes), BF16),
            pltpu.SemaphoreType.DMA((lines,)),
        ],
        compiler_params=PARAMS,
    )(dp, own, other, *parts)


def down_kernel(lines, at_ref, acts_ref, *rest):
    parts, own_ref, other_ref, held, sems = rest[:-4], rest[-4], rest[-3], rest[-2], rest[-1]
    blocks, units = held.shape[0], held.shape[1] // lines
    copies = []
    for s in range(lines):
        row = pl.multiple_of(lax.rem(at_ref[0] - s + lines, lines) * units, 128)
        for block in range(blocks):
            at = blocks * 256 + block * units
            part = parts[s].at[pl.ds(at, units)]
            to = held.at[block, pl.ds(row, units)]
            copies.append(pltpu.make_async_copy(part, to, sems.at[s * blocks + block]))
    for copy in copies:
        copy.start()
    for copy in copies:
        copy.wait()
    capacity = acts_ref.shape[1] // 2
    own = jnp.concatenate([acts_ref[d, :capacity] for d in range(lines)], axis=0)
    other = jnp.concatenate([acts_ref[d, capacity:] for d in range(lines)], axis=0)
    for block in range(blocks):
        at = block * 256
        own_ref[:, at : at + 256] = dot(own, held[block]).astype(BF16)
        other_ref[:, at : at + 256] = dot(other, held[block]).astype(BF16)


def down(dp, acts, parts, cols):
    lines, units = len(parts), acts.shape[2] // len(parts)
    slots = acts.shape[0] * acts.shape[1] // 2
    return pl.pallas_call(
        functools.partial(down_kernel, lines),
        out_shape=[shape((slots, cols), BF16), shape((slots, cols), BF16)],
        in_specs=[SMEM, VMEM] + [ANY] * lines,
        out_specs=[VMEM, VMEM],
        scratch_shapes=[
            pltpu.VMEM((cols // 256, lines * units, 256), BF16),
            pltpu.SemaphoreType.DMA((lines * (cols // 256),)),
        ],
        compiler_params=PARAMS,
    )(dp, acts, *parts)


def expand_kernel(own_ref, other_ref, gate_ref, select_ref, out_ref):
    for at in range(0, own_ref.shape[1], 256):
        total = own_ref[:, at : at + 256].astype(F32) + other_ref[:, at : at + 256].astype(F32)
        weighted = (total * gate_ref[...]).astype(BF16)
        out_ref[:, at : at + 256] = dot(select_ref[...], weighted).astype(BF16)


def expand(own, other, gates, select):
    return pl.pallas_call(
        expand_kernel,
        out_shape=shape((select.shape[0], own.shape[1]), BF16),
        in_specs=[VMEM] * 4,
        out_specs=VMEM,
        compiler_params=PARAMS,
    )(own, other, gates, select)


def join_kernel(line_ref, resid_ref, *rest):
    parts, out_ref = rest[:-1], rest[-1]
    total = jnp.dot(
        line_ref[...], resid_ref[...], precision=HIGHEST, preferred_element_type=F32
    )
    for part in parts:
        total = total + part[...].astype(F32)
    out_ref[...] = total.astype(BF16)


def join(line, resid, parts):
    return pl.pallas_call(
        join_kernel,
        out_shape=shape(parts[0].shape, BF16),
        in_specs=[VMEM] * (2 + len(parts)),
        out_specs=VMEM,
        compiler_params=PARAMS,
    )(line, resid, *parts)


def shards(
    queries,
    cache_vals,
    cache_scales,
    cache_len,
    fresh_vals,
    fresh_scales,
    fresh_len,
    fresh_owner,
    hidden,
    w_uv,
    w_out,
    norm_gain,
    route_ids,
    route_weights,
    w_gate,
    w_up,
    w_down,
):
    pd, dp, ep = lax.axis_index("pd"), lax.axis_index("dp"), lax.axis_index("ep")
    n_pd, n_dp, n_ep = lax.axis_size("pd"), lax.axis_size("dp"), lax.axis_size("ep")
    heads, key_width = queries.shape[1:]
    width = hidden.shape[1]
    cols = width // n_dp
    units = w_gate.shape[2]

    chips_y = CHIPS_Y
    chips_z = n_ep // chips_y
    z_groups = [[z * chips_y + y for z in range(chips_z)] for y in range(chips_y)]
    place_y = ep % chips_y

    def shift_y(value, amount):
        pairs = [
            (z * chips_y + y, z * chips_y + (y + amount) % chips_y)
            for z in range(chips_z)
            for y in range(chips_y)
        ]
        return lax.ppermute(value, "ep", pairs)

    at_dp = dp.astype(jnp.int32).reshape(1)
    parcels = make_parcels(at_dp, n_dp, fresh_owner, queries, hidden)
    parcels = list(parcels[:1]) + [shift(parcels[s], "dp", s) for s in range(1, n_dp)]

    whole, first = lax.optimization_barrier((queries, parcels[1]))

    order = np.arange(heads).reshape(n_pd, chips_z, chips_y).transpose(1, 0, 2).reshape(heads)
    order = jnp.asarray(np.eye(heads)[order], BF16)
    packed = old_attention(
        at_dp,
        n_dp,
        cache_len,
        whole,
        order,
        cache_vals[0].T,
        cache_scales[0],
        w_gate[0],
        w_up[0],
        w_down[0],
        chips_z,
    )
    old_out, packed = packed[0], packed[1:]
    uv_own = w_uv[0]
    out_own = lax.dynamic_slice_in_dim(w_out, dp * cols, cols, 1)
    uv_parts = [uv_own] + [shift_y(uv_own, s) for s in range(1, chips_y)]
    out_parts = [out_own] + [shift_y(out_own, s) for s in range(1, chips_y)]
    old_out, rest, uv_parts = lax.optimization_barrier((old_out, parcels[2:], uv_parts))
    parcels = [parcels[0], first] + list(rest)
    parcels, packed = lax.optimization_barrier((parcels, packed))
    parts = [packed[0]] + [shift(packed[s], "dp", s) for s in range(1, n_dp)]
    step = (dp - fresh_owner) % n_dp
    latent = new_attention(
        step, fresh_len, order, fresh_vals[0].T, fresh_scales[0], old_out, parcels
    )
    slab = 2 * n_ep
    capacity = 2 * slab * route_ids.shape[1] // n_ep
    latent, ids, gates, parcels, norm_gain = lax.optimization_barrier(
        (latent, route_ids.T, route_weights.T, parcels, norm_gain)
    )
    gain = lax.dynamic_slice_in_dim(norm_gain, dp * cols, cols, 0)[None]
    at = jnp.stack([pd, ep, place_y, ep // chips_y]).astype(jnp.int32)
    masks = make_masks(
        at,
        (chips_y, chips_z, n_dp, capacity),
        lax.dynamic_slice_in_dim(ids, pd * n_dp * slab, n_dp * slab, 1),
        lax.dynamic_slice_in_dim(gates, pd * n_dp * slab, n_dp * slab, 1),
    )
    head_rows = exchange(latent, "ep", z_groups)
    line = line_rows(at_dp, heads, gain, parcels)
    head_rows, near, uv_all, masks, line = lax.optimization_barrier(
        (head_rows, out_parts[1::2], jnp.stack(uv_parts), masks, line)
    )
    select, select_back, slot_gate, own_line = masks
    own, other = sort_rows(at, chips_y, head_rows.reshape(2 * chips_z * heads // chips_z, DLAT))
    values = head_values(n_dp, own, shift(other, "pd", 1), uv_all)
    values, far = lax.optimization_barrier((values, out_parts[2]))
    out_parts = [out_own, near[0], far, near[1]]
    values = exchange(values, "dp")
    values, near = lax.optimization_barrier((values, parts[1::2]))
    rows = n_dp * 2 * chips_z * 2
    order = np.arange(rows).reshape(n_dp, 2, chips_z, 2).transpose(1, 2, 0, 3).reshape(rows)
    order = jnp.asarray(np.eye(rows)[order], BF16)
    own, other = project(values.reshape(rows, chips_y * 128), order, out_parts)
    partial = (own + shift(other, "pd", 1).astype(F32)).astype(BF16)
    summands = exchange(partial.reshape(chips_z, n_dp * 2, cols), "ep", z_groups)
    resid_cols, parcel = residual(summands, line)
    column = exchange(parcel, "ep", z_groups)
    column, far = lax.optimization_barrier((column, parts[2]))
    parts = [parts[0], near[0], far, near[1]]
    column = column.reshape(chips_z * n_dp * 2, cols + 128)
    columns = [column] + [shift_y(column, s) for s in range(1, chips_y)]
    slot_rows = select_rows(at, select, columns)
    other_rows = shift(slot_rows, "pd", 1)

    halves = gate_up(at_dp, slot_rows, other_rows, parts)
    all_acts = exchange(activations(width, units, exchange(halves, "dp")), "dp")
    own, other = down(at_dp, all_acts, parts, cols)
    table = expand(own, shift(other, "pd", 1), slot_gate, select_back)
    table = table.reshape(chips_y, n_dp * chips_z * 2, cols)
    pieces = [lax.dynamic_index_in_dim(table, place_y, 0, keepdims=False)]
    for s in range(1, chips_y):
        part = lax.dynamic_index_in_dim(table, (place_y + s) % chips_y, 0, keepdims=False)
        pieces.append(shift_y(part, s))
    table = join(own_line, resid_cols, pieces).reshape(n_dp * chips_z, 2, cols)
    planes = [
        [d * n_ep + z * chips_y + y for d in range(n_dp) for z in range(chips_z)]
        for y in range(chips_y)
    ]
    table = exchange(table, ("dp", "ep"), planes).reshape(n_dp, chips_z, 2, cols)
    out = jnp.sum(table.astype(F32), axis=1).astype(BF16)
    return out.transpose(1, 0, 2).reshape(2, width)


def solution(mesh):
    in_specs = (
        P(("pd", "dp", "ep"), None, None),
        P(("pd", "dp", "ep"), None, None),
        P(("pd", "dp", "ep"), None, None),
        P(("pd", "dp", "ep")),
        P(("pd", "dp", "ep"), None, None),
        P(("pd", "dp", "ep"), None, None),
        P(("pd", "dp", "ep")),
        P(("pd", "dp", "ep")),
        P(("pd", "dp", "ep"), None),
        P(("pd", "ep"), None, None),
        P(("pd", "ep"), None),
        P(),
        P(),
        P(),
        P("ep", None, ("pd", "dp")),
        P("ep", None, ("pd", "dp")),
        P("ep", ("pd", "dp"), None),
    )
    out_specs = P(("pd", "dp", "ep"), None)
    return jax.shard_map(shards, mesh=mesh, in_specs=in_specs, out_specs=out_specs, check_vma=False)
```

```python
import functools

import jax
import jax.numpy as jnp
import numpy as np
from jax import lax
from jax.experimental import pallas as pl
from jax.experimental.pallas import tpu as pltpu
from jax.sharding import PartitionSpec as P

DLAT = 512
CHIPS_Y = 4


SOFT_SCALE = 0.07216878364870323
EPSILON = 1e-06
BF16 = jnp.bfloat16
F32 = jnp.float32


def shift(value, axis, amount):
    size = lax.axis_size(axis)
    return lax.ppermute(value, axis, [(i, (i + amount) % size) for i in range(size)])


def exchange(value, axis, groups=None):
    return lax.all_to_all(value, axis, 0, 0, axis_index_groups=groups)


def dot(left, right):
    return jnp.dot(left, right, preferred_element_type=F32)


HIGHEST = lax.Precision.HIGHEST
VMEM = pl.BlockSpec(memory_space=pltpu.VMEM)
SMEM = pl.BlockSpec(memory_space=pltpu.SMEM)
HBM = pl.BlockSpec(memory_space=pltpu.HBM)
ANY = pl.BlockSpec(memory_space=pl.ANY)
PARAMS = pltpu.CompilerParams(vmem_limit_bytes=16 * 1024 * 1024)
WIDE = pltpu.CompilerParams(vmem_limit_bytes=58 * 1024 * 1024)


def shape(dims, dtype):
    return jax.ShapeDtypeStruct(dims, dtype)


def attend(query, keys_ref, scales_ref, length, held_ref):
    for block in range(scales_ref.shape[0]):
        at = slice(block * 128, block * 128 + 128)
        scale = scales_ref[...].astype(F32)[block : block + 1]
        held_ref[at] = (keys_ref[at].astype(F32) * scale).astype(BF16)
    scores = dot(query[:, :DLAT], held_ref[...]) + dot(query[:, DLAT:], keys_ref[DLAT:])
    scores = scores * SOFT_SCALE
    token = lax.broadcasted_iota(jnp.int32, scores.shape, 1)
    scores = jnp.where(token < length, scores, -1e30)
    weights = jnp.exp(scores - jnp.max(scores, axis=1, keepdims=True))
    probs = (weights / jnp.sum(weights, axis=1, keepdims=True)).astype(BF16)
    return lax.dot_general(
        probs, held_ref[...], (((1,), (1,)), ((), ())), preferred_element_type=F32
    )


def parcel_kernel(lines, at_ref, owner_ref, query_ref, hidden_ref, *outs):
    heads, wide = query_ref.shape[1:]
    cols = hidden_ref.shape[1] // lines
    lanes = outs[0].shape[1]
    for s in range(lines):
        start = pl.multiple_of(lax.rem(at_ref[0] + s, lines) * cols, 128)
        hidden = hidden_ref[:, pl.ds(start, cols)].astype(F32)
        parts = [hidden[:, at : at + lanes] for at in range(0, cols, lanes)]
        parts = [jnp.pad(part, ((0, 0), (0, lanes - part.shape[1]))) for part in parts]
        used = 2 * len(parts)
        parts.append(jnp.full((16 - used, lanes), owner_ref[0].astype(F32)))
        outs[s][:heads, :wide] = query_ref[1]
        outs[s][:heads, wide:] = jnp.zeros((heads, lanes - wide), BF16)
        outs[s][heads:] = jnp.concatenate(parts, axis=0).astype(BF16)


def make_parcels(dp, lines, owner, query, hidden):
    out = shape((query.shape[1] + 16, -(-query.shape[2] // 128) * 128), BF16)
    return pl.pallas_call(
        functools.partial(parcel_kernel, lines),
        out_shape=[out] * lines,
        in_specs=[SMEM, SMEM, VMEM, VMEM],
        out_specs=[VMEM] * lines,
        compiler_params=PARAMS,
    )(dp, owner, query, hidden)


def slots_of(lines, capacity, ids_ref, before_ref):
    rows = ids_ref.shape[1]
    hits = ids_ref[...] == lax.axis_index("ep")
    routed = jnp.sum(jnp.where(hits, 1.0, 0.0), axis=0, keepdims=True)
    place = dot(jnp.broadcast_to(routed, (8, rows)).astype(BF16), before_ref[...])[:1]
    lane = lax.broadcasted_iota(jnp.int32, (1, rows), 1)
    first = lax.div(lane, rows // lines) * capacity
    return hits, jnp.where(routed > 0.0, place + first.astype(F32), -1.0)


def there_kernel(lines, capacity, ids_ref, before_ref, there_ref, select_ref):
    slots, rows = select_ref.shape
    slot = slots_of(lines, capacity, ids_ref, before_ref)[1]
    wide = jnp.broadcast_to(slot, (8, rows)).astype(BF16)
    slot_iota = lax.broadcasted_iota(jnp.int32, (slots, rows), 0).astype(F32)
    select_ref[...] = jnp.where(dot(wide, there_ref[...])[:1] == slot_iota, 1.0, 0.0).astype(BF16)


def back_kernel(sizes, ids_ref, gates_ref, before_ref, back_ref, *outs):
    chips_y, chips_z, lines, capacity = sizes
    table_ref, gate_ref, line_ref = outs
    rows, slots = table_ref.shape
    hits, slot = slots_of(lines, capacity, ids_ref, before_ref)
    gates = jnp.sum(jnp.where(hits, gates_ref[...], 0.0), axis=0, keepdims=True)
    wide = jnp.broadcast_to(slot, (8, rows)).astype(BF16)
    slot_iota = lax.broadcasted_iota(jnp.int32, (slots, rows), 0).astype(F32)
    back = jnp.where(dot(wide, back_ref[...])[:1] == slot_iota, 1.0, 0.0)
    table_ref[...] = back.T.astype(BF16)
    gate_ref[...] = jnp.sum(jnp.where(slot == slot_iota, gates, 0.0), axis=1, keepdims=True)
    pairs = 2 * chips_z
    out = lax.broadcasted_iota(jnp.int32, line_ref.shape, 0)
    come = lax.broadcasted_iota(jnp.int32, line_ref.shape, 1)
    own = lax.rem(lax.div(out, 2), chips_z) == lax.div(lax.axis_index("ep"), chips_y)
    own = own & (lax.div(out, pairs) * 2 + lax.rem(out, 2) == come)
    line_ref[...] = jnp.where(own, 1.0, 0.0)


def orders(sizes, rows, axes):
    chips_y, chips_z, lines, _ = sizes
    slab = rows // lines
    canon = np.arange(rows).reshape(lines, chips_z, chips_y, 2)
    before = np.kron(np.eye(lines), np.triu(np.ones((slab, slab)), 1))
    order = np.eye(rows)[canon.transpose(axes).reshape(rows)].T
    return jnp.asarray(before, BF16), jnp.asarray(order, BF16)


def mask_there(sizes, ids):
    rows, slots = ids.shape[1], sizes[2] * sizes[3]
    return pl.pallas_call(
        functools.partial(there_kernel, sizes[2], sizes[3]),
        out_shape=shape((slots, rows), BF16),
        in_specs=[VMEM] * 3,
        out_specs=VMEM,
        compiler_params=PARAMS,
    )(ids, *orders(sizes, rows, (2, 1, 0, 3)))


def mask_back(sizes, ids, gates):
    rows, slots = ids.shape[1], sizes[2] * sizes[3]
    return pl.pallas_call(
        functools.partial(back_kernel, sizes),
        out_shape=[
            shape((rows, slots), BF16),
            shape((slots, 1), F32),
            shape((sizes[2] * 2 * sizes[1], 2 * sizes[2]), F32),
        ],
        in_specs=[VMEM] * 4,
        out_specs=[VMEM] * 3,
        compiler_params=PARAMS,
    )(ids, gates, *orders(sizes, rows, (2, 0, 1, 3)))


def old_kernel(lines, at_ref, len_ref, query_ref, order_ref, keys_ref, scales_ref, *rest):
    gate_ref, up_ref, down_ref, out_ref = rest[:4]
    outs, held_ref, sems = rest[4:-2], rest[-2], rest[-1]
    cols, units = outs[1].shape[1], gate_ref.shape[1]
    copies = []
    for s in range(lines):
        start = pl.multiple_of(lax.rem(at_ref[0] + s, lines) * cols, 128)
        both, down = outs[2 * s], outs[2 * s + 1]
        copies.append((gate_ref.at[pl.ds(start, cols)], both.at[:, pl.ds(0, units)]))
        copies.append((up_ref.at[pl.ds(start, cols)], both.at[:, pl.ds(units, units)]))
        copies.append((down_ref.at[:, pl.ds(start, cols)], down))
    copies = [pltpu.make_async_copy(a, b, sems.at[i]) for i, (a, b) in enumerate(copies)]
    for copy in copies:
        copy.start()
    query = dot(order_ref[...], query_ref[0]).astype(BF16)
    result = attend(query, keys_ref, scales_ref, len_ref[0], held_ref)
    rows = out_ref.shape[1]
    for z in range(out_ref.shape[0]):
        out_ref[z] = result[z * rows : (z + 1) * rows].astype(BF16)
    for copy in copies:
        copy.wait()


def old_attention(dp, lines, length, query, order, keys, scales, gate, up, down, pieces):
    cols, units = gate.shape[0] // lines, gate.shape[1]
    rows = query.shape[1] // pieces
    return pl.pallas_call(
        functools.partial(old_kernel, lines),
        out_shape=[shape((pieces, rows, DLAT), BF16)]
        + [shape((cols, 2 * units), BF16), shape((units, cols), BF16)] * lines,
        in_specs=[SMEM, SMEM] + [VMEM] * 4 + [HBM] * 3,
        out_specs=[VMEM] * (2 * lines + 1),
        scratch_shapes=[
            pltpu.VMEM((DLAT, keys.shape[1]), BF16),
            pltpu.SemaphoreType.DMA((3 * lines,)),
        ],
        compiler_params=WIDE,
        cost_estimate=pl.CostEstimate(
            flops=2 * query.size * keys.shape[1],
            bytes_accessed=2 * (keys.size + 2 * (gate.size + up.size + down.size)),
            transcendentals=query.shape[1] * keys.shape[1],
        ),
    )(dp, length, query, order, keys, scales, gate, up, down)


def new_kernel(lines, step_ref, len_ref, order_ref, keys_ref, scales_ref, old_ref, *rest):
    parcel_refs, out_ref, held_ref = rest[:lines], rest[lines], rest[lines + 1]
    heads, width = order_ref.shape[0], keys_ref.shape[0]
    query = parcel_refs[0][:heads, :width]
    for s in range(1, lines):
        query = jnp.where(step_ref[0] == s, parcel_refs[s][:heads, :width], query)
    query = dot(order_ref[...], query).astype(BF16)
    result = attend(query, keys_ref, scales_ref, len_ref[0], held_ref)
    rows = out_ref.shape[2]
    for z in range(out_ref.shape[0]):
        out_ref[z, 0] = old_ref[z]
        out_ref[z, 1] = result[z * rows : (z + 1) * rows].astype(BF16)


def new_attention(step, length, order, keys, scales, old, parcels):
    return pl.pallas_call(
        functools.partial(new_kernel, len(parcels)),
        out_shape=shape((old.shape[0], 2) + old.shape[1:], BF16),
        in_specs=[SMEM, SMEM] + [VMEM] * (4 + len(parcels)),
        out_specs=VMEM,
        scratch_shapes=[pltpu.VMEM((DLAT, keys.shape[1]), BF16)],
        compiler_params=PARAMS,
    )(step, length, order, keys, scales, old, *parcels)


def sort_kernel(chips_y, rows_ref, own_ref, other_ref):
    half = own_ref.shape[0]
    pairs = half // chips_y
    core, place_y = lax.axis_index("pd"), lax.rem(lax.axis_index("ep"), chips_y)
    out = lax.broadcasted_iota(jnp.int32, (2 * half, 2 * half), 0)
    want = lax.div(out, half)
    want = jnp.where(want == 0, core, 1 - core)
    turn = lax.rem(place_y - lax.rem(lax.div(out, pairs), chips_y) + chips_y, chips_y)
    want = lax.rem(out, pairs) * (2 * chips_y) + want * chips_y + turn
    come = lax.broadcasted_iota(jnp.int32, (2 * half, 2 * half), 1)
    order = jnp.where(want == come, 1.0, 0.0).astype(BF16)
    result = dot(order, rows_ref[...]).astype(BF16)
    own_ref[...] = result[:half]
    other_ref[...] = result[half:]


def sort_rows(chips_y, rows):
    half = shape((rows.shape[0] // 2, rows.shape[1]), BF16)
    return pl.pallas_call(
        functools.partial(sort_kernel, chips_y),
        out_shape=[half, half],
        in_specs=[VMEM],
        out_specs=[VMEM, VMEM],
        compiler_params=PARAMS,
    )(rows)


def values_kernel(own_ref, other_ref, uv_ref, out_ref):
    count, _, width = uv_ref.shape
    rows = own_ref.shape[0] // count
    for s in range(count):
        for q, ref in enumerate((own_ref, other_ref)):
            result = dot(ref[s * rows : (s + 1) * rows], uv_ref[s]).astype(BF16)
            for i in range(out_ref.shape[0]):
                out_ref[i, q * rows : (q + 1) * rows, s * width : (s + 1) * width] = result


def head_values(lines, own, other, uv_all):
    count, _, width = uv_all.shape
    return pl.pallas_call(
        values_kernel,
        out_shape=shape((lines, 2 * own.shape[0] // count, count * width), BF16),
        in_specs=[VMEM] * 3,
        out_specs=VMEM,
        compiler_params=PARAMS,
    )(own, other, uv_all)


def project_kernel(values_ref, order_ref, *rest):
    out_refs, own_ref, other_ref = rest[:-2], rest[-2], rest[-1]
    rows = values_ref.shape[0] // 2
    values = dot(order_ref[...], values_ref[...]).astype(BF16)
    width = out_refs[0].shape[0]
    for start in range(0, own_ref.shape[1], 256):
        total = sum(
            dot(values[:, s * width : (s + 1) * width], ref[:, start : start + 256])
            for s, ref in enumerate(out_refs)
        )
        own_ref[:, start : start + 256] = total[:rows]
        other_ref[:, start : start + 256] = total[rows:].astype(BF16)


def project(values, order, out_parts):
    rows, cols = values.shape[0] // 2, out_parts[0].shape[1]
    return pl.pallas_call(
        project_kernel,
        out_shape=[shape((rows, cols), F32), shape((rows, cols), BF16)],
        in_specs=[VMEM] * (2 + len(out_parts)),
        out_specs=[VMEM, VMEM],
        compiler_params=PARAMS,
    )(values, order, *out_parts)


def line_kernel(heads, at_ref, gain_ref, *rest):
    parcel_refs, out_ref = rest[:-1], rest[-1]
    lines, cols = len(parcel_refs), gain_ref.shape[1]
    row = lax.broadcasted_iota(jnp.int32, (2 * lines, 128), 0)
    come = lax.broadcasted_iota(jnp.int32, (2 * lines, 128), 1)
    same = lax.rem(row, 2) == lax.rem(come, 2)
    old = lax.rem(row, 2) == 0
    row, come = lax.div(row, 2), lax.div(come, 2)
    order = jnp.where(same & old & (row == come), 1.0, 0.0)
    turned = jnp.zeros_like(order)
    hidden = []
    for s, ref in enumerate(parcel_refs):
        source = lax.rem(at_ref[0] - s + lines, lines)
        lower = ref[heads:].astype(F32)
        lanes = lower.shape[1]
        count = -(-cols // lanes)
        owner = lower[2 * count : 2 * count + 1, :1]
        moved = same & ~old & (come == source) & (row.astype(F32) == owner)
        order = order + jnp.where(moved, 1.0, 0.0)
        turned = turned + jnp.where(same & (come == s) & (row == source), 1.0, 0.0)
        pieces = [
            lower[2 * j : 2 * j + 2, : min(lanes, cols - j * lanes)] for j in range(count)
        ]
        hidden.append(jnp.concatenate(pieces, axis=1))
    hidden = jnp.concatenate(hidden, axis=0)
    rows = 2 * lines
    out_ref[:rows] = jnp.dot(
        turned[:, :rows], hidden, precision=HIGHEST, preferred_element_type=F32
    )
    out_ref[rows : 2 * rows] = jnp.broadcast_to(gain_ref[...].astype(F32), (rows, cols))
    out_ref[2 * rows :, :128] = order
    out_ref[2 * rows :, 128:] = jnp.zeros((rows, cols - 128), F32)


def line_rows(dp, heads, gain, parcels):
    return pl.pallas_call(
        functools.partial(line_kernel, heads),
        out_shape=shape((6 * len(parcels), gain.shape[1]), F32),
        in_specs=[SMEM] + [VMEM] * (1 + len(parcels)),
        out_specs=VMEM,
        compiler_params=PARAMS,
    )(dp, gain, *parcels)


def residual_kernel(sums_ref, line_ref, resid_ref, parcel_ref):
    rows, cols = resid_ref.shape
    total = sums_ref[0].astype(F32)
    for i in range(1, sums_ref.shape[0]):
        total = total + sums_ref[i].astype(F32)
    order = line_ref[2 * rows :, :128][:, :rows]
    resid = jnp.dot(order, total, precision=HIGHEST, preferred_element_type=F32)
    resid = resid + line_ref[:rows]
    resid_ref[...] = resid
    squares = jnp.sum(resid * resid, axis=1, keepdims=True)
    high = squares.astype(BF16)
    low = (squares - high.astype(F32)).astype(BF16)
    lanes = lax.broadcasted_iota(jnp.int32, (rows, 128), 1)
    beside = jnp.where(lanes < 64, high.astype(F32), low.astype(F32)).astype(BF16)
    parcel = (resid * line_ref[rows : 2 * rows]).astype(BF16)
    for i in range(parcel_ref.shape[0]):
        parcel_ref[i, :, :cols] = parcel
        parcel_ref[i, :, cols:] = beside


def residual(sums, line):
    copies, rows, cols = sums.shape
    return pl.pallas_call(
        residual_kernel,
        out_shape=[shape((rows, cols), F32), shape((copies, rows, cols + 128), BF16)],
        in_specs=[VMEM, VMEM],
        out_specs=[VMEM, VMEM],
        compiler_params=PARAMS,
    )(sums, line)


def select_kernel(select_ref, *rest):
    columns, out_ref, held_ref = rest[:-2], rest[-2], rest[-1]
    count, rows = len(columns), columns[0].shape[0]
    for s, ref in enumerate(columns):
        held_ref[lax.rem(lax.rem(lax.axis_index("ep"), count) - s + count, count)] = ref[...]
    for at in range(0, out_ref.shape[1], 384):
        lanes = slice(at, min(at + 384, out_ref.shape[1]))
        gathered = held_ref[:, :, lanes].reshape(count * rows, lanes.stop - at)
        out_ref[:, lanes] = dot(select_ref[...], gathered).astype(BF16)


def select_rows(select, columns):
    return pl.pallas_call(
        select_kernel,
        out_shape=shape((select.shape[0], columns[0].shape[1]), BF16),
        in_specs=[VMEM] * (1 + len(columns)),
        out_specs=VMEM,
        scratch_shapes=[pltpu.VMEM((len(columns),) + columns[0].shape, BF16)],
        compiler_params=PARAMS,
    )(select, *columns)


def acts_kernel(width, units, sums_ref, out_ref):
    total = sums_ref[0].astype(F32)
    for i in range(1, sums_ref.shape[0]):
        total = total + sums_ref[i].astype(F32)
    end = sums_ref.shape[2] - 128
    squares = total[:, end : end + 1] + total[:, end + 64 : end + 65]
    scale = lax.rsqrt(squares / width + EPSILON)
    for j in range(end // (2 * units)):
        at = 2 * units * j
        gate = total[:, at : at + units] * scale
        up = total[:, at + units : at + 2 * units] * scale
        acts = (gate / (1.0 + jnp.exp(-gate)) * up).astype(BF16)
        for i in range(out_ref.shape[0]):
            out_ref[i, :, j * units : (j + 1) * units] = acts


def activations(width, units, sums):
    lines, rows, lanes = sums.shape
    return pl.pallas_call(
        functools.partial(acts_kernel, width, units),
        out_shape=shape((lines, rows, (lanes - 128) // 2), BF16),
        in_specs=[VMEM],
        out_specs=VMEM,
        compiler_params=PARAMS,
    )(sums)


def gate_up_kernel(lines, at_ref, own_ref, other_ref, *rest):
    parts, out_ref, held, sems = rest[:-3], rest[-3], rest[-2], rest[-1]
    cols, lanes = held.shape[1:]
    copies = [pltpu.make_async_copy(parts[s], held.at[s], sems.at[s]) for s in range(lines)]
    for copy in copies:
        copy.start()
    for s in range(lines):
        copies[s].wait()
        lane = pl.multiple_of(lax.rem(at_ref[0] - s + lines, lines) * lanes, 128)
        for q, ref in enumerate((own_ref, other_ref)):
            capacity = ref.shape[0] // lines
            result = dot(ref[:, :cols], held[s]).astype(BF16)
            for d in range(lines):
                out_ref[d, q * capacity : (q + 1) * capacity, pl.ds(lane, lanes)] = result[
                    d * capacity : (d + 1) * capacity
                ]
    for q, ref in enumerate((own_ref, other_ref)):
        capacity = ref.shape[0] // lines
        for d in range(lines):
            out_ref[d, q * capacity : (q + 1) * capacity, lines * lanes :] = ref[
                d * capacity : (d + 1) * capacity, cols:
            ]


def gate_up(dp, own, other, parts):
    lines, (cols, lanes) = len(parts), parts[0].shape
    return pl.pallas_call(
        functools.partial(gate_up_kernel, lines),
        out_shape=shape((lines, 2 * own.shape[0] // lines, lines * lanes + 128), BF16),
        in_specs=[SMEM, VMEM, VMEM] + [ANY] * lines,
        out_specs=VMEM,
        scratch_shapes=[
            pltpu.VMEM((lines, cols, lanes), BF16),
            pltpu.SemaphoreType.DMA((lines,)),
        ],
        compiler_params=PARAMS,
    )(dp, own, other, *parts)


def down_kernel(lines, at_ref, acts_ref, *rest):
    parts, own_ref, other_ref, held, sems = rest[:-4], rest[-4], rest[-3], rest[-2], rest[-1]
    units, cols = parts[0].shape
    copies = []
    for s in range(lines):
        row = pl.multiple_of(lax.rem(at_ref[0] - s + lines, lines) * units, 128)
        copies.append(pltpu.make_async_copy(parts[s], held.at[pl.ds(row, units)], sems.at[s]))
    for copy in copies:
        copy.start()
    for copy in copies:
        copy.wait()
    capacity = acts_ref.shape[1] // 2
    own = jnp.concatenate([acts_ref[d, :capacity] for d in range(lines)], axis=0)
    other = jnp.concatenate([acts_ref[d, capacity:] for d in range(lines)], axis=0)
    for at in range(0, cols, 256):
        own_ref[:, at : at + 256] = dot(own, held[:, at : at + 256]).astype(BF16)
        other_ref[:, at : at + 256] = dot(other, held[:, at : at + 256]).astype(BF16)


def down(dp, acts, parts):
    lines, (units, cols) = len(parts), parts[0].shape
    slots = acts.shape[0] * acts.shape[1] // 2
    return pl.pallas_call(
        functools.partial(down_kernel, lines),
        out_shape=[shape((slots, cols), BF16), shape((slots, cols), BF16)],
        in_specs=[SMEM, VMEM] + [ANY] * lines,
        out_specs=[VMEM, VMEM],
        scratch_shapes=[
            pltpu.VMEM((lines * units, cols), BF16),
            pltpu.SemaphoreType.DMA((lines,)),
        ],
        compiler_params=PARAMS,
    )(dp, acts, *parts)


def expand_kernel(own_ref, other_ref, gate_ref, select_ref, out_ref):
    for at in range(0, own_ref.shape[1], 256):
        total = own_ref[:, at : at + 256].astype(F32) + other_ref[:, at : at + 256].astype(F32)
        weighted = (total * gate_ref[...]).astype(BF16)
        out_ref[:, at : at + 256] = dot(select_ref[...], weighted).astype(BF16)


def expand(own, other, gates, select):
    return pl.pallas_call(
        expand_kernel,
        out_shape=shape((select.shape[0], own.shape[1]), BF16),
        in_specs=[VMEM] * 4,
        out_specs=VMEM,
        compiler_params=PARAMS,
    )(own, other, gates, select)


def join_kernel(line_ref, resid_ref, *rest):
    parts, out_ref = rest[:-1], rest[-1]
    total = jnp.dot(
        line_ref[...], resid_ref[...], precision=HIGHEST, preferred_element_type=F32
    )
    for part in parts:
        total = total + part[...].astype(F32)
    out_ref[...] = total.astype(BF16)


def join(line, resid, parts):
    return pl.pallas_call(
        join_kernel,
        out_shape=shape(parts[0].shape, BF16),
        in_specs=[VMEM] * (2 + len(parts)),
        out_specs=VMEM,
        compiler_params=PARAMS,
    )(line, resid, *parts)


def shards(
    queries,
    cache_vals,
    cache_scales,
    cache_len,
    fresh_vals,
    fresh_scales,
    fresh_len,
    fresh_owner,
    hidden,
    w_uv,
    w_out,
    norm_gain,
    route_ids,
    route_weights,
    w_gate,
    w_up,
    w_down,
):
    pd, dp, ep = lax.axis_index("pd"), lax.axis_index("dp"), lax.axis_index("ep")
    n_pd, n_dp, n_ep = lax.axis_size("pd"), lax.axis_size("dp"), lax.axis_size("ep")
    heads, key_width = queries.shape[1:]
    width = hidden.shape[1]
    cols = width // n_dp
    units = w_gate.shape[2]

    chips_y = CHIPS_Y
    chips_z = n_ep // chips_y
    z_groups = [[z * chips_y + y for z in range(chips_z)] for y in range(chips_y)]
    place_y = ep % chips_y

    def shift_y(value, amount):
        pairs = [
            (z * chips_y + y, z * chips_y + (y + amount) % chips_y)
            for z in range(chips_z)
            for y in range(chips_y)
        ]
        return lax.ppermute(value, "ep", pairs)

    at_dp = dp.astype(jnp.int32).reshape(1)
    parcels = make_parcels(at_dp, n_dp, fresh_owner, queries, hidden)
    parcels = list(parcels[:1]) + [shift(parcels[s], "dp", s) for s in range(1, n_dp)]

    whole, first = lax.optimization_barrier((queries, parcels[1]))

    order = np.arange(heads).reshape(n_pd, chips_z, chips_y).transpose(1, 0, 2).reshape(heads)
    order = jnp.asarray(np.eye(heads)[order], BF16)
    packed = old_attention(
        at_dp,
        n_dp,
        cache_len,
        whole,
        order,
        cache_vals[0].T,
        cache_scales[0],
        w_gate[0],
        w_up[0],
        w_down[0],
        chips_z,
    )
    old_out, packed = packed[0], packed[1:]
    uv_own = w_uv[0]
    out_own = lax.dynamic_slice_in_dim(w_out, dp * cols, cols, 1)
    uv_parts = [uv_own] + [shift_y(uv_own, s) for s in range(1, chips_y)]
    out_parts = [out_own] + [shift_y(out_own, s) for s in range(1, chips_y)]
    old_out, rest, uv_parts = lax.optimization_barrier((old_out, parcels[2:], uv_parts))
    parcels = [parcels[0], first] + list(rest)
    parcels, packed = lax.optimization_barrier((parcels, packed))
    both_parts = [packed[0]] + [shift(packed[2 * s], "dp", s) for s in range(1, n_dp)]
    down_parts = [packed[1]] + [shift(packed[2 * s + 1], "dp", s) for s in range(1, n_dp)]
    step = (dp - fresh_owner) % n_dp
    latent = new_attention(
        step, fresh_len, order, fresh_vals[0].T, fresh_scales[0], old_out, parcels
    )
    slab = 2 * n_ep
    sizes = (chips_y, chips_z, n_dp, 2 * slab * route_ids.shape[1] // n_ep)
    latent, parcels, norm_gain = lax.optimization_barrier((latent, parcels, norm_gain))
    gain = lax.dynamic_slice_in_dim(norm_gain, dp * cols, cols, 0)[None]
    ids = lax.dynamic_slice_in_dim(route_ids.T, pd * n_dp * slab, n_dp * slab, 1)
    gates = lax.dynamic_slice_in_dim(route_weights.T, pd * n_dp * slab, n_dp * slab, 1)
    line = line_rows(at_dp, heads, gain, parcels)
    head_rows = exchange(latent, "ep", z_groups)
    head_rows, near, uv_all, line = lax.optimization_barrier(
        (head_rows, out_parts[1::2], jnp.stack(uv_parts), line)
    )
    own, other = sort_rows(chips_y, head_rows.reshape(2 * chips_z * heads // chips_z, DLAT))
    values = head_values(n_dp, own, shift(other, "pd", 1), uv_all)
    values, far = lax.optimization_barrier((values, out_parts[2]))
    out_parts = [out_own, near[0], far, near[1]]
    values = exchange(values, "dp")
    values, near = lax.optimization_barrier((values, both_parts[1::2]))
    rows = n_dp * 2 * chips_z * 2
    order = np.arange(rows).reshape(n_dp, 2, chips_z, 2).transpose(1, 2, 0, 3).reshape(rows)
    order = jnp.asarray(np.eye(rows)[order], BF16)
    own, other = project(values.reshape(rows, chips_y * 128), order, out_parts)
    partial = (own + shift(other, "pd", 1).astype(F32)).astype(BF16)
    summands = exchange(partial.reshape(chips_z, n_dp * 2, cols), "ep", z_groups)
    resid_cols, parcel = residual(summands, line)
    parcel, ids = lax.optimization_barrier((parcel, ids))
    select = mask_there(sizes, ids)
    column = exchange(parcel, "ep", z_groups)
    column, far, select = lax.optimization_barrier((column, both_parts[2], select))
    both_parts = [both_parts[0], near[0], far, near[1]]
    column = column.reshape(chips_z * n_dp * 2, cols + 128)
    columns = [column] + [shift_y(column, s) for s in range(1, chips_y)]
    columns, down_parts = lax.optimization_barrier((columns, down_parts))
    slot_rows = select_rows(select, columns)
    other_rows = shift(slot_rows, "pd", 1)

    halves = gate_up(at_dp, slot_rows, other_rows, both_parts)
    acts = activations(width, units, exchange(halves, "dp"))
    acts, ids, gates = lax.optimization_barrier((acts, ids, gates))
    masks = mask_back(sizes, ids, gates)
    all_acts, masks = lax.optimization_barrier((exchange(acts, "dp"), masks))
    select_back, slot_gate, own_line = masks
    own, other = down(at_dp, all_acts, down_parts)
    table = expand(own, shift(other, "pd", 1), slot_gate, select_back)
    table = table.reshape(chips_y, n_dp * chips_z * 2, cols)
    parts = [lax.dynamic_index_in_dim(table, place_y, 0, keepdims=False)]
    for s in range(1, chips_y):
        part = lax.dynamic_index_in_dim(table, (place_y + s) % chips_y, 0, keepdims=False)
        parts.append(shift_y(part, s))
    table = join(own_line, resid_cols, parts).reshape(n_dp * chips_z, 2, cols)
    planes = [
        [d * n_ep + z * chips_y + y for d in range(n_dp) for z in range(chips_z)]
        for y in range(chips_y)
    ]
    table = exchange(table, ("dp", "ep"), planes).reshape(n_dp, chips_z, 2, cols)
    out = jnp.sum(table.astype(F32), axis=1).astype(BF16)
    return out.transpose(1, 0, 2).reshape(2, width)


def solution(mesh):
    in_specs = (
        P(("pd", "dp", "ep"), None, None),
        P(("pd", "dp", "ep"), None, None),
        P(("pd", "dp", "ep"), None, None),
        P(("pd", "dp", "ep")),
        P(("pd", "dp", "ep"), None, None),
        P(("pd", "dp", "ep"), None, None),
        P(("pd", "dp", "ep")),
        P(("pd", "dp", "ep")),
        P(("pd", "dp", "ep"), None),
        P(("pd", "ep"), None, None),
        P(("pd", "ep"), None),
        P(),
        P(),
        P(),
        P("ep", None, ("pd", "dp")),
        P("ep", None, ("pd", "dp")),
        P("ep", ("pd", "dp"), None),
    )
    out_specs = P(("pd", "dp", "ep"), None)
    return jax.shard_map(shards, mesh=mesh, in_specs=in_specs, out_specs=out_specs, check_vma=False)
```

```python
import functools

import jax
import jax.numpy as jnp
import numpy as np
from jax import lax
from jax.experimental import pallas as pl
from jax.experimental.pallas import tpu as pltpu
from jax.sharding import PartitionSpec as P

DLAT = 512
CHIPS_Y = 4


SOFT_SCALE = 0.07216878364870323
EPSILON = 1e-06
BF16 = jnp.bfloat16
F32 = jnp.float32


def shift(value, axis, amount):
    size = lax.axis_size(axis)
    return lax.ppermute(value, axis, [(i, (i + amount) % size) for i in range(size)])


def exchange(value, axis, groups=None):
    return lax.all_to_all(value, axis, 0, 0, axis_index_groups=groups)


def dot(left, right):
    return jnp.dot(left, right, preferred_element_type=F32)


HIGHEST = lax.Precision.HIGHEST
VMEM = pl.BlockSpec(memory_space=pltpu.VMEM)
SMEM = pl.BlockSpec(memory_space=pltpu.SMEM)
HBM = pl.BlockSpec(memory_space=pltpu.HBM)
ANY = pl.BlockSpec(memory_space=pl.ANY)
PARAMS = pltpu.CompilerParams(vmem_limit_bytes=16 * 1024 * 1024)
WIDE = pltpu.CompilerParams(vmem_limit_bytes=58 * 1024 * 1024)


def shape(dims, dtype):
    return jax.ShapeDtypeStruct(dims, dtype)


def attend(query, keys_ref, scales_ref, length, held_ref):
    for block in range(scales_ref.shape[0]):
        at = slice(block * 128, block * 128 + 128)
        scale = scales_ref[...].astype(F32)[block : block + 1]
        held_ref[at] = (keys_ref[at].astype(F32) * scale).astype(BF16)
    scores = dot(query[:, :DLAT], held_ref[...]) + dot(query[:, DLAT:], keys_ref[DLAT:])
    scores = scores * SOFT_SCALE
    token = lax.broadcasted_iota(jnp.int32, scores.shape, 1)
    scores = jnp.where(token < length, scores, -1e30)
    weights = jnp.exp(scores - jnp.max(scores, axis=1, keepdims=True))
    probs = (weights / jnp.sum(weights, axis=1, keepdims=True)).astype(BF16)
    return lax.dot_general(
        probs, held_ref[...], (((1,), (1,)), ((), ())), preferred_element_type=F32
    )


def parcel_kernel(lines, at_ref, owner_ref, query_ref, hidden_ref, *outs):
    heads, wide = query_ref.shape[1:]
    cols = hidden_ref.shape[1] // lines
    lanes = outs[0].shape[1]
    for s in range(lines):
        start = pl.multiple_of(lax.rem(at_ref[0] + s, lines) * cols, 128)
        hidden = hidden_ref[:, pl.ds(start, cols)].astype(F32)
        parts = [hidden[:, at : at + lanes] for at in range(0, cols, lanes)]
        parts = [jnp.pad(part, ((0, 0), (0, lanes - part.shape[1]))) for part in parts]
        used = 2 * len(parts)
        parts.append(jnp.full((16 - used, lanes), owner_ref[0].astype(F32)))
        outs[s][:heads, :wide] = query_ref[1]
        outs[s][:heads, wide:] = jnp.zeros((heads, lanes - wide), BF16)
        outs[s][heads:] = jnp.concatenate(parts, axis=0).astype(BF16)


def make_parcels(dp, lines, owner, query, hidden):
    out = shape((query.shape[1] + 16, -(-query.shape[2] // 128) * 128), BF16)
    return pl.pallas_call(
        functools.partial(parcel_kernel, lines),
        out_shape=[out] * lines,
        in_specs=[SMEM, SMEM, VMEM, VMEM],
        out_specs=[VMEM] * lines,
        compiler_params=PARAMS,
    )(dp, owner, query, hidden)


def slots_of(lines, capacity, ids_ref, before_ref):
    rows = ids_ref.shape[1]
    hits = ids_ref[...] == lax.axis_index("ep")
    routed = jnp.sum(jnp.where(hits, 1.0, 0.0), axis=0, keepdims=True)
    place = dot(jnp.broadcast_to(routed, (8, rows)).astype(BF16), before_ref[...])[:1]
    lane = lax.broadcasted_iota(jnp.int32, (1, rows), 1)
    first = lax.div(lane, rows // lines) * capacity
    return hits, jnp.where(routed > 0.0, place + first.astype(F32), -1.0)


def there_kernel(lines, capacity, ids_ref, before_ref, there_ref, select_ref):
    slots, rows = select_ref.shape
    slot = slots_of(lines, capacity, ids_ref, before_ref)[1]
    wide = jnp.broadcast_to(slot, (8, rows)).astype(BF16)
    slot_iota = lax.broadcasted_iota(jnp.int32, (slots, rows), 0).astype(F32)
    select_ref[...] = jnp.where(dot(wide, there_ref[...])[:1] == slot_iota, 1.0, 0.0).astype(BF16)


def back_kernel(sizes, ids_ref, gates_ref, before_ref, back_ref, *outs):
    chips_y, chips_z, lines, capacity = sizes
    table_ref, gate_ref, line_ref = outs
    rows, slots = table_ref.shape
    hits, slot = slots_of(lines, capacity, ids_ref, before_ref)
    gates = jnp.sum(jnp.where(hits, gates_ref[...], 0.0), axis=0, keepdims=True)
    wide = jnp.broadcast_to(slot, (8, rows)).astype(BF16)
    slot_iota = lax.broadcasted_iota(jnp.int32, (slots, rows), 0).astype(F32)
    back = jnp.where(dot(wide, back_ref[...])[:1] == slot_iota, 1.0, 0.0)
    table_ref[...] = back.T.astype(BF16)
    gate_ref[...] = jnp.sum(jnp.where(slot == slot_iota, gates, 0.0), axis=1, keepdims=True)
    pairs = 2 * chips_z
    out = lax.broadcasted_iota(jnp.int32, line_ref.shape, 0)
    come = lax.broadcasted_iota(jnp.int32, line_ref.shape, 1)
    own = lax.rem(lax.div(out, 2), chips_z) == lax.div(lax.axis_index("ep"), chips_y)
    own = own & (lax.div(out, pairs) * 2 + lax.rem(out, 2) == come)
    line_ref[...] = jnp.where(own, 1.0, 0.0)


def orders(sizes, rows, axes):
    chips_y, chips_z, lines, _ = sizes
    slab = rows // lines
    canon = np.arange(rows).reshape(lines, chips_z, chips_y, 2)
    before = np.kron(np.eye(lines), np.triu(np.ones((slab, slab)), 1))
    order = np.eye(rows)[canon.transpose(axes).reshape(rows)].T
    return jnp.asarray(before, BF16), jnp.asarray(order, BF16)


def mask_there(sizes, ids):
    rows, slots = ids.shape[1], sizes[2] * sizes[3]
    return pl.pallas_call(
        functools.partial(there_kernel, sizes[2], sizes[3]),
        out_shape=shape((slots, rows), BF16),
        in_specs=[VMEM] * 3,
        out_specs=VMEM,
        compiler_params=PARAMS,
    )(ids, *orders(sizes, rows, (2, 1, 0, 3)))


def mask_back(sizes, ids, gates):
    rows, slots = ids.shape[1], sizes[2] * sizes[3]
    return pl.pallas_call(
        functools.partial(back_kernel, sizes),
        out_shape=[
            shape((rows, slots), BF16),
            shape((slots, 1), F32),
            shape((sizes[2] * 2 * sizes[1], 2 * sizes[2]), F32),
        ],
        in_specs=[VMEM] * 4,
        out_specs=[VMEM] * 3,
        compiler_params=PARAMS,
    )(ids, gates, *orders(sizes, rows, (2, 0, 1, 3)))


def old_kernel(lines, at_ref, len_ref, query_ref, order_ref, keys_ref, scales_ref, *rest):
    gate_ref, up_ref, down_ref, out_ref = rest[:4]
    outs, held_ref, sems = rest[4:-2], rest[-2], rest[-1]
    cols, units = outs[1].shape[1], gate_ref.shape[1]
    copies = []
    for s in range(lines):
        start = pl.multiple_of(lax.rem(at_ref[0] + s, lines) * cols, 128)
        both, down = outs[2 * s], outs[2 * s + 1]
        copies.append((gate_ref.at[pl.ds(start, cols)], both.at[:, pl.ds(0, units)]))
        copies.append((up_ref.at[pl.ds(start, cols)], both.at[:, pl.ds(units, units)]))
        copies.append((down_ref.at[:, pl.ds(start, cols)], down))
    copies = [pltpu.make_async_copy(a, b, sems.at[i]) for i, (a, b) in enumerate(copies)]
    for copy in copies:
        copy.start()
    query = dot(order_ref[...], query_ref[0]).astype(BF16)
    result = attend(query, keys_ref, scales_ref, len_ref[0], held_ref)
    rows = out_ref.shape[1]
    for z in range(out_ref.shape[0]):
        out_ref[z] = result[z * rows : (z + 1) * rows].astype(BF16)
    for copy in copies:
        copy.wait()


def old_attention(dp, lines, length, query, order, keys, scales, gate, up, down, pieces):
    cols, units = gate.shape[0] // lines, gate.shape[1]
    rows = query.shape[1] // pieces
    return pl.pallas_call(
        functools.partial(old_kernel, lines),
        out_shape=[shape((pieces, rows, DLAT), BF16)]
        + [shape((cols, 2 * units), BF16), shape((units, cols), BF16)] * lines,
        in_specs=[SMEM, SMEM] + [VMEM] * 4 + [HBM] * 3,
        out_specs=[VMEM] * (2 * lines + 1),
        scratch_shapes=[
            pltpu.VMEM((DLAT, keys.shape[1]), BF16),
            pltpu.SemaphoreType.DMA((3 * lines,)),
        ],
        compiler_params=WIDE,
        cost_estimate=pl.CostEstimate(
            flops=2 * query.size * keys.shape[1],
            bytes_accessed=2 * (keys.size + 2 * (gate.size + up.size + down.size)),
            transcendentals=query.shape[1] * keys.shape[1],
        ),
    )(dp, length, query, order, keys, scales, gate, up, down)


def new_kernel(lines, step_ref, len_ref, order_ref, keys_ref, scales_ref, old_ref, *rest):
    parcel_refs, out_ref, held_ref = rest[:lines], rest[lines], rest[lines + 1]
    heads, width = order_ref.shape[0], keys_ref.shape[0]
    query = parcel_refs[0][:heads, :width]
    for s in range(1, lines):
        query = jnp.where(step_ref[0] == s, parcel_refs[s][:heads, :width], query)
    query = dot(order_ref[...], query).astype(BF16)
    result = attend(query, keys_ref, scales_ref, len_ref[0], held_ref)
    rows = out_ref.shape[2]
    for z in range(out_ref.shape[0]):
        out_ref[z, 0] = old_ref[z]
        out_ref[z, 1] = result[z * rows : (z + 1) * rows].astype(BF16)


def new_attention(step, length, order, keys, scales, old, parcels):
    return pl.pallas_call(
        functools.partial(new_kernel, len(parcels)),
        out_shape=shape((old.shape[0], 2) + old.shape[1:], BF16),
        in_specs=[SMEM, SMEM] + [VMEM] * (4 + len(parcels)),
        out_specs=VMEM,
        scratch_shapes=[pltpu.VMEM((DLAT, keys.shape[1]), BF16)],
        compiler_params=PARAMS,
    )(step, length, order, keys, scales, old, *parcels)


def sort_kernel(chips_y, rows_ref, own_ref, other_ref):
    half = own_ref.shape[0]
    pairs = half // chips_y
    core, place_y = lax.axis_index("pd"), lax.rem(lax.axis_index("ep"), chips_y)
    out = lax.broadcasted_iota(jnp.int32, (2 * half, 2 * half), 0)
    want = lax.div(out, half)
    want = jnp.where(want == 0, core, 1 - core)
    turn = lax.rem(place_y - lax.rem(lax.div(out, pairs), chips_y) + chips_y, chips_y)
    want = lax.rem(out, pairs) * (2 * chips_y) + want * chips_y + turn
    come = lax.broadcasted_iota(jnp.int32, (2 * half, 2 * half), 1)
    order = jnp.where(want == come, 1.0, 0.0).astype(BF16)
    result = dot(order, rows_ref[...]).astype(BF16)
    own_ref[...] = result[:half]
    other_ref[...] = result[half:]


def sort_rows(chips_y, rows):
    half = shape((rows.shape[0] // 2, rows.shape[1]), BF16)
    return pl.pallas_call(
        functools.partial(sort_kernel, chips_y),
        out_shape=[half, half],
        in_specs=[VMEM],
        out_specs=[VMEM, VMEM],
        compiler_params=PARAMS,
    )(rows)


def values_kernel(own_ref, other_ref, uv_ref, out_ref):
    count, _, width = uv_ref.shape
    rows = own_ref.shape[0] // count
    for s in range(count):
        for q, ref in enumerate((own_ref, other_ref)):
            result = dot(ref[s * rows : (s + 1) * rows], uv_ref[s]).astype(BF16)
            for i in range(out_ref.shape[0]):
                out_ref[i, q * rows : (q + 1) * rows, s * width : (s + 1) * width] = result


def head_values(lines, own, other, uv_all):
    count, _, width = uv_all.shape
    return pl.pallas_call(
        values_kernel,
        out_shape=shape((lines, 2 * own.shape[0] // count, count * width), BF16),
        in_specs=[VMEM] * 3,
        out_specs=VMEM,
        compiler_params=PARAMS,
    )(own, other, uv_all)


def project_kernel(values_ref, order_ref, *rest):
    out_refs, own_ref, other_ref = rest[:-2], rest[-2], rest[-1]
    rows = values_ref.shape[0] // 2
    values = dot(order_ref[...], values_ref[...]).astype(BF16)
    width = out_refs[0].shape[0]
    for start in range(0, own_ref.shape[1], 256):
        total = sum(
            dot(values[:, s * width : (s + 1) * width], ref[:, start : start + 256])
            for s, ref in enumerate(out_refs)
        )
        own_ref[:, start : start + 256] = total[:rows]
        other_ref[:, start : start + 256] = total[rows:].astype(BF16)


def project(values, order, out_parts):
    rows, cols = values.shape[0] // 2, out_parts[0].shape[1]
    return pl.pallas_call(
        project_kernel,
        out_shape=[shape((rows, cols), F32), shape((rows, cols), BF16)],
        in_specs=[VMEM] * (2 + len(out_parts)),
        out_specs=[VMEM, VMEM],
        compiler_params=PARAMS,
    )(values, order, *out_parts)


def line_kernel(heads, at_ref, gain_ref, *rest):
    parcel_refs, out_ref = rest[:-1], rest[-1]
    lines, cols = len(parcel_refs), gain_ref.shape[1]
    row = lax.broadcasted_iota(jnp.int32, (2 * lines, 128), 0)
    come = lax.broadcasted_iota(jnp.int32, (2 * lines, 128), 1)
    same = lax.rem(row, 2) == lax.rem(come, 2)
    old = lax.rem(row, 2) == 0
    row, come = lax.div(row, 2), lax.div(come, 2)
    order = jnp.where(same & old & (row == come), 1.0, 0.0)
    turned = jnp.zeros_like(order)
    hidden = []
    for s, ref in enumerate(parcel_refs):
        source = lax.rem(at_ref[0] - s + lines, lines)
        lower = ref[heads:].astype(F32)
        lanes = lower.shape[1]
        count = -(-cols // lanes)
        owner = lower[2 * count : 2 * count + 1, :1]
        moved = same & ~old & (come == source) & (row.astype(F32) == owner)
        order = order + jnp.where(moved, 1.0, 0.0)
        turned = turned + jnp.where(same & (come == s) & (row == source), 1.0, 0.0)
        pieces = [
            lower[2 * j : 2 * j + 2, : min(lanes, cols - j * lanes)] for j in range(count)
        ]
        hidden.append(jnp.concatenate(pieces, axis=1))
    hidden = jnp.concatenate(hidden, axis=0)
    rows = 2 * lines
    out_ref[:rows] = jnp.dot(
        turned[:, :rows], hidden, precision=HIGHEST, preferred_element_type=F32
    )
    out_ref[rows : 2 * rows] = jnp.broadcast_to(gain_ref[...].astype(F32), (rows, cols))
    out_ref[2 * rows :, :128] = order
    out_ref[2 * rows :, 128:] = jnp.zeros((rows, cols - 128), F32)


def line_rows(dp, heads, gain, parcels):
    return pl.pallas_call(
        functools.partial(line_kernel, heads),
        out_shape=shape((6 * len(parcels), gain.shape[1]), F32),
        in_specs=[SMEM] + [VMEM] * (1 + len(parcels)),
        out_specs=VMEM,
        compiler_params=PARAMS,
    )(dp, gain, *parcels)


def residual_kernel(sums_ref, line_ref, resid_ref, parcel_ref):
    rows, cols = resid_ref.shape
    total = sums_ref[0].astype(F32)
    for i in range(1, sums_ref.shape[0]):
        total = total + sums_ref[i].astype(F32)
    order = line_ref[2 * rows :, :128][:, :rows]
    resid = jnp.dot(order, total, precision=HIGHEST, preferred_element_type=F32)
    resid = resid + line_ref[:rows]
    resid_ref[...] = resid
    squares = jnp.sum(resid * resid, axis=1, keepdims=True)
    high = squares.astype(BF16)
    low = (squares - high.astype(F32)).astype(BF16)
    lanes = lax.broadcasted_iota(jnp.int32, (rows, 128), 1)
    beside = jnp.where(lanes < 64, high.astype(F32), low.astype(F32)).astype(BF16)
    parcel = (resid * line_ref[rows : 2 * rows]).astype(BF16)
    for i in range(parcel_ref.shape[0]):
        parcel_ref[i, :, :cols] = parcel
        parcel_ref[i, :, cols:] = beside


def residual(sums, line):
    copies, rows, cols = sums.shape
    return pl.pallas_call(
        residual_kernel,
        out_shape=[shape((rows, cols), F32), shape((copies, rows, cols + 128), BF16)],
        in_specs=[VMEM, VMEM],
        out_specs=[VMEM, VMEM],
        compiler_params=PARAMS,
    )(sums, line)


def select_kernel(select_ref, *rest):
    columns, out_ref, held_ref = rest[:-2], rest[-2], rest[-1]
    count, rows = len(columns), columns[0].shape[0]
    for s, ref in enumerate(columns):
        held_ref[lax.rem(lax.rem(lax.axis_index("ep"), count) - s + count, count)] = ref[...]
    for at in range(0, out_ref.shape[1], 384):
        lanes = slice(at, min(at + 384, out_ref.shape[1]))
        gathered = held_ref[:, :, lanes].reshape(count * rows, lanes.stop - at)
        out_ref[:, lanes] = dot(select_ref[...], gathered).astype(BF16)


def select_rows(select, columns):
    return pl.pallas_call(
        select_kernel,
        out_shape=shape((select.shape[0], columns[0].shape[1]), BF16),
        in_specs=[VMEM] * (1 + len(columns)),
        out_specs=VMEM,
        scratch_shapes=[pltpu.VMEM((len(columns),) + columns[0].shape, BF16)],
        compiler_params=PARAMS,
    )(select, *columns)


def acts_kernel(width, units, sums_ref, out_ref):
    total = sums_ref[0].astype(F32)
    for i in range(1, sums_ref.shape[0]):
        total = total + sums_ref[i].astype(F32)
    end = sums_ref.shape[2] - 128
    squares = total[:, end : end + 1] + total[:, end + 64 : end + 65]
    scale = lax.rsqrt(squares / width + EPSILON)
    for j in range(end // (2 * units)):
        at = 2 * units * j
        gate = total[:, at : at + units] * scale
        up = total[:, at + units : at + 2 * units] * scale
        acts = (gate / (1.0 + jnp.exp(-gate)) * up).astype(BF16)
        for i in range(out_ref.shape[0]):
            out_ref[i, :, j * units : (j + 1) * units] = acts


def activations(width, units, sums):
    lines, rows, lanes = sums.shape
    return pl.pallas_call(
        functools.partial(acts_kernel, width, units),
        out_shape=shape((lines, rows, (lanes - 128) // 2), BF16),
        in_specs=[VMEM],
        out_specs=VMEM,
        compiler_params=PARAMS,
    )(sums)


def gate_up_kernel(lines, at_ref, own_ref, other_ref, *rest):
    parts, out_ref, held, sems = rest[:-3], rest[-3], rest[-2], rest[-1]
    cols, lanes = held.shape[1:]
    copies = [pltpu.make_async_copy(parts[s], held.at[s], sems.at[s]) for s in range(lines)]
    for copy in copies:
        copy.start()
    for s in range(lines):
        copies[s].wait()
        lane = pl.multiple_of(lax.rem(at_ref[0] - s + lines, lines) * lanes, 128)
        for q, ref in enumerate((own_ref, other_ref)):
            capacity = ref.shape[0] // lines
            result = dot(ref[:, :cols], held[s]).astype(BF16)
            for d in range(lines):
                out_ref[d, q * capacity : (q + 1) * capacity, pl.ds(lane, lanes)] = result[
                    d * capacity : (d + 1) * capacity
                ]
    for q, ref in enumerate((own_ref, other_ref)):
        capacity = ref.shape[0] // lines
        for d in range(lines):
            out_ref[d, q * capacity : (q + 1) * capacity, lines * lanes :] = ref[
                d * capacity : (d + 1) * capacity, cols:
            ]


def gate_up(dp, own, other, parts):
    lines, (cols, lanes) = len(parts), parts[0].shape
    return pl.pallas_call(
        functools.partial(gate_up_kernel, lines),
        out_shape=shape((lines, 2 * own.shape[0] // lines, lines * lanes + 128), BF16),
        in_specs=[SMEM, VMEM, VMEM] + [ANY] * lines,
        out_specs=VMEM,
        scratch_shapes=[
            pltpu.VMEM((lines, cols, lanes), BF16),
            pltpu.SemaphoreType.DMA((lines,)),
        ],
        compiler_params=PARAMS,
    )(dp, own, other, *parts)


def down_kernel(lines, at_ref, acts_ref, *rest):
    parts, own_ref, other_ref, held, sems = rest[:-4], rest[-4], rest[-3], rest[-2], rest[-1]
    units, cols = parts[0].shape
    copies = []
    for s in range(lines):
        row = pl.multiple_of(lax.rem(at_ref[0] - s + lines, lines) * units, 128)
        copies.append(pltpu.make_async_copy(parts[s], held.at[pl.ds(row, units)], sems.at[s]))
    for copy in copies:
        copy.start()
    for copy in copies:
        copy.wait()
    capacity = acts_ref.shape[1] // 2
    own = jnp.concatenate([acts_ref[d, :capacity] for d in range(lines)], axis=0)
    other = jnp.concatenate([acts_ref[d, capacity:] for d in range(lines)], axis=0)
    for at in range(0, cols, 256):
        own_ref[:, at : at + 256] = dot(own, held[:, at : at + 256]).astype(BF16)
        other_ref[:, at : at + 256] = dot(other, held[:, at : at + 256]).astype(BF16)


def down(dp, acts, parts):
    lines, (units, cols) = len(parts), parts[0].shape
    slots = acts.shape[0] * acts.shape[1] // 2
    return pl.pallas_call(
        functools.partial(down_kernel, lines),
        out_shape=[shape((slots, cols), BF16), shape((slots, cols), BF16)],
        in_specs=[SMEM, VMEM] + [ANY] * lines,
        out_specs=[VMEM, VMEM],
        scratch_shapes=[
            pltpu.VMEM((lines * units, cols), BF16),
            pltpu.SemaphoreType.DMA((lines,)),
        ],
        compiler_params=PARAMS,
    )(dp, acts, *parts)


def expand_kernel(own_ref, other_ref, gate_ref, select_ref, out_ref):
    for at in range(0, own_ref.shape[1], 256):
        total = own_ref[:, at : at + 256].astype(F32) + other_ref[:, at : at + 256].astype(F32)
        weighted = (total * gate_ref[...]).astype(BF16)
        out_ref[:, at : at + 256] = dot(select_ref[...], weighted).astype(BF16)


def expand(own, other, gates, select):
    return pl.pallas_call(
        expand_kernel,
        out_shape=shape((select.shape[0], own.shape[1]), BF16),
        in_specs=[VMEM] * 4,
        out_specs=VMEM,
        compiler_params=PARAMS,
    )(own, other, gates, select)


def join_kernel(line_ref, resid_ref, *rest):
    parts, out_ref = rest[:-1], rest[-1]
    total = jnp.dot(
        line_ref[...], resid_ref[...], precision=HIGHEST, preferred_element_type=F32
    )
    for part in parts:
        total = total + part[...].astype(F32)
    out_ref[...] = total.astype(BF16)


def join(line, resid, parts):
    return pl.pallas_call(
        join_kernel,
        out_shape=shape(parts[0].shape, BF16),
        in_specs=[VMEM] * (2 + len(parts)),
        out_specs=VMEM,
        compiler_params=PARAMS,
    )(line, resid, *parts)


def shards(
    queries,
    cache_vals,
    cache_scales,
    cache_len,
    fresh_vals,
    fresh_scales,
    fresh_len,
    fresh_owner,
    hidden,
    w_uv,
    w_out,
    norm_gain,
    route_ids,
    route_weights,
    w_gate,
    w_up,
    w_down,
):
    pd, dp, ep = lax.axis_index("pd"), lax.axis_index("dp"), lax.axis_index("ep")
    n_pd, n_dp, n_ep = lax.axis_size("pd"), lax.axis_size("dp"), lax.axis_size("ep")
    heads, key_width = queries.shape[1:]
    width = hidden.shape[1]
    cols = width // n_dp
    units = w_gate.shape[2]

    chips_y = CHIPS_Y
    chips_z = n_ep // chips_y
    z_groups = [[z * chips_y + y for z in range(chips_z)] for y in range(chips_y)]
    place_y = ep % chips_y

    def shift_y(value, amount):
        pairs = [
            (z * chips_y + y, z * chips_y + (y + amount) % chips_y)
            for z in range(chips_z)
            for y in range(chips_y)
        ]
        return lax.ppermute(value, "ep", pairs)

    at_dp = dp.astype(jnp.int32).reshape(1)
    parcels = make_parcels(at_dp, n_dp, fresh_owner, queries, hidden)
    parcels = list(parcels[:1]) + [shift(parcels[s], "dp", s) for s in range(1, n_dp)]

    whole, first = lax.optimization_barrier((queries, parcels[1]))

    order = np.arange(heads).reshape(n_pd, chips_z, chips_y).transpose(1, 0, 2).reshape(heads)
    order = jnp.asarray(np.eye(heads)[order], BF16)
    packed = old_attention(
        at_dp,
        n_dp,
        cache_len,
        whole,
        order,
        cache_vals[0].T,
        cache_scales[0],
        w_gate[0],
        w_up[0],
        w_down[0],
        chips_z,
    )
    old_out, packed = packed[0], packed[1:]
    uv_own = w_uv[0]
    out_own = lax.dynamic_slice_in_dim(w_out, dp * cols, cols, 1)
    uv_parts = [uv_own] + [shift_y(uv_own, s) for s in range(1, chips_y)]
    out_parts = [out_own] + [shift_y(out_own, s) for s in range(1, chips_y)]
    old_out, rest, uv_parts = lax.optimization_barrier((old_out, parcels[2:], uv_parts))
    parcels = [parcels[0], first] + list(rest)
    step = (dp - fresh_owner) % n_dp
    latent = new_attention(
        step, fresh_len, order, fresh_vals[0].T, fresh_scales[0], old_out, parcels
    )
    slab = 2 * n_ep
    sizes = (chips_y, chips_z, n_dp, 2 * slab * route_ids.shape[1] // n_ep)
    latent, parcels, norm_gain = lax.optimization_barrier((latent, parcels, norm_gain))
    gain = lax.dynamic_slice_in_dim(norm_gain, dp * cols, cols, 0)[None]
    ids = lax.dynamic_slice_in_dim(route_ids.T, pd * n_dp * slab, n_dp * slab, 1)
    gates = lax.dynamic_slice_in_dim(route_weights.T, pd * n_dp * slab, n_dp * slab, 1)
    line = line_rows(at_dp, heads, gain, parcels)
    line, packed = lax.optimization_barrier((line, packed))
    both_parts = [packed[0]] + [shift(packed[2 * s], "dp", s) for s in range(1, n_dp)]
    down_parts = [packed[1]] + [shift(packed[2 * s + 1], "dp", s) for s in range(1, n_dp)]
    head_rows = exchange(latent, "ep", z_groups)
    head_rows, near, uv_all, line = lax.optimization_barrier(
        (head_rows, out_parts[1::2], jnp.stack(uv_parts), line)
    )
    own, other = sort_rows(chips_y, head_rows.reshape(2 * chips_z * heads // chips_z, DLAT))
    values = head_values(n_dp, own, shift(other, "pd", 1), uv_all)
    values, far = lax.optimization_barrier((values, out_parts[2]))
    out_parts = [out_own, near[0], far, near[1]]
    values = exchange(values, "dp")
    rows = n_dp * 2 * chips_z * 2
    order = np.arange(rows).reshape(n_dp, 2, chips_z, 2).transpose(1, 2, 0, 3).reshape(rows)
    order = jnp.asarray(np.eye(rows)[order], BF16)
    own, other = project(values.reshape(rows, chips_y * 128), order, out_parts)
    partial = (own + shift(other, "pd", 1).astype(F32)).astype(BF16)
    partial, near = lax.optimization_barrier((partial, both_parts[1::2]))
    summands = exchange(partial.reshape(chips_z, n_dp * 2, cols), "ep", z_groups)
    resid_cols, parcel = residual(summands, line)
    parcel, ids = lax.optimization_barrier((parcel, ids))
    select = mask_there(sizes, ids)
    column = exchange(parcel, "ep", z_groups)
    column, far, select = lax.optimization_barrier((column, both_parts[2], select))
    both_parts = [both_parts[0], near[0], far, near[1]]
    column = column.reshape(chips_z * n_dp * 2, cols + 128)
    columns = [column] + [shift_y(column, s) for s in range(1, chips_y)]
    columns, down_parts = lax.optimization_barrier((columns, down_parts))
    slot_rows = select_rows(select, columns)
    other_rows = shift(slot_rows, "pd", 1)

    halves = gate_up(at_dp, slot_rows, other_rows, both_parts)
    acts = activations(width, units, exchange(halves, "dp"))
    acts, ids, gates = lax.optimization_barrier((acts, ids, gates))
    masks = mask_back(sizes, ids, gates)
    all_acts, masks = lax.optimization_barrier((exchange(acts, "dp"), masks))
    select_back, slot_gate, own_line = masks
    own, other = down(at_dp, all_acts, down_parts)
    table = expand(own, shift(other, "pd", 1), slot_gate, select_back)
    table = table.reshape(chips_y, n_dp * chips_z * 2, cols)
    parts = [lax.dynamic_index_in_dim(table, place_y, 0, keepdims=False)]
    for s in range(1, chips_y):
        part = lax.dynamic_index_in_dim(table, (place_y + s) % chips_y, 0, keepdims=False)
        parts.append(shift_y(part, s))
    table = join(own_line, resid_cols, parts).reshape(n_dp * chips_z, 2, cols)
    planes = [
        [d * n_ep + z * chips_y + y for d in range(n_dp) for z in range(chips_z)]
        for y in range(chips_y)
    ]
    table = exchange(table, ("dp", "ep"), planes).reshape(n_dp, chips_z, 2, cols)
    out = jnp.sum(table.astype(F32), axis=1).astype(BF16)
    return out.transpose(1, 0, 2).reshape(2, width)


def solution(mesh):
    in_specs = (
        P(("pd", "dp", "ep"), None, None),
        P(("pd", "dp", "ep"), None, None),
        P(("pd", "dp", "ep"), None, None),
        P(("pd", "dp", "ep")),
        P(("pd", "dp", "ep"), None, None),
        P(("pd", "dp", "ep"), None, None),
        P(("pd", "dp", "ep")),
        P(("pd", "dp", "ep")),
        P(("pd", "dp", "ep"), None),
        P(("pd", "ep"), None, None),
        P(("pd", "ep"), None),
        P(),
        P(),
        P(),
        P("ep", None, ("pd", "dp")),
        P("ep", None, ("pd", "dp")),
        P("ep", ("pd", "dp"), None),
    )
    out_specs = P(("pd", "dp", "ep"), None)
    return jax.shard_map(shards, mesh=mesh, in_specs=in_specs, out_specs=out_specs, check_vma=False)
```

```python
import functools

import jax
import jax.numpy as jnp
import numpy as np
from jax import lax
from jax.experimental import pallas as pl
from jax.experimental.pallas import tpu as pltpu
from jax.sharding import PartitionSpec as P

DLAT = 512
CHIPS_Y = 4


SOFT_SCALE = 0.07216878364870323
EPSILON = 1e-06
BF16 = jnp.bfloat16
F32 = jnp.float32


def shift(value, axis, amount):
    size = lax.axis_size(axis)
    return lax.ppermute(value, axis, [(i, (i + amount) % size) for i in range(size)])


def exchange(value, axis, groups=None):
    return lax.all_to_all(value, axis, 0, 0, axis_index_groups=groups)


def dot(left, right):
    return jnp.dot(left, right, preferred_element_type=F32)


HIGHEST = lax.Precision.HIGHEST
VMEM = pl.BlockSpec(memory_space=pltpu.VMEM)
SMEM = pl.BlockSpec(memory_space=pltpu.SMEM)
HBM = pl.BlockSpec(memory_space=pltpu.HBM)
ANY = pl.BlockSpec(memory_space=pl.ANY)
PARAMS = pltpu.CompilerParams(vmem_limit_bytes=16 * 1024 * 1024)
WIDE = pltpu.CompilerParams(vmem_limit_bytes=58 * 1024 * 1024)


def shape(dims, dtype):
    return jax.ShapeDtypeStruct(dims, dtype)


def attend(query, keys_ref, scales_ref, length, held_ref):
    for block in range(scales_ref.shape[0]):
        at = slice(block * 128, block * 128 + 128)
        scale = scales_ref[...].astype(F32)[block : block + 1]
        held_ref[at] = (keys_ref[at].astype(F32) * scale).astype(BF16)
    scores = dot(query[:, :DLAT], held_ref[...]) + dot(query[:, DLAT:], keys_ref[DLAT:])
    scores = scores * SOFT_SCALE
    token = lax.broadcasted_iota(jnp.int32, scores.shape, 1)
    scores = jnp.where(token < length, scores, -1e30)
    weights = jnp.exp(scores - jnp.max(scores, axis=1, keepdims=True))
    probs = (weights / jnp.sum(weights, axis=1, keepdims=True)).astype(BF16)
    return lax.dot_general(
        probs, held_ref[...], (((1,), (1,)), ((), ())), preferred_element_type=F32
    )


def parcel_kernel(lines, at_ref, owner_ref, query_ref, hidden_ref, *outs):
    heads, wide = query_ref.shape[1:]
    cols = hidden_ref.shape[1] // lines
    lanes = outs[0].shape[1]
    for s in range(lines):
        start = pl.multiple_of(lax.rem(at_ref[0] + s, lines) * cols, 128)
        hidden = hidden_ref[:, pl.ds(start, cols)].astype(F32)
        parts = [hidden[:, at : at + lanes] for at in range(0, cols, lanes)]
        parts = [jnp.pad(part, ((0, 0), (0, lanes - part.shape[1]))) for part in parts]
        used = 2 * len(parts)
        parts.append(jnp.full((16 - used, lanes), owner_ref[0].astype(F32)))
        outs[s][:heads, :wide] = query_ref[1]
        outs[s][:heads, wide:] = jnp.zeros((heads, lanes - wide), BF16)
        outs[s][heads:] = jnp.concatenate(parts, axis=0).astype(BF16)


def make_parcels(dp, lines, owner, query, hidden):
    out = shape((query.shape[1] + 16, -(-query.shape[2] // 128) * 128), BF16)
    return pl.pallas_call(
        functools.partial(parcel_kernel, lines),
        out_shape=[out] * lines,
        in_specs=[SMEM, SMEM, VMEM, VMEM],
        out_specs=[VMEM] * lines,
        compiler_params=PARAMS,
    )(dp, owner, query, hidden)


def slots_of(lines, capacity, ids_ref, before_ref):
    rows = ids_ref.shape[1]
    hits = ids_ref[...] == lax.axis_index("ep")
    routed = jnp.sum(jnp.where(hits, 1.0, 0.0), axis=0, keepdims=True)
    place = dot(jnp.broadcast_to(routed, (8, rows)).astype(BF16), before_ref[...])[:1]
    lane = lax.broadcasted_iota(jnp.int32, (1, rows), 1)
    first = lax.div(lane, rows // lines) * capacity
    return hits, jnp.where(routed > 0.0, place + first.astype(F32), -1.0)


def there_kernel(lines, capacity, ids_ref, before_ref, there_ref, select_ref):
    slots, rows = select_ref.shape
    slot = slots_of(lines, capacity, ids_ref, before_ref)[1]
    wide = jnp.broadcast_to(slot, (8, rows)).astype(BF16)
    slot_iota = lax.broadcasted_iota(jnp.int32, (slots, rows), 0).astype(F32)
    select_ref[...] = jnp.where(dot(wide, there_ref[...])[:1] == slot_iota, 1.0, 0.0).astype(BF16)


def back_kernel(sizes, ids_ref, gates_ref, before_ref, back_ref, *outs):
    chips_y, chips_z, lines, capacity = sizes
    table_ref, gate_ref, line_ref = outs
    rows, slots = table_ref.shape
    hits, slot = slots_of(lines, capacity, ids_ref, before_ref)
    gates = jnp.sum(jnp.where(hits, gates_ref[...], 0.0), axis=0, keepdims=True)
    wide = jnp.broadcast_to(slot, (8, rows)).astype(BF16)
    slot_iota = lax.broadcasted_iota(jnp.int32, (slots, rows), 0).astype(F32)
    back = jnp.where(dot(wide, back_ref[...])[:1] == slot_iota, 1.0, 0.0)
    table_ref[...] = back.T.astype(BF16)
    gate_ref[...] = jnp.sum(jnp.where(slot == slot_iota, gates, 0.0), axis=1, keepdims=True)
    pairs = 2 * chips_z
    out = lax.broadcasted_iota(jnp.int32, line_ref.shape, 0)
    come = lax.broadcasted_iota(jnp.int32, line_ref.shape, 1)
    own = lax.rem(lax.div(out, 2), chips_z) == lax.div(lax.axis_index("ep"), chips_y)
    own = own & (lax.div(out, pairs) * 2 + lax.rem(out, 2) == come)
    line_ref[...] = jnp.where(own, 1.0, 0.0)


def orders(sizes, rows, axes):
    chips_y, chips_z, lines, _ = sizes
    slab = rows // lines
    canon = np.arange(rows).reshape(lines, chips_z, chips_y, 2)
    before = np.kron(np.eye(lines), np.triu(np.ones((slab, slab)), 1))
    order = np.eye(rows)[canon.transpose(axes).reshape(rows)].T
    return jnp.asarray(before, BF16), jnp.asarray(order, BF16)


def mask_there(sizes, ids):
    rows, slots = ids.shape[1], sizes[2] * sizes[3]
    return pl.pallas_call(
        functools.partial(there_kernel, sizes[2], sizes[3]),
        out_shape=shape((slots, rows), BF16),
        in_specs=[VMEM] * 3,
        out_specs=VMEM,
        compiler_params=PARAMS,
    )(ids, *orders(sizes, rows, (2, 1, 0, 3)))


def mask_back(sizes, ids, gates):
    rows, slots = ids.shape[1], sizes[2] * sizes[3]
    return pl.pallas_call(
        functools.partial(back_kernel, sizes),
        out_shape=[
            shape((rows, slots), BF16),
            shape((slots, 1), F32),
            shape((sizes[2] * 2 * sizes[1], 2 * sizes[2]), F32),
        ],
        in_specs=[VMEM] * 4,
        out_specs=[VMEM] * 3,
        compiler_params=PARAMS,
    )(ids, gates, *orders(sizes, rows, (2, 0, 1, 3)))


def old_kernel(lines, at_ref, len_ref, query_ref, order_ref, keys_ref, scales_ref, *rest):
    gate_ref, up_ref, down_ref, out_ref = rest[:4]
    outs, held_ref, sems = rest[4:-2], rest[-2], rest[-1]
    cols, units = outs[1].shape[1], gate_ref.shape[1]
    copies = []
    for s in range(lines):
        start = pl.multiple_of(lax.rem(at_ref[0] + s, lines) * cols, 128)
        both, down = outs[2 * s], outs[2 * s + 1]
        copies.append((gate_ref.at[pl.ds(start, cols)], both.at[:, pl.ds(0, units)]))
        copies.append((up_ref.at[pl.ds(start, cols)], both.at[:, pl.ds(units, units)]))
        copies.append((down_ref.at[:, pl.ds(start, cols)], down))
    copies = [pltpu.make_async_copy(a, b, sems.at[i]) for i, (a, b) in enumerate(copies)]
    for copy in copies:
        copy.start()
    query = dot(order_ref[...], query_ref[0]).astype(BF16)
    result = attend(query, keys_ref, scales_ref, len_ref[0], held_ref)
    rows = out_ref.shape[1]
    for z in range(out_ref.shape[0]):
        out_ref[z] = result[z * rows : (z + 1) * rows].astype(BF16)
    for copy in copies:
        copy.wait()


def old_attention(dp, lines, length, query, order, keys, scales, gate, up, down, pieces):
    cols, units = gate.shape[0] // lines, gate.shape[1]
    rows = query.shape[1] // pieces
    return pl.pallas_call(
        functools.partial(old_kernel, lines),
        out_shape=[shape((pieces, rows, DLAT), BF16)]
        + [shape((cols, 2 * units), BF16), shape((units, cols), BF16)] * lines,
        in_specs=[SMEM, SMEM] + [VMEM] * 4 + [HBM] * 3,
        out_specs=[VMEM] * (2 * lines + 1),
        scratch_shapes=[
            pltpu.VMEM((DLAT, keys.shape[1]), BF16),
            pltpu.SemaphoreType.DMA((3 * lines,)),
        ],
        compiler_params=WIDE,
        cost_estimate=pl.CostEstimate(
            flops=2 * query.size * keys.shape[1],
            bytes_accessed=2 * (keys.size + 2 * (gate.size + up.size + down.size)),
            transcendentals=query.shape[1] * keys.shape[1],
        ),
    )(dp, length, query, order, keys, scales, gate, up, down)


def new_kernel(lines, step_ref, len_ref, order_ref, keys_ref, scales_ref, old_ref, *rest):
    parcel_refs, out_ref, held_ref = rest[:lines], rest[lines], rest[lines + 1]
    heads, width = order_ref.shape[0], keys_ref.shape[0]
    query = parcel_refs[0][:heads, :width]
    for s in range(1, lines):
        query = jnp.where(step_ref[0] == s, parcel_refs[s][:heads, :width], query)
    query = dot(order_ref[...], query).astype(BF16)
    result = attend(query, keys_ref, scales_ref, len_ref[0], held_ref)
    rows = out_ref.shape[2]
    for z in range(out_ref.shape[0]):
        out_ref[z, 0] = old_ref[z]
        out_ref[z, 1] = result[z * rows : (z + 1) * rows].astype(BF16)


def new_attention(step, length, order, keys, scales, old, parcels):
    return pl.pallas_call(
        functools.partial(new_kernel, len(parcels)),
        out_shape=shape((old.shape[0], 2) + old.shape[1:], BF16),
        in_specs=[SMEM, SMEM] + [VMEM] * (4 + len(parcels)),
        out_specs=VMEM,
        scratch_shapes=[pltpu.VMEM((DLAT, keys.shape[1]), BF16)],
        compiler_params=PARAMS,
    )(step, length, order, keys, scales, old, *parcels)


def sort_kernel(chips_y, rows_ref, own_ref, other_ref):
    half = own_ref.shape[0]
    pairs = half // chips_y
    core, place_y = lax.axis_index("pd"), lax.rem(lax.axis_index("ep"), chips_y)
    out = lax.broadcasted_iota(jnp.int32, (2 * half, 2 * half), 0)
    want = lax.div(out, half)
    want = jnp.where(want == 0, core, 1 - core)
    turn = lax.rem(place_y - lax.rem(lax.div(out, pairs), chips_y) + chips_y, chips_y)
    want = lax.rem(out, pairs) * (2 * chips_y) + want * chips_y + turn
    come = lax.broadcasted_iota(jnp.int32, (2 * half, 2 * half), 1)
    order = jnp.where(want == come, 1.0, 0.0).astype(BF16)
    result = dot(order, rows_ref[...]).astype(BF16)
    own_ref[...] = result[:half]
    other_ref[...] = result[half:]


def sort_rows(chips_y, rows):
    half = shape((rows.shape[0] // 2, rows.shape[1]), BF16)
    return pl.pallas_call(
        functools.partial(sort_kernel, chips_y),
        out_shape=[half, half],
        in_specs=[VMEM],
        out_specs=[VMEM, VMEM],
        compiler_params=PARAMS,
    )(rows)


def values_kernel(own_ref, other_ref, uv_ref, out_ref):
    count, _, width = uv_ref.shape
    rows = own_ref.shape[0] // count
    for s in range(count):
        for q, ref in enumerate((own_ref, other_ref)):
            result = dot(ref[s * rows : (s + 1) * rows], uv_ref[s]).astype(BF16)
            for i in range(out_ref.shape[0]):
                out_ref[i, q * rows : (q + 1) * rows, s * width : (s + 1) * width] = result


def head_values(lines, own, other, uv_all):
    count, _, width = uv_all.shape
    return pl.pallas_call(
        values_kernel,
        out_shape=shape((lines, 2 * own.shape[0] // count, count * width), BF16),
        in_specs=[VMEM] * 3,
        out_specs=VMEM,
        compiler_params=PARAMS,
    )(own, other, uv_all)


def project_kernel(values_ref, order_ref, *rest):
    out_refs, own_ref, other_ref = rest[:-2], rest[-2], rest[-1]
    rows = values_ref.shape[0] // 2
    values = dot(order_ref[...], values_ref[...]).astype(BF16)
    width = out_refs[0].shape[0]
    for start in range(0, own_ref.shape[1], 256):
        total = sum(
            dot(values[:, s * width : (s + 1) * width], ref[:, start : start + 256])
            for s, ref in enumerate(out_refs)
        )
        own_ref[:, start : start + 256] = total[:rows]
        other_ref[:, start : start + 256] = total[rows:].astype(BF16)


def project(values, order, out_parts):
    rows, cols = values.shape[0] // 2, out_parts[0].shape[1]
    return pl.pallas_call(
        project_kernel,
        out_shape=[shape((rows, cols), F32), shape((rows, cols), BF16)],
        in_specs=[VMEM] * (2 + len(out_parts)),
        out_specs=[VMEM, VMEM],
        compiler_params=PARAMS,
    )(values, order, *out_parts)


def line_kernel(heads, at_ref, gain_ref, *rest):
    parcel_refs, out_ref = rest[:-1], rest[-1]
    lines, cols = len(parcel_refs), gain_ref.shape[1]
    row = lax.broadcasted_iota(jnp.int32, (2 * lines, 128), 0)
    come = lax.broadcasted_iota(jnp.int32, (2 * lines, 128), 1)
    same = lax.rem(row, 2) == lax.rem(come, 2)
    old = lax.rem(row, 2) == 0
    row, come = lax.div(row, 2), lax.div(come, 2)
    order = jnp.where(same & old & (row == come), 1.0, 0.0)
    turned = jnp.zeros_like(order)
    hidden = []
    for s, ref in enumerate(parcel_refs):
        source = lax.rem(at_ref[0] - s + lines, lines)
        lower = ref[heads:].astype(F32)
        lanes = lower.shape[1]
        count = -(-cols // lanes)
        owner = lower[2 * count : 2 * count + 1, :1]
        moved = same & ~old & (come == source) & (row.astype(F32) == owner)
        order = order + jnp.where(moved, 1.0, 0.0)
        turned = turned + jnp.where(same & (come == s) & (row == source), 1.0, 0.0)
        pieces = [
            lower[2 * j : 2 * j + 2, : min(lanes, cols - j * lanes)] for j in range(count)
        ]
        hidden.append(jnp.concatenate(pieces, axis=1))
    hidden = jnp.concatenate(hidden, axis=0)
    rows = 2 * lines
    out_ref[:rows] = jnp.dot(
        turned[:, :rows], hidden, precision=HIGHEST, preferred_element_type=F32
    )
    out_ref[rows : 2 * rows] = jnp.broadcast_to(gain_ref[...].astype(F32), (rows, cols))
    out_ref[2 * rows :, :128] = order
    out_ref[2 * rows :, 128:] = jnp.zeros((rows, cols - 128), F32)


def line_rows(dp, heads, gain, parcels):
    return pl.pallas_call(
        functools.partial(line_kernel, heads),
        out_shape=shape((6 * len(parcels), gain.shape[1]), F32),
        in_specs=[SMEM] + [VMEM] * (1 + len(parcels)),
        out_specs=VMEM,
        compiler_params=PARAMS,
    )(dp, gain, *parcels)


def residual_kernel(sums_ref, line_ref, resid_ref, parcel_ref):
    rows, cols = resid_ref.shape
    total = sums_ref[0].astype(F32)
    for i in range(1, sums_ref.shape[0]):
        total = total + sums_ref[i].astype(F32)
    order = line_ref[2 * rows :, :128][:, :rows]
    resid = jnp.dot(order, total, precision=HIGHEST, preferred_element_type=F32)
    resid = resid + line_ref[:rows]
    resid_ref[...] = resid
    squares = jnp.sum(resid * resid, axis=1, keepdims=True)
    high = squares.astype(BF16)
    low = (squares - high.astype(F32)).astype(BF16)
    lanes = lax.broadcasted_iota(jnp.int32, (rows, 128), 1)
    beside = jnp.where(lanes < 64, high.astype(F32), low.astype(F32)).astype(BF16)
    parcel = (resid * line_ref[rows : 2 * rows]).astype(BF16)
    for i in range(parcel_ref.shape[0]):
        parcel_ref[i, :, :cols] = parcel
        parcel_ref[i, :, cols:] = beside


def residual(sums, line):
    copies, rows, cols = sums.shape
    return pl.pallas_call(
        residual_kernel,
        out_shape=[shape((rows, cols), F32), shape((copies, rows, cols + 128), BF16)],
        in_specs=[VMEM, VMEM],
        out_specs=[VMEM, VMEM],
        compiler_params=PARAMS,
    )(sums, line)


def select_kernel(select_ref, *rest):
    columns, out_ref, held_ref = rest[:-2], rest[-2], rest[-1]
    count, rows = len(columns), columns[0].shape[0]
    for s, ref in enumerate(columns):
        held_ref[lax.rem(lax.rem(lax.axis_index("ep"), count) - s + count, count)] = ref[...]
    for at in range(0, out_ref.shape[1], 384):
        lanes = slice(at, min(at + 384, out_ref.shape[1]))
        gathered = held_ref[:, :, lanes].reshape(count * rows, lanes.stop - at)
        out_ref[:, lanes] = dot(select_ref[...], gathered).astype(BF16)


def select_rows(select, columns):
    return pl.pallas_call(
        select_kernel,
        out_shape=shape((select.shape[0], columns[0].shape[1]), BF16),
        in_specs=[VMEM] * (1 + len(columns)),
        out_specs=VMEM,
        scratch_shapes=[pltpu.VMEM((len(columns),) + columns[0].shape, BF16)],
        compiler_params=PARAMS,
    )(select, *columns)


def acts_kernel(width, units, sums_ref, out_ref):
    total = sums_ref[0].astype(F32)
    for i in range(1, sums_ref.shape[0]):
        total = total + sums_ref[i].astype(F32)
    end = sums_ref.shape[2] - 128
    squares = total[:, end : end + 1] + total[:, end + 64 : end + 65]
    scale = lax.rsqrt(squares / width + EPSILON)
    for j in range(end // (2 * units)):
        at = 2 * units * j
        gate = total[:, at : at + units] * scale
        up = total[:, at + units : at + 2 * units] * scale
        acts = (gate / (1.0 + jnp.exp(-gate)) * up).astype(BF16)
        for i in range(out_ref.shape[0]):
            out_ref[i, :, j * units : (j + 1) * units] = acts


def activations(width, units, sums):
    lines, rows, lanes = sums.shape
    return pl.pallas_call(
        functools.partial(acts_kernel, width, units),
        out_shape=shape((lines, rows, (lanes - 128) // 2), BF16),
        in_specs=[VMEM],
        out_specs=VMEM,
        compiler_params=PARAMS,
    )(sums)


def gate_up_kernel(lines, at_ref, own_ref, other_ref, *rest):
    parts, out_ref, held, sems = rest[:-3], rest[-3], rest[-2], rest[-1]
    cols, lanes = held.shape[1:]
    copies = [pltpu.make_async_copy(parts[s], held.at[s], sems.at[s]) for s in range(lines)]
    for copy in copies:
        copy.start()
    for s in range(lines):
        copies[s].wait()
        lane = pl.multiple_of(lax.rem(at_ref[0] - s + lines, lines) * lanes, 128)
        for q, ref in enumerate((own_ref, other_ref)):
            capacity = ref.shape[0] // lines
            result = dot(ref[:, :cols], held[s]).astype(BF16)
            for d in range(lines):
                out_ref[d, q * capacity : (q + 1) * capacity, pl.ds(lane, lanes)] = result[
                    d * capacity : (d + 1) * capacity
                ]
    for q, ref in enumerate((own_ref, other_ref)):
        capacity = ref.shape[0] // lines
        for d in range(lines):
            out_ref[d, q * capacity : (q + 1) * capacity, lines * lanes :] = ref[
                d * capacity : (d + 1) * capacity, cols:
            ]


def gate_up(dp, own, other, parts):
    lines, (cols, lanes) = len(parts), parts[0].shape
    return pl.pallas_call(
        functools.partial(gate_up_kernel, lines),
        out_shape=shape((lines, 2 * own.shape[0] // lines, lines * lanes + 128), BF16),
        in_specs=[SMEM, VMEM, VMEM] + [ANY] * lines,
        out_specs=VMEM,
        scratch_shapes=[
            pltpu.VMEM((lines, cols, lanes), BF16),
            pltpu.SemaphoreType.DMA((lines,)),
        ],
        compiler_params=PARAMS,
    )(dp, own, other, *parts)


def down_kernel(lines, at_ref, acts_ref, *rest):
    parts, own_ref, other_ref, held, sems = rest[:-4], rest[-4], rest[-3], rest[-2], rest[-1]
    units, cols = parts[0].shape
    copies = []
    for s in range(lines):
        row = pl.multiple_of(lax.rem(at_ref[0] - s + lines, lines) * units, 128)
        copies.append(pltpu.make_async_copy(parts[s], held.at[pl.ds(row, units)], sems.at[s]))
    for copy in copies:
        copy.start()
    for copy in copies:
        copy.wait()
    capacity = acts_ref.shape[1] // 2
    own = jnp.concatenate([acts_ref[d, :capacity] for d in range(lines)], axis=0)
    other = jnp.concatenate([acts_ref[d, capacity:] for d in range(lines)], axis=0)
    for at in range(0, cols, 256):
        own_ref[:, at : at + 256] = dot(own, held[:, at : at + 256]).astype(BF16)
        other_ref[:, at : at + 256] = dot(other, held[:, at : at + 256]).astype(BF16)


def down(dp, acts, parts):
    lines, (units, cols) = len(parts), parts[0].shape
    slots = acts.shape[0] * acts.shape[1] // 2
    return pl.pallas_call(
        functools.partial(down_kernel, lines),
        out_shape=[shape((slots, cols), BF16), shape((slots, cols), BF16)],
        in_specs=[SMEM, VMEM] + [ANY] * lines,
        out_specs=[VMEM, VMEM],
        scratch_shapes=[
            pltpu.VMEM((lines * units, cols), BF16),
            pltpu.SemaphoreType.DMA((lines,)),
        ],
        compiler_params=PARAMS,
    )(dp, acts, *parts)


def expand_kernel(own_ref, other_ref, gate_ref, select_ref, out_ref):
    for at in range(0, own_ref.shape[1], 256):
        total = own_ref[:, at : at + 256].astype(F32) + other_ref[:, at : at + 256].astype(F32)
        weighted = (total * gate_ref[...]).astype(BF16)
        out_ref[:, at : at + 256] = dot(select_ref[...], weighted).astype(BF16)


def expand(own, other, gates, select):
    return pl.pallas_call(
        expand_kernel,
        out_shape=shape((select.shape[0], own.shape[1]), BF16),
        in_specs=[VMEM] * 4,
        out_specs=VMEM,
        compiler_params=PARAMS,
    )(own, other, gates, select)


def join_kernel(line_ref, resid_ref, *rest):
    parts, out_ref = rest[:-1], rest[-1]
    total = jnp.dot(
        line_ref[...], resid_ref[...], precision=HIGHEST, preferred_element_type=F32
    )
    for part in parts:
        total = total + part[...].astype(F32)
    out_ref[...] = total.astype(BF16)


def join(line, resid, parts):
    return pl.pallas_call(
        join_kernel,
        out_shape=shape(parts[0].shape, BF16),
        in_specs=[VMEM] * (2 + len(parts)),
        out_specs=VMEM,
        compiler_params=PARAMS,
    )(line, resid, *parts)


def shards(
    queries,
    cache_vals,
    cache_scales,
    cache_len,
    fresh_vals,
    fresh_scales,
    fresh_len,
    fresh_owner,
    hidden,
    w_uv,
    w_out,
    norm_gain,
    route_ids,
    route_weights,
    w_gate,
    w_up,
    w_down,
):
    pd, dp, ep = lax.axis_index("pd"), lax.axis_index("dp"), lax.axis_index("ep")
    n_pd, n_dp, n_ep = lax.axis_size("pd"), lax.axis_size("dp"), lax.axis_size("ep")
    heads, key_width = queries.shape[1:]
    width = hidden.shape[1]
    cols = width // n_dp
    units = w_gate.shape[2]

    chips_y = CHIPS_Y
    chips_z = n_ep // chips_y
    z_groups = [[z * chips_y + y for z in range(chips_z)] for y in range(chips_y)]
    place_y = ep % chips_y

    def shift_y(value, amount):
        pairs = [
            (z * chips_y + y, z * chips_y + (y + amount) % chips_y)
            for z in range(chips_z)
            for y in range(chips_y)
        ]
        return lax.ppermute(value, "ep", pairs)

    at_dp = dp.astype(jnp.int32).reshape(1)
    parcels = make_parcels(at_dp, n_dp, fresh_owner, queries, hidden)
    parcels = list(parcels[:1]) + [shift(parcels[s], "dp", s) for s in range(1, n_dp)]

    whole, first = lax.optimization_barrier((queries, parcels[1]))

    order = np.arange(heads).reshape(n_pd, chips_z, chips_y).transpose(1, 0, 2).reshape(heads)
    order = jnp.asarray(np.eye(heads)[order], BF16)
    packed = old_attention(
        at_dp,
        n_dp,
        cache_len,
        whole,
        order,
        cache_vals[0].T,
        cache_scales[0],
        w_gate[0],
        w_up[0],
        w_down[0],
        chips_z,
    )
    old_out, packed = packed[0], packed[1:]
    uv_own = w_uv[0]
    out_own = lax.dynamic_slice_in_dim(w_out, dp * cols, cols, 1)
    uv_parts = [uv_own] + [shift_y(uv_own, s) for s in range(1, chips_y)]
    out_parts = [out_own] + [shift_y(out_own, s) for s in range(1, chips_y)]
    old_out, rest, uv_parts = lax.optimization_barrier((old_out, parcels[2:], uv_parts))
    parcels = [parcels[0], first] + list(rest)
    parcels, packed = lax.optimization_barrier((parcels, packed))
    both_parts = [packed[0]] + [shift(packed[2 * s], "dp", s) for s in range(1, n_dp)]
    down_parts = [packed[1]] + [shift(packed[2 * s + 1], "dp", s) for s in range(1, n_dp)]
    step = (dp - fresh_owner) % n_dp
    latent = new_attention(
        step, fresh_len, order, fresh_vals[0].T, fresh_scales[0], old_out, parcels
    )
    slab = 2 * n_ep
    sizes = (chips_y, chips_z, n_dp, 2 * slab * route_ids.shape[1] // n_ep)
    latent, parcels, norm_gain = lax.optimization_barrier((latent, parcels, norm_gain))
    gain = lax.dynamic_slice_in_dim(norm_gain, dp * cols, cols, 0)[None]
    ids = lax.dynamic_slice_in_dim(route_ids.T, pd * n_dp * slab, n_dp * slab, 1)
    gates = lax.dynamic_slice_in_dim(route_weights.T, pd * n_dp * slab, n_dp * slab, 1)
    line = line_rows(at_dp, heads, gain, parcels)
    head_rows = exchange(latent, "ep", z_groups)
    head_rows, near, uv_all, line = lax.optimization_barrier(
        (head_rows, out_parts[1::2], jnp.stack(uv_parts), line)
    )
    own, other = sort_rows(chips_y, head_rows.reshape(2 * chips_z * heads // chips_z, DLAT))
    values = head_values(n_dp, own, shift(other, "pd", 1), uv_all)
    values, far = lax.optimization_barrier((values, out_parts[2]))
    out_parts = [out_own, near[0], far, near[1]]
    values = exchange(values, "dp")
    values, near = lax.optimization_barrier((values, both_parts[1::2]))
    rows = n_dp * 2 * chips_z * 2
    order = np.arange(rows).reshape(n_dp, 2, chips_z, 2).transpose(1, 2, 0, 3).reshape(rows)
    order = jnp.asarray(np.eye(rows)[order], BF16)
    own, other = project(values.reshape(rows, chips_y * 128), order, out_parts)
    partial = (own + shift(other, "pd", 1).astype(F32)).astype(BF16)
    summands = exchange(partial.reshape(chips_z, n_dp * 2, cols), "ep", z_groups)
    resid_cols, parcel = residual(summands, line)
    parcel, ids, gates = lax.optimization_barrier((parcel, ids, gates))
    select = mask_there(sizes, ids)
    masks = mask_back(sizes, ids, gates)
    column = exchange(parcel, "ep", z_groups)
    column, far, select, masks = lax.optimization_barrier(
        (column, both_parts[2], select, masks)
    )
    select_back, slot_gate, own_line = masks
    both_parts = [both_parts[0], near[0], far, near[1]]
    column = column.reshape(chips_z * n_dp * 2, cols + 128)
    columns = [column] + [shift_y(column, s) for s in range(1, chips_y)]
    columns, down_parts = lax.optimization_barrier((columns, down_parts))
    slot_rows = select_rows(select, columns)
    other_rows = shift(slot_rows, "pd", 1)

    halves = gate_up(at_dp, slot_rows, other_rows, both_parts)
    all_acts = exchange(activations(width, units, exchange(halves, "dp")), "dp")
    own, other = down(at_dp, all_acts, down_parts)
    table = expand(own, shift(other, "pd", 1), slot_gate, select_back)
    table = table.reshape(chips_y, n_dp * chips_z * 2, cols)
    parts = [lax.dynamic_index_in_dim(table, place_y, 0, keepdims=False)]
    for s in range(1, chips_y):
        part = lax.dynamic_index_in_dim(table, (place_y + s) % chips_y, 0, keepdims=False)
        parts.append(shift_y(part, s))
    table = join(own_line, resid_cols, parts).reshape(n_dp * chips_z, 2, cols)
    planes = [
        [d * n_ep + z * chips_y + y for d in range(n_dp) for z in range(chips_z)]
        for y in range(chips_y)
    ]
    table = exchange(table, ("dp", "ep"), planes).reshape(n_dp, chips_z, 2, cols)
    out = jnp.sum(table.astype(F32), axis=1).astype(BF16)
    return out.transpose(1, 0, 2).reshape(2, width)


def solution(mesh):
    in_specs = (
        P(("pd", "dp", "ep"), None, None),
        P(("pd", "dp", "ep"), None, None),
        P(("pd", "dp", "ep"), None, None),
        P(("pd", "dp", "ep")),
        P(("pd", "dp", "ep"), None, None),
        P(("pd", "dp", "ep"), None, None),
        P(("pd", "dp", "ep")),
        P(("pd", "dp", "ep")),
        P(("pd", "dp", "ep"), None),
        P(("pd", "ep"), None, None),
        P(("pd", "ep"), None),
        P(),
        P(),
        P(),
        P("ep", None, ("pd", "dp")),
        P("ep", None, ("pd", "dp")),
        P("ep", ("pd", "dp"), None),
    )
    out_specs = P(("pd", "dp", "ep"), None)
    return jax.shard_map(shards, mesh=mesh, in_specs=in_specs, out_specs=out_specs, check_vma=False)
```

```python
import functools

import jax
import jax.numpy as jnp
import numpy as np
from jax import lax
from jax.experimental import pallas as pl
from jax.experimental.pallas import tpu as pltpu
from jax.sharding import PartitionSpec as P

DLAT = 512
CHIPS_Y = 4


SOFT_SCALE = 0.07216878364870323
EPSILON = 1e-06
BF16 = jnp.bfloat16
F32 = jnp.float32


def shift(value, axis, amount):
    size = lax.axis_size(axis)
    return lax.ppermute(value, axis, [(i, (i + amount) % size) for i in range(size)])


def exchange(value, axis, groups=None):
    return lax.all_to_all(value, axis, 0, 0, axis_index_groups=groups)


def dot(left, right):
    return jnp.dot(left, right, preferred_element_type=F32)


HIGHEST = lax.Precision.HIGHEST
VMEM = pl.BlockSpec(memory_space=pltpu.VMEM)
SMEM = pl.BlockSpec(memory_space=pltpu.SMEM)
HBM = pl.BlockSpec(memory_space=pltpu.HBM)
ANY = pl.BlockSpec(memory_space=pl.ANY)
PARAMS = pltpu.CompilerParams(vmem_limit_bytes=16 * 1024 * 1024)
WIDE = pltpu.CompilerParams(vmem_limit_bytes=58 * 1024 * 1024)


def shape(dims, dtype):
    return jax.ShapeDtypeStruct(dims, dtype)


def attend(query, keys_ref, scales_ref, length, held_ref):
    for block in range(scales_ref.shape[0]):
        at = slice(block * 128, block * 128 + 128)
        scale = scales_ref[...].astype(F32)[block : block + 1]
        held_ref[at] = (keys_ref[at].astype(F32) * scale).astype(BF16)
    scores = dot(query[:, :DLAT], held_ref[...]) + dot(query[:, DLAT:], keys_ref[DLAT:])
    scores = scores * SOFT_SCALE
    token = lax.broadcasted_iota(jnp.int32, scores.shape, 1)
    scores = jnp.where(token < length, scores, -1e30)
    weights = jnp.exp(scores - jnp.max(scores, axis=1, keepdims=True))
    probs = (weights / jnp.sum(weights, axis=1, keepdims=True)).astype(BF16)
    return lax.dot_general(
        probs, held_ref[...], (((1,), (1,)), ((), ())), preferred_element_type=F32
    )


def parcel_kernel(lines, at_ref, owner_ref, query_ref, hidden_ref, *outs):
    heads, wide = query_ref.shape[1:]
    cols = hidden_ref.shape[1] // lines
    lanes = outs[0].shape[1]
    for s in range(lines):
        start = pl.multiple_of(lax.rem(at_ref[0] + s, lines) * cols, 128)
        hidden = hidden_ref[:, pl.ds(start, cols)].astype(F32)
        parts = [hidden[:, at : at + lanes] for at in range(0, cols, lanes)]
        parts = [jnp.pad(part, ((0, 0), (0, lanes - part.shape[1]))) for part in parts]
        used = 2 * len(parts)
        parts.append(jnp.full((16 - used, lanes), owner_ref[0].astype(F32)))
        outs[s][:heads, :wide] = query_ref[1]
        outs[s][:heads, wide:] = jnp.zeros((heads, lanes - wide), BF16)
        outs[s][heads:] = jnp.concatenate(parts, axis=0).astype(BF16)


def make_parcels(dp, lines, owner, query, hidden):
    out = shape((query.shape[1] + 16, -(-query.shape[2] // 128) * 128), BF16)
    return pl.pallas_call(
        functools.partial(parcel_kernel, lines),
        out_shape=[out] * lines,
        in_specs=[SMEM, SMEM, VMEM, VMEM],
        out_specs=[VMEM] * lines,
        compiler_params=PARAMS,
    )(dp, owner, query, hidden)


def slots_of(lines, capacity, ids_ref, before_ref):
    rows = ids_ref.shape[1]
    hits = ids_ref[...] == lax.axis_index("ep")
    routed = jnp.sum(jnp.where(hits, 1.0, 0.0), axis=0, keepdims=True)
    place = dot(jnp.broadcast_to(routed, (8, rows)).astype(BF16), before_ref[...])[:1]
    lane = lax.broadcasted_iota(jnp.int32, (1, rows), 1)
    first = lax.div(lane, rows // lines) * capacity
    return hits, jnp.where(routed > 0.0, place + first.astype(F32), -1.0)


def there_kernel(lines, capacity, ids_ref, before_ref, there_ref, select_ref):
    slots, rows = select_ref.shape
    slot = slots_of(lines, capacity, ids_ref, before_ref)[1]
    wide = jnp.broadcast_to(slot, (8, rows)).astype(BF16)
    slot_iota = lax.broadcasted_iota(jnp.int32, (slots, rows), 0).astype(F32)
    select_ref[...] = jnp.where(dot(wide, there_ref[...])[:1] == slot_iota, 1.0, 0.0).astype(BF16)


def back_kernel(sizes, ids_ref, gates_ref, before_ref, back_ref, *outs):
    chips_y, chips_z, lines, capacity = sizes
    table_ref, gate_ref, line_ref = outs
    rows, slots = table_ref.shape
    hits, slot = slots_of(lines, capacity, ids_ref, before_ref)
    gates = jnp.sum(jnp.where(hits, gates_ref[...], 0.0), axis=0, keepdims=True)
    wide = jnp.broadcast_to(slot, (8, rows)).astype(BF16)
    slot_iota = lax.broadcasted_iota(jnp.int32, (slots, rows), 0).astype(F32)
    back = jnp.where(dot(wide, back_ref[...])[:1] == slot_iota, 1.0, 0.0)
    table_ref[...] = back.T.astype(BF16)
    gate_ref[...] = jnp.sum(jnp.where(slot == slot_iota, gates, 0.0), axis=1, keepdims=True)
    pairs = 2 * chips_z
    out = lax.broadcasted_iota(jnp.int32, line_ref.shape, 0)
    come = lax.broadcasted_iota(jnp.int32, line_ref.shape, 1)
    own = lax.rem(lax.div(out, 2), chips_z) == lax.div(lax.axis_index("ep"), chips_y)
    own = own & (lax.div(out, pairs) * 2 + lax.rem(out, 2) == come)
    line_ref[...] = jnp.where(own, 1.0, 0.0)


def orders(sizes, rows, axes):
    chips_y, chips_z, lines, _ = sizes
    slab = rows // lines
    canon = np.arange(rows).reshape(lines, chips_z, chips_y, 2)
    before = np.kron(np.eye(lines), np.triu(np.ones((slab, slab)), 1))
    order = np.eye(rows)[canon.transpose(axes).reshape(rows)].T
    return jnp.asarray(before, BF16), jnp.asarray(order, BF16)


def mask_there(sizes, ids):
    rows, slots = ids.shape[1], sizes[2] * sizes[3]
    return pl.pallas_call(
        functools.partial(there_kernel, sizes[2], sizes[3]),
        out_shape=shape((slots, rows), BF16),
        in_specs=[VMEM] * 3,
        out_specs=VMEM,
        compiler_params=PARAMS,
    )(ids, *orders(sizes, rows, (2, 1, 0, 3)))


def mask_back(sizes, ids, gates):
    rows, slots = ids.shape[1], sizes[2] * sizes[3]
    return pl.pallas_call(
        functools.partial(back_kernel, sizes),
        out_shape=[
            shape((rows, slots), BF16),
            shape((slots, 1), F32),
            shape((sizes[2] * 2 * sizes[1], 2 * sizes[2]), F32),
        ],
        in_specs=[VMEM] * 4,
        out_specs=[VMEM] * 3,
        compiler_params=PARAMS,
    )(ids, gates, *orders(sizes, rows, (2, 0, 1, 3)))


def old_kernel(lines, at_ref, len_ref, query_ref, order_ref, keys_ref, scales_ref, *rest):
    gate_ref, up_ref, down_ref, out_ref = rest[:4]
    outs, held_ref, sems = rest[4:-2], rest[-2], rest[-1]
    cols, units = outs[1].shape[1], gate_ref.shape[1]
    copies = []
    for s in range(lines):
        start = pl.multiple_of(lax.rem(at_ref[0] + s, lines) * cols, 128)
        both, down = outs[2 * s], outs[2 * s + 1]
        copies.append((gate_ref.at[pl.ds(start, cols)], both.at[:, pl.ds(0, units)]))
        copies.append((up_ref.at[pl.ds(start, cols)], both.at[:, pl.ds(units, units)]))
        copies.append((down_ref.at[:, pl.ds(start, cols)], down))
    copies = [pltpu.make_async_copy(a, b, sems.at[i]) for i, (a, b) in enumerate(copies)]
    for copy in copies:
        copy.start()
    query = dot(order_ref[...], query_ref[0]).astype(BF16)
    result = attend(query, keys_ref, scales_ref, len_ref[0], held_ref)
    rows = out_ref.shape[1]
    for z in range(out_ref.shape[0]):
        out_ref[z] = result[z * rows : (z + 1) * rows].astype(BF16)
    for copy in copies:
        copy.wait()


def old_attention(dp, lines, length, query, order, keys, scales, gate, up, down, pieces):
    cols, units = gate.shape[0] // lines, gate.shape[1]
    rows = query.shape[1] // pieces
    return pl.pallas_call(
        functools.partial(old_kernel, lines),
        out_shape=[shape((pieces, rows, DLAT), BF16)]
        + [shape((cols, 2 * units), BF16), shape((units, cols), BF16)] * lines,
        in_specs=[SMEM, SMEM] + [VMEM] * 4 + [HBM] * 3,
        out_specs=[VMEM] * (2 * lines + 1),
        scratch_shapes=[
            pltpu.VMEM((DLAT, keys.shape[1]), BF16),
            pltpu.SemaphoreType.DMA((3 * lines,)),
        ],
        compiler_params=WIDE,
        cost_estimate=pl.CostEstimate(
            flops=2 * query.size * keys.shape[1],
            bytes_accessed=2 * (keys.size + 2 * (gate.size + up.size + down.size)),
            transcendentals=query.shape[1] * keys.shape[1],
        ),
    )(dp, length, query, order, keys, scales, gate, up, down)


def new_kernel(lines, step_ref, len_ref, order_ref, keys_ref, scales_ref, old_ref, *rest):
    parcel_refs, out_ref, held_ref = rest[:lines], rest[lines], rest[lines + 1]
    heads, width = order_ref.shape[0], keys_ref.shape[0]
    query = parcel_refs[0][:heads, :width]
    for s in range(1, lines):
        query = jnp.where(step_ref[0] == s, parcel_refs[s][:heads, :width], query)
    query = dot(order_ref[...], query).astype(BF16)
    result = attend(query, keys_ref, scales_ref, len_ref[0], held_ref)
    rows = out_ref.shape[2]
    for z in range(out_ref.shape[0]):
        out_ref[z, 0] = old_ref[z]
        out_ref[z, 1] = result[z * rows : (z + 1) * rows].astype(BF16)


def new_attention(step, length, order, keys, scales, old, parcels):
    return pl.pallas_call(
        functools.partial(new_kernel, len(parcels)),
        out_shape=shape((old.shape[0], 2) + old.shape[1:], BF16),
        in_specs=[SMEM, SMEM] + [VMEM] * (4 + len(parcels)),
        out_specs=VMEM,
        scratch_shapes=[pltpu.VMEM((DLAT, keys.shape[1]), BF16)],
        compiler_params=PARAMS,
    )(step, length, order, keys, scales, old, *parcels)


def sort_kernel(chips_y, rows_ref, own_ref, other_ref):
    half = own_ref.shape[0]
    pairs = half // chips_y
    core, place_y = lax.axis_index("pd"), lax.rem(lax.axis_index("ep"), chips_y)
    out = lax.broadcasted_iota(jnp.int32, (2 * half, 2 * half), 0)
    want = lax.div(out, half)
    want = jnp.where(want == 0, core, 1 - core)
    turn = lax.rem(place_y - lax.rem(lax.div(out, pairs), chips_y) + chips_y, chips_y)
    want = lax.rem(out, pairs) * (2 * chips_y) + want * chips_y + turn
    come = lax.broadcasted_iota(jnp.int32, (2 * half, 2 * half), 1)
    order = jnp.where(want == come, 1.0, 0.0).astype(BF16)
    result = dot(order, rows_ref[...]).astype(BF16)
    own_ref[...] = result[:half]
    other_ref[...] = result[half:]


def sort_rows(chips_y, rows):
    half = shape((rows.shape[0] // 2, rows.shape[1]), BF16)
    return pl.pallas_call(
        functools.partial(sort_kernel, chips_y),
        out_shape=[half, half],
        in_specs=[VMEM],
        out_specs=[VMEM, VMEM],
        compiler_params=PARAMS,
    )(rows)


def values_kernel(own_ref, other_ref, uv_ref, out_ref):
    count, _, width = uv_ref.shape
    rows = own_ref.shape[0] // count
    for s in range(count):
        for q, ref in enumerate((own_ref, other_ref)):
            result = dot(ref[s * rows : (s + 1) * rows], uv_ref[s]).astype(BF16)
            for i in range(out_ref.shape[0]):
                out_ref[i, q * rows : (q + 1) * rows, s * width : (s + 1) * width] = result


def head_values(lines, own, other, uv_all):
    count, _, width = uv_all.shape
    return pl.pallas_call(
        values_kernel,
        out_shape=shape((lines, 2 * own.shape[0] // count, count * width), BF16),
        in_specs=[VMEM] * 3,
        out_specs=VMEM,
        compiler_params=PARAMS,
    )(own, other, uv_all)


def project_kernel(values_ref, order_ref, *rest):
    out_refs, own_ref, other_ref = rest[:-2], rest[-2], rest[-1]
    rows = values_ref.shape[0] // 2
    values = dot(order_ref[...], values_ref[...]).astype(BF16)
    width = out_refs[0].shape[0]
    for start in range(0, own_ref.shape[1], 256):
        total = sum(
            dot(values[:, s * width : (s + 1) * width], ref[:, start : start + 256])
            for s, ref in enumerate(out_refs)
        )
        own_ref[:, start : start + 256] = total[:rows]
        other_ref[:, start : start + 256] = total[rows:].astype(BF16)


def project(values, order, out_parts):
    rows, cols = values.shape[0] // 2, out_parts[0].shape[1]
    return pl.pallas_call(
        project_kernel,
        out_shape=[shape((rows, cols), F32), shape((rows, cols), BF16)],
        in_specs=[VMEM] * (2 + len(out_parts)),
        out_specs=[VMEM, VMEM],
        compiler_params=PARAMS,
    )(values, order, *out_parts)


def line_kernel(heads, at_ref, gain_ref, *rest):
    parcel_refs, out_ref = rest[:-1], rest[-1]
    lines, cols = len(parcel_refs), gain_ref.shape[1]
    row = lax.broadcasted_iota(jnp.int32, (2 * lines, 128), 0)
    come = lax.broadcasted_iota(jnp.int32, (2 * lines, 128), 1)
    same = lax.rem(row, 2) == lax.rem(come, 2)
    old = lax.rem(row, 2) == 0
    row, come = lax.div(row, 2), lax.div(come, 2)
    order = jnp.where(same & old & (row == come), 1.0, 0.0)
    turned = jnp.zeros_like(order)
    hidden = []
    for s, ref in enumerate(parcel_refs):
        source = lax.rem(at_ref[0] - s + lines, lines)
        lower = ref[heads:].astype(F32)
        lanes = lower.shape[1]
        count = -(-cols // lanes)
        owner = lower[2 * count : 2 * count + 1, :1]
        moved = same & ~old & (come == source) & (row.astype(F32) == owner)
        order = order + jnp.where(moved, 1.0, 0.0)
        turned = turned + jnp.where(same & (come == s) & (row == source), 1.0, 0.0)
        pieces = [
            lower[2 * j : 2 * j + 2, : min(lanes, cols - j * lanes)] for j in range(count)
        ]
        hidden.append(jnp.concatenate(pieces, axis=1))
    hidden = jnp.concatenate(hidden, axis=0)
    rows = 2 * lines
    out_ref[:rows] = jnp.dot(
        turned[:, :rows], hidden, precision=HIGHEST, preferred_element_type=F32
    )
    out_ref[rows : 2 * rows] = jnp.broadcast_to(gain_ref[...].astype(F32), (rows, cols))
    out_ref[2 * rows :, :128] = order
    out_ref[2 * rows :, 128:] = jnp.zeros((rows, cols - 128), F32)


def line_rows(dp, heads, gain, parcels):
    return pl.pallas_call(
        functools.partial(line_kernel, heads),
        out_shape=shape((6 * len(parcels), gain.shape[1]), F32),
        in_specs=[SMEM] + [VMEM] * (1 + len(parcels)),
        out_specs=VMEM,
        compiler_params=PARAMS,
    )(dp, gain, *parcels)


def residual_kernel(sums_ref, line_ref, resid_ref, parcel_ref):
    rows, cols = resid_ref.shape
    total = sums_ref[0].astype(F32)
    for i in range(1, sums_ref.shape[0]):
        total = total + sums_ref[i].astype(F32)
    order = line_ref[2 * rows :, :128][:, :rows]
    resid = jnp.dot(order, total, precision=HIGHEST, preferred_element_type=F32)
    resid = resid + line_ref[:rows]
    resid_ref[...] = resid
    squares = jnp.sum(resid * resid, axis=1, keepdims=True)
    high = squares.astype(BF16)
    low = (squares - high.astype(F32)).astype(BF16)
    lanes = lax.broadcasted_iota(jnp.int32, (rows, 128), 1)
    beside = jnp.where(lanes < 64, high.astype(F32), low.astype(F32)).astype(BF16)
    parcel = (resid * line_ref[rows : 2 * rows]).astype(BF16)
    for i in range(parcel_ref.shape[0]):
        parcel_ref[i, :, :cols] = parcel
        parcel_ref[i, :, cols:] = beside


def residual(sums, line):
    copies, rows, cols = sums.shape
    return pl.pallas_call(
        residual_kernel,
        out_shape=[shape((rows, cols), F32), shape((copies, rows, cols + 128), BF16)],
        in_specs=[VMEM, VMEM],
        out_specs=[VMEM, VMEM],
        compiler_params=PARAMS,
    )(sums, line)


def select_kernel(select_ref, *rest):
    columns, out_ref, held_ref = rest[:-2], rest[-2], rest[-1]
    count, rows = len(columns), columns[0].shape[0]
    for s, ref in enumerate(columns):
        held_ref[lax.rem(lax.rem(lax.axis_index("ep"), count) - s + count, count)] = ref[...]
    for at in range(0, out_ref.shape[1], 384):
        lanes = slice(at, min(at + 384, out_ref.shape[1]))
        gathered = held_ref[:, :, lanes].reshape(count * rows, lanes.stop - at)
        out_ref[:, lanes] = dot(select_ref[...], gathered).astype(BF16)


def select_rows(select, columns):
    return pl.pallas_call(
        select_kernel,
        out_shape=shape((select.shape[0], columns[0].shape[1]), BF16),
        in_specs=[VMEM] * (1 + len(columns)),
        out_specs=VMEM,
        scratch_shapes=[pltpu.VMEM((len(columns),) + columns[0].shape, BF16)],
        compiler_params=PARAMS,
    )(select, *columns)


def acts_kernel(width, units, sums_ref, out_ref):
    total = sums_ref[0].astype(F32)
    for i in range(1, sums_ref.shape[0]):
        total = total + sums_ref[i].astype(F32)
    end = sums_ref.shape[2] - 128
    squares = total[:, end : end + 1] + total[:, end + 64 : end + 65]
    scale = lax.rsqrt(squares / width + EPSILON)
    for j in range(end // (2 * units)):
        at = 2 * units * j
        gate = total[:, at : at + units] * scale
        up = total[:, at + units : at + 2 * units] * scale
        acts = (gate / (1.0 + jnp.exp(-gate)) * up).astype(BF16)
        for i in range(out_ref.shape[0]):
            out_ref[i, :, j * units : (j + 1) * units] = acts


def activations(width, units, sums):
    lines, rows, lanes = sums.shape
    return pl.pallas_call(
        functools.partial(acts_kernel, width, units),
        out_shape=shape((lines, rows, (lanes - 128) // 2), BF16),
        in_specs=[VMEM],
        out_specs=VMEM,
        compiler_params=PARAMS,
    )(sums)


def gate_up_kernel(lines, at_ref, own_ref, other_ref, *rest):
    parts, out_ref, held, sems = rest[:-3], rest[-3], rest[-2], rest[-1]
    cols, lanes = held.shape[1:]
    copies = [pltpu.make_async_copy(parts[s], held.at[s], sems.at[s]) for s in range(lines)]
    for copy in copies:
        copy.start()
    for s in range(lines):
        copies[s].wait()
        lane = pl.multiple_of(lax.rem(at_ref[0] - s + lines, lines) * lanes, 128)
        for q, ref in enumerate((own_ref, other_ref)):
            capacity = ref.shape[0] // lines
            result = dot(ref[:, :cols], held[s]).astype(BF16)
            for d in range(lines):
                out_ref[d, q * capacity : (q + 1) * capacity, pl.ds(lane, lanes)] = result[
                    d * capacity : (d + 1) * capacity
                ]
    for q, ref in enumerate((own_ref, other_ref)):
        capacity = ref.shape[0] // lines
        for d in range(lines):
            out_ref[d, q * capacity : (q + 1) * capacity, lines * lanes :] = ref[
                d * capacity : (d + 1) * capacity, cols:
            ]


def gate_up(dp, own, other, parts):
    lines, (cols, lanes) = len(parts), parts[0].shape
    return pl.pallas_call(
        functools.partial(gate_up_kernel, lines),
        out_shape=shape((lines, 2 * own.shape[0] // lines, lines * lanes + 128), BF16),
        in_specs=[SMEM, VMEM, VMEM] + [ANY] * lines,
        out_specs=VMEM,
        scratch_shapes=[
            pltpu.VMEM((lines, cols, lanes), BF16),
            pltpu.SemaphoreType.DMA((lines,)),
        ],
        compiler_params=PARAMS,
    )(dp, own, other, *parts)


def down_kernel(lines, at_ref, acts_ref, *rest):
    parts, own_ref, other_ref, held, sems = rest[:-4], rest[-4], rest[-3], rest[-2], rest[-1]
    units, cols = parts[0].shape
    copies = []
    for s in range(lines):
        row = pl.multiple_of(lax.rem(at_ref[0] - s + lines, lines) * units, 128)
        copies.append(pltpu.make_async_copy(parts[s], held.at[pl.ds(row, units)], sems.at[s]))
    for copy in copies:
        copy.start()
    for copy in copies:
        copy.wait()
    capacity = acts_ref.shape[1] // 2
    own = jnp.concatenate([acts_ref[d, :capacity] for d in range(lines)], axis=0)
    other = jnp.concatenate([acts_ref[d, capacity:] for d in range(lines)], axis=0)
    for at in range(0, cols, 256):
        own_ref[:, at : at + 256] = dot(own, held[:, at : at + 256]).astype(BF16)
        other_ref[:, at : at + 256] = dot(other, held[:, at : at + 256]).astype(BF16)


def down(dp, acts, parts):
    lines, (units, cols) = len(parts), parts[0].shape
    slots = acts.shape[0] * acts.shape[1] // 2
    return pl.pallas_call(
        functools.partial(down_kernel, lines),
        out_shape=[shape((slots, cols), BF16), shape((slots, cols), BF16)],
        in_specs=[SMEM, VMEM] + [ANY] * lines,
        out_specs=[VMEM, VMEM],
        scratch_shapes=[
            pltpu.VMEM((lines * units, cols), BF16),
            pltpu.SemaphoreType.DMA((lines,)),
        ],
        compiler_params=PARAMS,
    )(dp, acts, *parts)


def expand_kernel(own_ref, other_ref, gate_ref, select_ref, out_ref):
    for at in range(0, own_ref.shape[1], 256):
        total = own_ref[:, at : at + 256].astype(F32) + other_ref[:, at : at + 256].astype(F32)
        weighted = (total * gate_ref[...]).astype(BF16)
        out_ref[:, at : at + 256] = dot(select_ref[...], weighted).astype(BF16)


def expand(own, other, gates, select):
    return pl.pallas_call(
        expand_kernel,
        out_shape=shape((select.shape[0], own.shape[1]), BF16),
        in_specs=[VMEM] * 4,
        out_specs=VMEM,
        compiler_params=PARAMS,
    )(own, other, gates, select)


def join_kernel(line_ref, resid_ref, *rest):
    parts, out_ref = rest[:-1], rest[-1]
    total = jnp.dot(
        line_ref[...], resid_ref[...], precision=HIGHEST, preferred_element_type=F32
    )
    for part in parts:
        total = total + part[...].astype(F32)
    out_ref[...] = total.astype(BF16)


def join(line, resid, parts):
    return pl.pallas_call(
        join_kernel,
        out_shape=shape(parts[0].shape, BF16),
        in_specs=[VMEM] * (2 + len(parts)),
        out_specs=VMEM,
        compiler_params=PARAMS,
    )(line, resid, *parts)


def shards(
    queries,
    cache_vals,
    cache_scales,
    cache_len,
    fresh_vals,
    fresh_scales,
    fresh_len,
    fresh_owner,
    hidden,
    w_uv,
    w_out,
    norm_gain,
    route_ids,
    route_weights,
    w_gate,
    w_up,
    w_down,
):
    pd, dp, ep = lax.axis_index("pd"), lax.axis_index("dp"), lax.axis_index("ep")
    n_pd, n_dp, n_ep = lax.axis_size("pd"), lax.axis_size("dp"), lax.axis_size("ep")
    heads, key_width = queries.shape[1:]
    width = hidden.shape[1]
    cols = width // n_dp
    units = w_gate.shape[2]

    chips_y = CHIPS_Y
    chips_z = n_ep // chips_y
    z_groups = [[z * chips_y + y for z in range(chips_z)] for y in range(chips_y)]
    place_y = ep % chips_y

    def shift_y(value, amount):
        pairs = [
            (z * chips_y + y, z * chips_y + (y + amount) % chips_y)
            for z in range(chips_z)
            for y in range(chips_y)
        ]
        return lax.ppermute(value, "ep", pairs)

    at_dp = dp.astype(jnp.int32).reshape(1)
    parcels = make_parcels(at_dp, n_dp, fresh_owner, queries, hidden)
    parcels = list(parcels[:1]) + [shift(parcels[s], "dp", s) for s in range(1, n_dp)]

    whole, first = lax.optimization_barrier((queries, parcels[1]))

    order = np.arange(heads).reshape(n_pd, chips_z, chips_y).transpose(1, 0, 2).reshape(heads)
    order = jnp.asarray(np.eye(heads)[order], BF16)
    packed = old_attention(
        at_dp,
        n_dp,
        cache_len,
        whole,
        order,
        cache_vals[0].T,
        cache_scales[0],
        w_gate[0],
        w_up[0],
        w_down[0],
        chips_z,
    )
    old_out, packed = packed[0], packed[1:]
    uv_own = w_uv[0]
    out_own = lax.dynamic_slice_in_dim(w_out, dp * cols, cols, 1)
    uv_parts = [uv_own] + [shift_y(uv_own, s) for s in range(1, chips_y)]
    out_parts = [out_own] + [shift_y(out_own, s) for s in range(1, chips_y)]
    old_out, rest, uv_parts = lax.optimization_barrier((old_out, parcels[2:], uv_parts))
    parcels = [parcels[0], first] + list(rest)
    parcels, packed = lax.optimization_barrier((parcels, packed))
    both_parts = [packed[0]] + [shift(packed[2 * s], "dp", s) for s in range(1, n_dp)]
    down_parts = [packed[1]] + [shift(packed[2 * s + 1], "dp", s) for s in range(1, n_dp)]
    step = (dp - fresh_owner) % n_dp
    latent = new_attention(
        step, fresh_len, order, fresh_vals[0].T, fresh_scales[0], old_out, parcels
    )
    slab = 2 * n_ep
    sizes = (chips_y, chips_z, n_dp, 2 * slab * route_ids.shape[1] // n_ep)
    latent, parcels, norm_gain = lax.optimization_barrier((latent, parcels, norm_gain))
    gain = lax.dynamic_slice_in_dim(norm_gain, dp * cols, cols, 0)[None]
    ids = lax.dynamic_slice_in_dim(route_ids.T, pd * n_dp * slab, n_dp * slab, 1)
    gates = lax.dynamic_slice_in_dim(route_weights.T, pd * n_dp * slab, n_dp * slab, 1)
    line = line_rows(at_dp, heads, gain, parcels)
    head_rows = exchange(latent, "ep", z_groups)
    head_rows, near, uv_all, line = lax.optimization_barrier(
        (head_rows, out_parts[1::2], jnp.stack(uv_parts), line)
    )
    own, other = sort_rows(chips_y, head_rows.reshape(2 * chips_z * heads // chips_z, DLAT))
    values = head_values(n_dp, own, shift(other, "pd", 1), uv_all)
    values, far = lax.optimization_barrier((values, out_parts[2]))
    out_parts = [out_own, near[0], far, near[1]]
    values = exchange(values, "dp")
    values, near = lax.optimization_barrier((values, both_parts[1::2]))
    rows = n_dp * 2 * chips_z * 2
    order = np.arange(rows).reshape(n_dp, 2, chips_z, 2).transpose(1, 2, 0, 3).reshape(rows)
    order = jnp.asarray(np.eye(rows)[order], BF16)
    own, other = project(values.reshape(rows, chips_y * 128), order, out_parts)
    partial = (own + shift(other, "pd", 1).astype(F32)).astype(BF16)
    summands = exchange(partial.reshape(chips_z, n_dp * 2, cols), "ep", z_groups)
    resid_cols, parcel = residual(summands, line)
    parcel, ids, gates = lax.optimization_barrier((parcel, ids, gates))
    select = mask_there(sizes, ids)
    masks = mask_back(sizes, ids, gates)
    column = exchange(parcel, "ep", z_groups)
    column, far, select, masks = lax.optimization_barrier(
        (column, both_parts[2], select, masks)
    )
    select_back, slot_gate, own_line = masks
    both_parts = [both_parts[0], near[0], far, near[1]]
    column = column.reshape(chips_z * n_dp * 2, cols + 128)
    far_first = sorted(range(1, chips_y), key=lambda s: -min(s, chips_y - s))
    moved = {s: shift_y(column, s) for s in far_first}
    columns = [column] + [moved[s] for s in range(1, chips_y)]
    columns, down_parts = lax.optimization_barrier((columns, down_parts))
    slot_rows = select_rows(select, columns)
    other_rows = shift(slot_rows, "pd", 1)

    halves = gate_up(at_dp, slot_rows, other_rows, both_parts)
    all_acts = exchange(activations(width, units, exchange(halves, "dp")), "dp")
    own, other = down(at_dp, all_acts, down_parts)
    table = expand(own, shift(other, "pd", 1), slot_gate, select_back)
    table = table.reshape(chips_y, n_dp * chips_z * 2, cols)
    parts = [lax.dynamic_index_in_dim(table, place_y, 0, keepdims=False)]
    for s in far_first:
        part = lax.dynamic_index_in_dim(table, (place_y + s) % chips_y, 0, keepdims=False)
        parts.append(shift_y(part, s))
    table = join(own_line, resid_cols, parts).reshape(n_dp * chips_z, 2, cols)
    planes = [
        [d * n_ep + z * chips_y + y for d in range(n_dp) for z in range(chips_z)]
        for y in range(chips_y)
    ]
    table = exchange(table, ("dp", "ep"), planes).reshape(n_dp, chips_z, 2, cols)
    out = jnp.sum(table.astype(F32), axis=1).astype(BF16)
    return out.transpose(1, 0, 2).reshape(2, width)


def solution(mesh):
    in_specs = (
        P(("pd", "dp", "ep"), None, None),
        P(("pd", "dp", "ep"), None, None),
        P(("pd", "dp", "ep"), None, None),
        P(("pd", "dp", "ep")),
        P(("pd", "dp", "ep"), None, None),
        P(("pd", "dp", "ep"), None, None),
        P(("pd", "dp", "ep")),
        P(("pd", "dp", "ep")),
        P(("pd", "dp", "ep"), None),
        P(("pd", "ep"), None, None),
        P(("pd", "ep"), None),
        P(),
        P(),
        P(),
        P("ep", None, ("pd", "dp")),
        P("ep", None, ("pd", "dp")),
        P("ep", ("pd", "dp"), None),
    )
    out_specs = P(("pd", "dp", "ep"), None)
    return jax.shard_map(shards, mesh=mesh, in_specs=in_specs, out_specs=out_specs, check_vma=False)
```
